128 devices in a mesh: ctx: 8 (over z_hi, x), fsdp: 16 (over y, z_lo, core).
Axes of the slice: x: 4, y: 4, z: 4 (z_hi: 2, z_lo: 2; z = z_hi * 2 + z_lo), core: 2. Of those that a mesh axis runs over, the one named last changes fastest.
Arguments:
- tokens: bfloat16 [16, 16, 128, 768], P('fsdp', 'ctx'), may hold values from -6 to 6
- lengths: int32 [16], P('fsdp'), may hold values from 1024 to 2048, as said below
- block_map: int32 [16], replicated, may hold values from 0 to 15, as said below
- first_gain: bfloat16 [768], P('fsdp'), may hold values from 0.25 to 1.75
- first_shift: bfloat16 [768], P('fsdp'), may hold values from -1.75 to 1.75
- query_weight: bfloat16 [768, 768], P('fsdp'), may hold values from -0.21875 to 0.21875
- query_bias: bfloat16 [768], P('fsdp'), may hold values from -1.75 to 1.75
- keyval_weight: bfloat16 [768, 128], P('fsdp'), may hold values from -0.21875 to 0.21875
- value_bias: bfloat16 [64], P('fsdp'), may hold values from -3 to 3
- output_weight: bfloat16 [768, 768], P('fsdp'), may hold values from -1.75 to 1.75
- output_bias: bfloat16 [768], P('fsdp'), may hold values from -1.75 to 1.75
- second_gain: bfloat16 [768], P('fsdp'), may hold values from 0.25 to 1.75
- second_shift: bfloat16 [768], P('fsdp'), may hold values from -1.75 to 1.75
- up_weight: bfloat16 [768, 3072], P('fsdp'), may hold values from -0.21875 to 0.21875
- up_bias: bfloat16 [3072], P('fsdp'), may hold values from -1.75 to 1.75
- down_weight: bfloat16 [3072, 768], P('fsdp'), may hold values from -0.109375 to 0.109375
- down_bias: bfloat16 [768], P('fsdp'), may hold values from -1.75 to 1.75
- cotangent: float32 [16, 16, 128, 768], P('fsdp', 'ctx'), may hold values from -6 to 6
Outputs:
- layer_out: bfloat16 [16, 16, 128, 768], P('fsdp', 'ctx')
- input_grad: float32 [16, 16, 128, 768], P('fsdp', 'ctx')
- first_gain_grad: float32 [768], P('fsdp')
- first_shift_grad: float32 [768], P('fsdp')
- query_weight_grad: float32 [768, 768], P('fsdp')
- query_bias_grad: float32 [768], P('fsdp')
- keyval_weight_grad: float32 [768, 128], P('fsdp')
- value_bias_grad: float32 [64], P('fsdp')
- output_weight_grad: float32 [768, 768], P('fsdp')
- output_bias_grad: float32 [768], P('fsdp')
- second_gain_grad: float32 [768], P('fsdp')
- second_shift_grad: float32 [768], P('fsdp')
- up_weight_grad: float32 [768, 3072], P('fsdp')
- up_bias_grad: float32 [3072], P('fsdp')
- down_weight_grad: float32 [3072, 768], P('fsdp')
- down_bias_grad: float32 [768], P('fsdp')
The draws below stay inside these ranges and needn't reach their ends.
Inputs may be any that keep to these rules, and one draw needn't show every extreme that they name: `lengths`: every draw has a sequence of exactly 2048 valid tokens, which one drawn from the seed. `block_map`: each block once; slots 2c and 2c + 1 hold a block b and its mirror 16 - 1 - b.
All inputs are finite; a program needn't handle non-finite values.
Results may differ from the reference program's by a relative error of at most 0.024.
Values may be sent and summed in bfloat16 or wider, within the bound.
A program may use at most 128 MiB of HBM per device.

```python
import math
import jax
import jax.numpy as jnp
from jax import lax

MODEL_WIDTH = 768
H = 12
HD = 64
FF = 3072
BLOCK_POSITIONS = 128
SEQUENCE_TOTAL = 16
BLOCKS_PER_SEQ = 16
LEN = 2048


def draw_lengths(key, part):
    key = jax.random.fold_in(key, 11)
    key_one, second = jax.random.split(key)
    drawn = jax.random.randint(key_one, (SEQUENCE_TOTAL,), LEN // 2, LEN + 1, dtype=jnp.int32)
    chosen = jax.random.randint(second, (), 0, SEQUENCE_TOTAL, dtype=jnp.int32)
    return jnp.where(jnp.arange(SEQUENCE_TOTAL, dtype=jnp.int32) == chosen, LEN, drawn).astype(jnp.int32)


def draw_block_map(key, part):
    key = jax.random.fold_in(key, 23)
    key_one, second = jax.random.split(key)
    sequence_pairs = BLOCKS_PER_SEQ // 2
    pairing_permutation = jax.random.permutation(key_one, sequence_pairs).astype(jnp.int32)
    flip_bits = jax.random.randint(second, (sequence_pairs,), 0, 2, dtype=jnp.int32)
    reverse_rule = BLOCKS_PER_SEQ - 1 - pairing_permutation
    leading_block_slot = jnp.where(flip_bits == 0, pairing_permutation, reverse_rule)
    trailing_block_slot = jnp.where(flip_bits == 0, reverse_rule, pairing_permutation)
    return jnp.stack([leading_block_slot, trailing_block_slot], axis=1).reshape(BLOCKS_PER_SEQ).astype(jnp.int32)


def steps_of(own_key, extent, cuts, least, top_value):
    factor_of, own = 1.0, jax.random.fold_in(own_key, 6)
    for position, shards_of in cuts:
        steps = jnp.exp(jax.random.uniform(jax.random.fold_in(own, position), (shards_of,), jnp.float32, least / len(cuts), top_value / len(cuts)))
        factor_of = factor_of * jnp.repeat(steps, extent[position] // shards_of).reshape([-1 if axis == position else 1 for axis in range(len(extent))])
    return factor_of


def gaussian(stream_key, dims, deviation, reach, shards=(), kind=jnp.bfloat16):
    gain = steps_of(stream_key, dims, shards, -0.22, 0.18) if shards else 1.0
    array = jax.random.normal(stream_key, dims, jnp.float32) * deviation * gain
    return jnp.minimum(jnp.maximum(array, -reach), reach).astype(kind)


def setup_inputs(seed: int = 0) -> dict:
    key_of = jax.random.split(jax.random.key(seed), 19)
    return {
        "tokens": gaussian(key_of[0], (SEQUENCE_TOTAL, BLOCKS_PER_SEQ, BLOCK_POSITIONS, MODEL_WIDTH), 1.0, 6.0, ((0, 16), (1, 8))),
        "lengths": draw_lengths(jax.random.fold_in(key_of[18], 71), 0),
        "block_map": draw_block_map(jax.random.fold_in(key_of[18], 71), 0),
        "first_gain": jnp.clip(1.0 + 0.15 * jax.random.normal(key_of[3], (MODEL_WIDTH,), jnp.float32), 0.25, 1.75).astype(jnp.bfloat16),
        "first_shift": gaussian(key_of[4], (MODEL_WIDTH,), 0.3, 1.75, ((0, 16),)),
        "query_weight": gaussian(key_of[5], (MODEL_WIDTH, MODEL_WIDTH), MODEL_WIDTH ** -0.5, 0.21875, ((0, 16),)),
        "query_bias": gaussian(key_of[6], (MODEL_WIDTH,), 0.3, 1.75, ((0, 16),)),
        "keyval_weight": gaussian(key_of[7], (MODEL_WIDTH, 2 * HD), MODEL_WIDTH ** -0.5, 0.21875, ((0, 16),)),
        "value_bias": gaussian(key_of[8], (HD,), 0.5, 3.0, ((0, 16),)),
        "output_weight": gaussian(key_of[9], (MODEL_WIDTH, MODEL_WIDTH), (MODEL_WIDTH // 64) ** -0.5, 1.75, ((0, 16),)),
        "output_bias": gaussian(key_of[10], (MODEL_WIDTH,), 0.3, 1.75, ((0, 16),)),
        "second_gain": jnp.clip(1.0 + 0.15 * jax.random.normal(key_of[11], (MODEL_WIDTH,), jnp.float32), 0.25, 1.75).astype(jnp.bfloat16),
        "second_shift": gaussian(key_of[12], (MODEL_WIDTH,), 0.3, 1.75, ((0, 16),)),
        "up_weight": gaussian(key_of[13], (MODEL_WIDTH, FF), MODEL_WIDTH ** -0.5, 0.21875, ((0, 16),)),
        "up_bias": gaussian(key_of[14], (FF,), 0.3, 1.75, ((0, 16),)),
        "down_weight": gaussian(key_of[15], (FF, MODEL_WIDTH), FF ** -0.5, 0.109375, ((0, 16),)),
        "down_bias": gaussian(key_of[16], (MODEL_WIDTH,), 0.3, 1.75, ((0, 16),)),
        "cotangent": gaussian(key_of[17], (SEQUENCE_TOTAL, BLOCKS_PER_SEQ, BLOCK_POSITIONS, MODEL_WIDTH), 1.0, 6.0, ((0, 16), (1, 8)), jnp.float32),
    }


@jax.custom_vjp
def low(v):
    return lax.optimization_barrier(v.astype(jnp.bfloat16)).astype(jnp.float32)

@jax.custom_vjp
def low_back(v):
    return v

def low_keep(v):
    return (low(v), None)

def low_pass(kept, grad):
    return (grad,)

def back_keep(v):
    return (v, None)

def back_low(kept, grad):
    return (low(grad),)
low.defvjp(low_keep, low_pass)
low_back.defvjp(back_keep, back_low)
EPS = 1e-05
MASKED = -1e+30
HIGH = lax.Precision.HIGHEST

def layer_norm(values, gain_vec, bias_vec):
    centre = values - lax.optimization_barrier(jnp.mean(values, -1, keepdims=True))
    spread = lax.optimization_barrier(jnp.mean(centre * centre, -1, keepdims=True))
    return centre * lax.rsqrt(spread + EPS) * gain_vec + bias_vec

def gelu_tanh(values):
    return jax.nn.gelu(values, approximate=True)

def round_both(values):
    return low(low_back(values))

def attend(query_rows, key_part, value_part, query_pos, key_pos, seq_length):
    score_scale = HD ** (-0.5)
    key_live = key_pos < seq_length
    block_rows = math.gcd(512, query_rows.shape[0])

    def one_block(pieces):
        query_blk, pos_blk = pieces
        scores = low_back(jnp.dot(query_blk, key_part.T, precision=HIGH) * score_scale)
        allowed = (key_pos[None, :] <= pos_blk[:, None]) & key_live[None, :]
        scores = jnp.where(allowed, scores, MASKED)
        probs = jax.nn.softmax(scores, axis=-1)
        return jnp.dot(low(probs), value_part, precision=HIGH)
    outputs = lax.map(jax.checkpoint(one_block), (query_rows.reshape(-1, block_rows, HD), query_pos.reshape(-1, block_rows)))
    return outputs.reshape(-1, HD)

def one_sequence(param_set, x_seq, seq_length, positions):
    first_gain, first_shift, query_weight, query_bias, keyval_weight, value_bias, output_weight, output_bias, second_gain, second_shift, up_weight, up_bias, down_weight, down_bias = param_set
    normed_one = low(layer_norm(x_seq, first_gain, first_shift))
    query = round_both(jnp.dot(normed_one, query_weight, precision=HIGH) + query_bias)
    keyval_bias = jnp.concatenate([jnp.zeros_like(value_bias), value_bias])
    keyval = round_both(jnp.dot(normed_one, keyval_weight, precision=HIGH) + keyval_bias)
    query_pos = jnp.repeat(positions, H)
    attended = attend(query.reshape(-1, HD), keyval[:, :HD], keyval[:, HD:], query_pos, positions, seq_length)
    attended = round_both(attended.reshape(x_seq.shape[0], MODEL_WIDTH))
    mixed = x_seq + low_back(jnp.dot(attended, output_weight, precision=HIGH) + output_bias)
    normed_two = low(layer_norm(mixed, second_gain, second_shift))
    upward = low_back(jnp.dot(normed_two, up_weight, precision=HIGH) + up_bias)
    middle = low(gelu_tanh(upward))
    branch = low_back(jnp.dot(middle, down_weight, precision=HIGH) + down_bias)
    valid = (positions < seq_length).astype(x_seq.dtype)[:, None]
    return valid * (mixed + branch)

def reference(tokens, lengths, block_map, first_gain, first_shift, query_weight, query_bias, keyval_weight, value_bias, output_weight, output_bias, second_gain, second_shift, up_weight, up_bias, down_weight, down_bias, cotangent):
    offsets = jnp.arange(BLOCK_POSITIONS, dtype=jnp.int32)
    positions = (block_map[:, None] * BLOCK_POSITIONS + offsets[None, :]).reshape(-1).astype(jnp.int32)
    params = tuple((weight.astype(jnp.float32) for weight in (first_gain, first_shift, query_weight, query_bias, keyval_weight, value_bias, output_weight, output_bias, second_gain, second_shift, up_weight, up_bias, down_weight, down_bias)))
    input_sequences = tokens.astype(jnp.float32).reshape(SEQUENCE_TOTAL, BLOCKS_PER_SEQ * BLOCK_POSITIONS, MODEL_WIDTH)

    def whole(x_all, param_set):

        def step(carry, pieces):
            return (carry, one_sequence(param_set, pieces[0], pieces[1], positions))
        return lax.scan(jax.checkpoint(step), None, (x_all, lengths))[1]
    layer_vals, backward_function = jax.vjp(whole, input_sequences, params)
    input_gradient, gradient_tuple = backward_function(cotangent.astype(jnp.float32).reshape(SEQUENCE_TOTAL, BLOCKS_PER_SEQ * BLOCK_POSITIONS, MODEL_WIDTH))
    return (layer_vals.reshape(tokens.shape).astype(jnp.bfloat16), input_gradient.reshape(tokens.shape), gradient_tuple[0], gradient_tuple[1], gradient_tuple[2], gradient_tuple[3], gradient_tuple[4], gradient_tuple[5], gradient_tuple[6], gradient_tuple[7], gradient_tuple[8], gradient_tuple[9], gradient_tuple[10], gradient_tuple[11], gradient_tuple[12], gradient_tuple[13])
```

```python
import functools

import jax
import jax.numpy as jnp
from jax import lax
from jax.experimental import pallas as pl
from jax.experimental.pallas import tpu as pltpu
from jax.sharding import PartitionSpec as P

EPS = 1e-05
NEG = -1e30
MESH = pl.DeviceIdType.MESH
F32 = jnp.float32
BF16 = jnp.bfloat16

WIDTH = 768
HEADS = 12
HD = 64
FF = 3072
HALF = FF // 2
BLK = 128
ROWS = 2 * BLK
GROUPS = HEADS // 2
PEERS = 8
N_A, N_B = 8, 7
ITEMS = N_A + N_B + 2
KEYS = ITEMS * BLK
SEMS = 224


def dot(left, right):
    return jnp.dot(left, right, preferred_element_type=F32)


def dot_nt(left, right):
    return lax.dot_general(left, right, (((1,), (1,)), ((), ())), preferred_element_type=F32)


def normalize(values):
    centre = values - jnp.mean(values, -1, keepdims=True)
    spread = jnp.mean(centre * centre, -1, keepdims=True)
    rate = lax.rsqrt(spread + EPS)
    return centre * rate, rate


def norm_back(normed, rate, grad, gain):
    scaled = grad * gain
    first = jnp.mean(scaled, -1, keepdims=True)
    second = jnp.mean(scaled * normed, -1, keepdims=True)
    return rate * (scaled - first - normed * second)


def layer_kernel(
    lengths,
    block_map,
    tokens,
    cotangent,
    vecs,
    wq,
    wkv,
    wo,
    wup,
    wdn,
    out_ref,
    ing_ref,
    gq_ref,
    go_ref,
    gt_ref,
    gup_ref,
    gdn_ref,
    f_vec,
    f_q,
    f_kv,
    f_o,
    f_up,
    r_up,
    f_dn,
    g_q,
    g_o,
    g_t,
    g_up,
    g_dn,
    rc_q,
    rc_o,
    rz_q,
    rz_o,
    rz_up,
    rz_dn,
    s_up,
    s_dn,
    ry_q,
    ry_o,
    ry_up,
    ry_dn,
    rx_up,
    rx_dn,
    rh_up,
    rh_dn,
    f2_up,
    f2_dn,
    r_t,
    c_q,
    c_o,
    c_t,
    kv_all,
    dkv_out,
    dkv_in,
    k_both,
    v_both,
    kt_both,
    vt_both,
    q_both,
    q_rows,
    probs,
    score,
    acc,
    o_norm,
    l_inv,
    att_t,
    do_both,
    do_rows,
    x_low,
    xn,
    xn_t,
    mixed_s,
    n2s,
    gos,
    mid,
    dup,
    part_out,
    part_in,
    dsec_own,
    dsec_out,
    dsec_in,
    send_sem,
    recv_sem,
    local_sem,
):
    ctx = lax.axis_index("ctx")
    fs = lax.axis_index("fsdp")
    zh, xx = ctx // 4, ctx % 4
    yy, zl, co = fs // 4, (fs // 2) % 2, fs % 2
    oz, oc = 1 - zl, 1 - co

    def peer(j):
        return ((zh + j // 4) % 2) * 4 + (xx + j % 4) % 4

    def from_peer(j):
        return ((zh + j // 4) % 2) * 4 + (xx + 4 - j % 4) % 4

    def shard_peer(k):
        return ((yy + k // 4) % 4) * 4 + ((zl + (k // 2) % 2) % 2) * 2 + (co + k % 2) % 2

    sib = (ctx, fs + 1 - 2 * co)
    z_near = (ctx, fs + 2 - 4 * zl)
    z_far = (ctx + 4 - 8 * zh, fs + 2 - 4 * zl)
    z_of = (z_near, z_far)

    def y_peer(k):
        return (ctx, ((yy + k) % 4) * 4 + zl * 2 + co)

    def x_peer(k):
        return (zh * 4 + (xx + k) % 4, fs)

    h_peer = (ctx + 4 - 8 * zh, fs)

    count = [0]
    started = []

    def send(src, dst, to):
        i = count[0]
        count[0] += 1
        copy = pltpu.make_async_remote_copy(
            src_ref=src,
            dst_ref=dst,
            send_sem=send_sem.at[i],
            recv_sem=recv_sem.at[i],
            device_id=to,
            device_id_type=MESH,
        )
        copy.start()
        started.append(copy)
        return copy

    def arrived(copies):
        for copy in copies:
            copy.wait_recv()

    locals_ = []

    def keep(src, dst):
        i = len(locals_)
        copy = pltpu.make_async_copy(src, dst, local_sem.at[i])
        copy.start()
        locals_.append(copy)
        return copy

    barrier = pltpu.get_barrier_semaphore()
    greeted = [(peer(j), fs) for j in range(1, PEERS)]
    greeted += [(ctx, shard_peer(k)) for k in range(1, 16)]
    greeted += [z_far]
    for device in greeted:
        pl.semaphore_signal(barrier, inc=1, device_id=device, device_id_type=MESH)
    pl.semaphore_wait(barrier, len(greeted))

    def gather_y(src, full):
        out = [send(src, full.at[yy, zl, co], y_peer(k)) for k in (1, 2, 3)]
        return out, keep(src, full.at[yy, zl, co])

    def gather_z(full):
        return [
            send(
                full.at[pl.ds(2 * e, 2), zl, co], full.at[pl.ds(2 * e, 2), zl, co], z_of[e]
            )
            for e in (0, 1)
        ]

    attn = ((vecs, f_vec), (wkv, f_kv), (wq, f_q), (wo, f_o))
    step_y = [gather_y(src, full) for src, full in attn]

    slot0, slot1 = block_map[2 * ctx], block_map[2 * ctx + 1]
    low = jnp.minimum(slot0, slot1)
    swap = slot0 > slot1
    length = lengths[0]

    t0, t1 = tokens[0], tokens[1]
    x_low[0:BLK] = jnp.where(swap, t1, t0)
    x_low[BLK:ROWS] = jnp.where(swap, t0, t1)

    row = lax.broadcasted_iota(jnp.int32, (ROWS, 1), 0)
    pos = jnp.where(row < BLK, low * BLK, (14 - low) * BLK) + row
    valid = (pos < length).astype(F32)

    def grad_out():
        c0, c1 = cotangent[0], cotangent[1]
        both = jnp.concatenate([jnp.where(swap, c1, c0), jnp.where(swap, c0, c1)], 0)
        return valid * both

    gos[0] = grad_out().astype(BF16)
    go_copy = send(gos.at[0], gos.at[1], sib)

    def gather_c(full, z):
        return send(full.at[:, z, co], full.at[:, z, co], sib)

    step_z, step_c = [], []
    for (_, full), (copies, own) in zip(attn, step_y):
        arrived(copies)
        own.wait()
        step_z.append(gather_z(full))
        step_c.append(gather_c(full, zl))

    def mine(c):
        return pl.ds(pl.multiple_of(c * HALF, HALF), HALF)

    def up_y():
        out = [send(wup.at[:, mine(co)], f_up.at[yy, zl, co], y_peer(k)) for k in (1, 2, 3)]
        out += [send(wup.at[:, mine(oc)], r_up.at[yy, zl], y_peer(k)) for k in (1, 2, 3)]
        return out, [keep(wup.at[:, mine(co)], f_up.at[yy, zl, co]), keep(wup.at[:, mine(oc)], r_up.at[yy, zl])]

    def up_z():
        out = []
        for e in (0, 1):
            part_y = pl.ds(2 * e, 2)
            out.append(send(f_up.at[part_y, zl, co], f_up.at[part_y, zl, co], z_of[e]))
            out.append(send(r_up.at[part_y, zl], r_up.at[part_y, zl], z_of[e]))
        return out

    def dn_slot(y, z):
        other = y // 2 + co - 2 * (y // 2) * co
        return (1 - other) * ((y % 2) * 4 + z * 2 + co) + other * (8 + (y % 2) * 2 + z)

    def dn_y():
        dst = f_dn.at[dn_slot(yy, zl)]
        return [send(wdn, dst, y_peer(k)) for k in (1, 2, 3)], [keep(wdn, dst)]

    def dn_z():
        return [
            send(f_dn.at[dn_slot(y, zl)], f_dn.at[dn_slot(y, zl)], z_of[y // 2]) for y in range(4)
        ]

    y_up, own_up = up_y()
    y_dn, own_dn = dn_y()

    for i, (_, full) in enumerate(attn):
        arrived(step_z[i])
        step_c.append(gather_c(full, oz))

    def up_c(z):
        return [send(r_up.at[:, z], f_up.at[:, z, co], sib)]

    def dn_c(z):
        return [send(f_dn.at[8 + y * 2 + z], f_dn.at[y * 4 + z * 2 + co], sib) for y in (0, 1)]

    arrived([step_c[0], step_c[4]])
    vec = f_vec[...].astype(F32).reshape(16, 16, WIDTH)
    vec = jnp.sum(vec, 0)
    gain1, shift1, qbias, obias = vec[0:1], vec[1:2], vec[2:3], vec[3:4]
    gain2, shift2, dbias, kvbias = vec[4:5], vec[5:6], vec[6:7], vec[7:8, 0 : 2 * HD]

    n1, _ = normalize(x_low[...].astype(F32))
    xn_v = n1 * gain1 + shift1
    xn[...] = xn_v.astype(BF16)
    xn_t[...] = xn_v.T.astype(BF16)

    arrived([step_c[1], step_c[5]])
    kv = dot(xn[...], f_kv[...].reshape(WIDTH, 2 * HD)) + kvbias
    kv_all[0] = kv.astype(BF16)
    kv_copies = [send(kv_all.at[0], kv_all.at[j], (peer(j), fs)) for j in range(1, PEERS)]

    arrived(y_up)
    for copy in own_up:
        copy.wait()
    z_up = up_z()
    c_up = up_c(zl)
    arrived(y_dn)
    for copy in own_dn:
        copy.wait()
    z_dn = dn_z()
    c_dn = dn_c(zl)

    arrived([step_c[2], step_c[6]])
    q = dot(xn[...], f_q[...].reshape(WIDTH, WIDTH)) + qbias
    q = (q.astype(BF16).astype(F32) * (HD**-0.5)).T
    for g in range(GROUPS):
        h0, h1 = q[g * BLK : g * BLK + HD], q[g * BLK + HD : (g + 1) * BLK]
        both = jnp.concatenate(
            [
                jnp.concatenate([h0[:, BLK:], h1[:, BLK:]], 1),
                jnp.concatenate([h0[:, :BLK], h1[:, :BLK]], 1),
            ],
            0,
        )
        q_both[g] = both.astype(BF16)
        q_rows[g] = both.T.astype(BF16)

    arrived(kv_copies)
    lane = lax.broadcasted_iota(jnp.int32, (BLK, BLK), 1)
    sub = lax.broadcasted_iota(jnp.int32, (BLK, BLK), 0)
    extra = lax.broadcasted_iota(jnp.int32, (16, BLK), 0)

    picks, limits = [], []
    for j in range(1, PEERS):
        c = from_peer(j)
        other = jnp.minimum(block_map[2 * c], block_map[2 * c + 1])
        high = other > low
        picks.append(jnp.where(high, 1.0, 0.0).astype(F32))
        limits.append(length - jnp.where(high, 15 - other, other) * BLK)

    def place(item, block, to_high):
        rows = pl.ds(item * BLK, BLK)
        left = jnp.where(lane < HD, to_high, 1.0 - to_high)
        kk = jnp.concatenate([block[:, :HD], block[:, :HD]], 1) * left
        vv = jnp.concatenate([block[:, HD:], block[:, HD:]], 1) * left
        k_both[rows] = kk.astype(BF16)
        v_both[rows] = vv.astype(BF16)
        kt_both[:, rows] = kk.T.astype(BF16)
        vt_both[0:BLK, rows] = vv.T.astype(BF16)
        vt_both[BLK : BLK + 16, rows] = jnp.where(extra < 8, to_high, 1.0 - to_high).astype(BF16)

    one, zero = jnp.float32(1.0), jnp.float32(0.0)
    for j in range(PEERS):
        block = kv_all[j].astype(F32)
        place(j, block[:BLK], one)
        if j:
            pick = picks[j - 1]
            place(N_A + j - 1, jnp.where(pick > 0.5, block[BLK:], block[:BLK]), pick)
        else:
            place(N_A + N_B, block[BLK:], one)
            place(N_A + N_B + 1, block[:BLK], zero)

    sub2 = lax.broadcasted_iota(jnp.int32, (BLK, ROWS), 0)
    lane2 = lax.broadcasted_iota(jnp.int32, (BLK, ROWS), 1) % BLK

    def fold(values, op):
        return op(values.reshape(BLK // 8, 8, ROWS), 0)

    def forward_group(g, carry):
        score[...] = dot(k_both[...], q_both[g])
        top_h = jnp.full((8, ROWS), NEG, F32)
        top_l = jnp.full((8, ROWS), NEG, F32)
        for item in range(ITEMS):
            rows = slice(item * BLK, (item + 1) * BLK)
            s = score[rows]
            if item < N_A:
                top_h = jnp.maximum(top_h, fold(s, jnp.max))
            elif item < N_A + N_B:
                j = item - N_A
                s = jnp.where(sub2 < limits[j], s, NEG)
                score[rows] = s
                best = fold(s, jnp.max)
                top_h = jnp.maximum(top_h, jnp.where(picks[j] > 0.5, best, NEG))
                top_l = jnp.maximum(top_l, jnp.where(picks[j] > 0.5, NEG, best))
            elif item == N_A + N_B:
                limit = length - (15 - low) * BLK
                s = jnp.where((sub2 <= lane2) & (sub2 < limit), s, NEG)
                score[rows] = s
                top_h = jnp.maximum(top_h, fold(s, jnp.max))
            else:
                s = jnp.where(sub2 <= lane2, s, NEG)
                score[rows] = s
                top_l = jnp.maximum(top_l, fold(s, jnp.max))
        top_h = jnp.max(top_h, 0, keepdims=True)
        top_l = jnp.max(top_l, 0, keepdims=True)
        for item in range(ITEMS):
            rows = slice(item * BLK, (item + 1) * BLK)
            if item < N_A or item == N_A + N_B:
                top = top_h
            elif item < N_A + N_B:
                top = jnp.where(picks[item - N_A] > 0.5, top_h, top_l)
            else:
                top = top_l
            probs[g, rows] = jnp.exp(score[rows] - top).astype(BF16)
        o = dot(vt_both[...], probs[g])
        inv_h = 1.0 / o[BLK : BLK + 1]
        inv_l = 1.0 / o[BLK + 8 : BLK + 9]
        high, lower = o[0:HD] * inv_h, o[HD:BLK] * inv_l
        o_norm[g, 0:HD] = high
        o_norm[g, HD:BLK] = lower
        l_inv[g, 0:8] = jnp.broadcast_to(inv_h, (8, ROWS))
        l_inv[g, 8:16] = jnp.broadcast_to(inv_l, (8, ROWS))
        att_t[g, 0:HD, 0:BLK] = lower[:, :BLK].astype(BF16)
        att_t[g, 0:HD, BLK:ROWS] = high[:, :BLK].astype(BF16)
        att_t[g, HD:BLK, 0:BLK] = lower[:, BLK:].astype(BF16)
        att_t[g, HD:BLK, BLK:ROWS] = high[:, BLK:].astype(BF16)
        return carry

    lax.fori_loop(0, GROUPS // 2, forward_group, 0)
    arrived(z_up)
    c_up += up_c(oz)
    arrived(z_dn)
    c_dn += dn_c(oz)
    lax.fori_loop(GROUPS // 2, GROUPS, forward_group, 0)

    arrived([step_c[3], step_c[7]])
    attended = att_t[...].reshape(WIDTH, ROWS).astype(F32).T.astype(BF16)
    mixed = x_low[...].astype(F32) + dot(attended, f_o[...].reshape(WIDTH, WIDTH)) + obias
    mixed_s[...] = mixed
    n2, _ = normalize(mixed)
    n2s[0] = (n2 * gain2 + shift2).astype(BF16)
    n2_copy = send(n2s.at[0], n2s.at[1], sib)

    arrived([go_copy] + c_up + c_dn + [n2_copy])
    sub_cols = 256
    n_sub = HALF // sub_cols
    coef = 0.7978845608028654

    up_sums = []
    for s in range(n_sub):
        cols = slice(s * sub_cols, (s + 1) * sub_cols)
        per = WIDTH // sub_cols
        bias_row = jnp.where(co == 0, vec[8 + s // per : 9 + s // per], vec[10 + s // per : 11 + s // per])
        bias = bias_row[:, (s % per) * sub_cols : (s % per + 1) * sub_cols]
        n2b = n2s[...].reshape(2 * ROWS, WIDTH)
        gob = gos[...].reshape(2 * ROWS, WIDTH)
        up = dot(n2b, f_up[:, :, :, :, cols].reshape(WIDTH, sub_cols)) + bias
        w_rows = f_dn[4 * (s // per) : 4 * (s // per) + 4].reshape(WIDTH, WIDTH)
        w_rows = w_rows[(s % per) * sub_cols : (s % per + 1) * sub_cols]
        dmid = dot_nt(gob, w_rows)
        square = up * up
        th = jnp.tanh(coef * up * (1.0 + 0.044715 * square))
        half_sum = 0.5 + 0.5 * th
        mid[:, cols] = (up * half_sum).astype(BF16)
        slope = half_sum + 0.5 * up * (1.0 - th * th) * coef * (1.0 + 3 * 0.044715 * square)
        du = (dmid * slope).astype(BF16)
        dup[:, cols] = du
        up_sums.append(jnp.sum(du.astype(F32), 0, keepdims=True))

    thirds = [slice(256 * n, 256 * (n + 1)) for n in range(3)]
    for n in thirds:
        w = f_up[...].reshape(WIDTH, HALF)[n]
        piece = dot_nt(dup[...], w)
        dsec_own[:, n] = piece[:ROWS]
        dsec_out[:, n] = piece[ROWS:].astype(BF16)
    dsec_copy = send(dsec_out, dsec_in, sib)

    z_dn = []
    for j in (0, 1):
        m_t = mid[:, j * WIDTH : (j + 1) * WIDTH].astype(F32).T.astype(BF16)
        for n in thirds:
            piece = dot(m_t, gos[:, :, n].reshape(2 * ROWS, 256))
            g_dn[j, :, :, :, n] = piece.astype(BF16).reshape(2, 2, 192, 256)
        z_dn.append(send(g_dn.at[j, oz], rz_dn.at[j], z_of[j]))
    n2_t = n2s[...].reshape(2 * ROWS, WIDTH).astype(F32).T.astype(BF16)
    for s in range(n_sub):
        cols = slice(s * sub_cols, (s + 1) * sub_cols)
        piece = dot(n2_t, dup[:, cols])
        g_up[:, :, :, :, cols] = piece.astype(BF16).reshape(4, 2, 2, 48, sub_cols)
    z_up = [send(g_up.at[pl.ds(2 * e, 2), oz], rz_up.at[pl.ds(2 * e, 2)], z_of[e]) for e in (0, 1)]

    arrived([dsec_copy])
    dsec = dsec_own[...] + dsec_in[...].astype(F32)
    n2, rate2 = normalize(mixed_s[...])
    sum_gain2 = jnp.sum(dsec * n2, 0, keepdims=True)
    sum_shift2 = jnp.sum(dsec, 0, keepdims=True)
    dmix = grad_out() + norm_back(n2, rate2, dsec, gain2)
    ing_ref[0] = dmix[:BLK]
    ing_ref[1] = dmix[BLK:]
    dmix_low = dmix.astype(BF16)
    dmix_r = dmix_low.astype(F32)
    sum_obias = jnp.sum(dmix_r, 0, keepdims=True)
    sum_dbias = jnp.sum(gos[0].astype(F32), 0, keepdims=True)

    g_o[...] = (
        dot(att_t[...].reshape(WIDTH, ROWS), dmix_low).astype(BF16).reshape(4, 2, 2, 48, WIDTH)
    )
    c_go = send(g_o.at[:, :, oc], rc_o, sib)

    for n in thirds:
        piece = dot(mid[...], f_dn[0:8, :, n].reshape(HALF, 256))
        dsec_own[:, n] = piece[:ROWS]
        part_out[:, n] = piece[ROWS:].astype(BF16)
    part_copy = send(part_out, part_in, sib)

    datt = dot(f_o[...].reshape(WIDTH, WIDTH), dmix_r.T.astype(BF16)).astype(BF16).astype(F32)
    deltas = []
    for g in range(GROUPS):
        h0, h1 = datt[g * BLK : g * BLK + HD], datt[g * BLK + HD : (g + 1) * BLK]
        high = jnp.concatenate([h0[:, BLK:], h1[:, BLK:]], 1) * l_inv[g, 0:1]
        lower = jnp.concatenate([h0[:, :BLK], h1[:, :BLK]], 1) * l_inv[g, 8:9]
        both = jnp.concatenate([high, lower], 0)
        do_both[g] = both.astype(BF16)
        do_rows[g] = both.T.astype(BF16)
        both = both.astype(BF16).astype(F32) * o_norm[g]
        l_inv[g, 0:8] = jnp.broadcast_to(jnp.sum(both[:HD], 0, keepdims=True), (8, ROWS))
        l_inv[g, 8:16] = jnp.broadcast_to(jnp.sum(both[HD:], 0, keepdims=True), (8, ROWS))

    def dn_after_z():
        for j in (0, 1):
            arrived([z_dn[j]])
            total = g_dn[j, zl].astype(F32) + rz_dn[j].astype(F32)
            g_dn[j, zl] = total.astype(BF16)
        copies = []
        for j in (0, 1):
            copies.append(send(g_dn.at[j, zl, oc], s_dn.at[2 * co + j], sib))
            s_dn[2 * co + j] = g_dn[j, zl, co]
        return copies

    def up_after_z():
        copies = []
        for e in (0, 1):
            arrived([z_up[e]])
            part_y = pl.ds(2 * e, 2)
            total = g_up[part_y, zl].astype(F32) + rz_up[part_y].astype(F32)
            g_up[part_y, zl] = total.astype(BF16)
            copies.append(send(g_up.at[part_y, zl, oc], s_up.at[part_y, :, mine(co)], sib))
            s_up[part_y, :, mine(co)] = g_up[part_y, zl, co]
        return copies

    def y_sends(src, dst):
        return [send(src.at[(yy + k) % 4], dst.at[k - 1], y_peer(k)) for k in (1, 2, 3)]

    acc[...] = jnp.zeros_like(acc)

    def backward_group(g, carry):
        acc[:, BLK:ROWS] += dot(probs[g], do_rows[g])
        delta_h, delta_l = l_inv[g, 0:1], l_inv[g, 8:9]
        score[...] = dot(v_both[...], do_both[g])
        for item in range(ITEMS):
            rows = slice(item * BLK, (item + 1) * BLK)
            if item < N_A or item == N_A + N_B:
                delta = delta_h
            elif item < N_A + N_B:
                delta = jnp.where(picks[item - N_A] > 0.5, delta_h, delta_l)
            else:
                delta = delta_l
            probs[g, rows] = (probs[g, rows].astype(F32) * (score[rows] - delta)).astype(BF16)
        dq = dot(kt_both[...], probs[g]) * (HD**-0.5)
        do_both[g, 0:HD, 0:BLK] = dq[HD:, :BLK].astype(BF16)
        do_both[g, 0:HD, BLK:ROWS] = dq[:HD, :BLK].astype(BF16)
        do_both[g, HD:BLK, 0:BLK] = dq[HD:, BLK:].astype(BF16)
        do_both[g, HD:BLK, BLK:ROWS] = dq[:HD, BLK:].astype(BF16)
        acc[:, 0:BLK] += dot(probs[g], q_rows[g])
        return carry

    lax.fori_loop(0, 2, backward_group, 0)

    c_dn = dn_after_z()
    c_up = up_after_z()
    arrived([c_go])
    g_o[:, :, co] = (g_o[:, :, co].astype(F32) + rc_o[...].astype(F32)).astype(BF16)

    def z_sends(grad, dst):
        return [
            send(grad.at[pl.ds(2 * e, 2), oz, co], dst.at[pl.ds(2 * e, 2)], z_of[e]) for e in (0, 1)
        ]

    z_o = z_sends(g_o, rz_o)
    lax.fori_loop(2, 4, backward_group, 0)

    arrived(c_dn)
    y_dn = y_sends(s_dn, ry_dn)
    arrived(c_up)
    y_up = y_sends(s_up, ry_up)

    def after_z(copies, grad, got):
        arrived(copies)
        grad[:, zl, co] = (grad[:, zl, co].astype(F32) + got[...].astype(F32)).astype(BF16)
        return [
            send(grad.at[(yy + k) % 4, zl, co], ry.at[k - 1], y_peer(k))
            for ry in [{id(rz_o): ry_o, id(rz_q): ry_q}[id(got)]]
            for k in (1, 2, 3)
        ]

    y_o = after_z(z_o, g_o, rz_o)
    lax.fori_loop(4, 6, backward_group, 0)

    def halves(item, second):
        rows = slice(item * BLK, (item + 1) * BLK)
        at = HD if second else 0
        return jnp.concatenate(
            [acc[rows, at : at + HD], acc[rows, BLK + at : BLK + at + HD]], 1
        )

    dkv_copies = []
    for j in range(1, PEERS):
        item = N_A + j - 1
        pick = picks[j - 1]
        other = jnp.where(pick > 0.5, halves(item, False), halves(item, True))
        dkv_out[j, 0:BLK] = (halves(j, False) + (1.0 - pick) * other).astype(BF16)
        dkv_out[j, BLK:ROWS] = (pick * other).astype(BF16)
        dkv_copies.append(send(dkv_out.at[j], dkv_in.at[j], (from_peer(j), fs)))

    dq = do_both[...].reshape(WIDTH, ROWS).astype(F32).T
    sum_qbias = jnp.sum(dq, 0, keepdims=True)
    dq = dq.astype(BF16)
    g_q[...] = dot(xn_t[...], dq).astype(BF16).reshape(4, 2, 2, 48, WIDTH)
    c_gq = send(g_q.at[:, :, oc], rc_q, sib)
    dfirst = dot_nt(dq, f_q[...].reshape(WIDTH, WIDTH))

    def y_sum(own, got):
        total = own.astype(F32)
        for k in range(3):
            total = total + got[k].astype(F32)
        return total

    arrived(y_dn)
    s_dn[yy] = y_sum(s_dn[yy], ry_dn).astype(BF16)
    arrived(y_up)
    s_up[yy] = y_sum(s_up[yy], ry_up).astype(BF16)

    def quarter_dn(k):
        return pl.ds(pl.multiple_of(k * 48, 16), 48)

    def quarter_up(k):
        return pl.ds(pl.multiple_of(k * WIDTH, WIDTH), WIDTH)

    x_dn, x_up = [], []
    for k in (1, 2, 3):
        q4 = (xx + k) % 4
        x_dn.append(send(s_dn.at[yy, quarter_dn(q4)], rx_dn.at[k - 1], x_peer(k)))
        x_up.append(send(s_up.at[yy, :, quarter_up(q4)], rx_up.at[k - 1], x_peer(k)))

    arrived(y_o)
    g_o[yy, zl, co] = y_sum(g_o[yy, zl, co], ry_o).astype(BF16)

    def ctx_sends(src, dst):
        return [send(src, dst.at[j], (peer(j), fs)) for j in range(1, PEERS)]

    ctx_o = ctx_sends(g_o.at[yy, zl, co], c_o)

    arrived([c_gq])
    g_q[:, :, co] = (g_q[:, :, co].astype(F32) + rc_q[...].astype(F32)).astype(BF16)
    z_q = z_sends(g_q, rz_q)

    top = halves(0, False) + halves(N_A + N_B + 1, True)
    dkv = jnp.concatenate([top, halves(N_A + N_B, False)], 0)
    arrived(dkv_copies)
    for j in range(1, PEERS):
        dkv = dkv + dkv_in[j].astype(F32)
    dkv = dkv.astype(BF16)
    sum_kv = jnp.sum(dkv.astype(F32), 0, keepdims=True)
    g_kv = dot(xn_t[...], dkv)
    dfirst = dfirst + dot_nt(dkv, f_kv[...].reshape(WIDTH, 2 * HD))

    n1, rate1 = normalize(x_low[...].astype(F32))
    sum_gain1 = jnp.sum(dfirst * n1, 0, keepdims=True)
    sum_shift1 = jnp.sum(dfirst, 0, keepdims=True)

    zeros = jnp.zeros((1, WIDTH), F32)
    columns = jnp.concatenate(
        [zeros] * 4
        + [sum_dbias, sum_gain2, sum_shift2, sum_obias, sum_gain1, sum_shift1, sum_qbias]
        + [jnp.zeros((BLK - 11, WIDTH), F32)],
        0,
    ).T
    lanes = lax.broadcasted_iota(jnp.int32, (WIDTH, BLK), 1)
    columns = jnp.where(lanes < HD, columns, sum_kv)
    g_t[:, :, :, :, 0:BLK] = g_kv.astype(BF16).reshape(4, 2, 2, 48, BLK)
    g_t[:, :, :, :, BLK:ROWS] = columns.astype(BF16).reshape(4, 2, 2, 48, BLK)
    lanes = lax.broadcasted_iota(jnp.int32, (48, BLK), 1)
    for j in (0, 1):
        sums = jnp.concatenate(up_sums[3 * j : 3 * j + 3], 1)
        sums = jnp.broadcast_to(sums, (BLK, WIDTH)).T
        for k in range(4):
            block = g_t[2 * co + j, k // 2, k % 2, :, BLK:ROWS].astype(F32)
            for r in range(4):
                at = k * 192 + r * 48
                block = jnp.where(lanes == r, sums[at : at + 48], block)
            g_t[2 * co + j, k // 2, k % 2, :, BLK:ROWS] = block.astype(BF16)

    t_copies = []
    for k in range(1, 16):
        dst = shard_peer(k)
        t_copies.append(
            send(g_t.at[dst // 4, (dst // 2) % 2, dst % 2], r_t.at[k], (ctx, dst))
        )

    y_q = after_z(z_q, g_q, rz_q)

    ing = ing_ref[...].reshape(ROWS, WIDTH) + norm_back(n1, rate1, dfirst, gain1)
    ing_ref[0] = jnp.where(swap, ing[BLK:], ing[:BLK])
    ing_ref[1] = jnp.where(swap, ing[:BLK], ing[BLK:])
    arrived([part_copy])
    res = valid * (mixed_s[...] + dsec_own[...] + part_in[...].astype(F32) + dbias)
    out_ref[0] = jnp.where(swap, res[BLK:], res[:BLK]).astype(BF16)
    out_ref[1] = jnp.where(swap, res[:BLK], res[BLK:]).astype(BF16)

    h_out = []
    arrived(x_dn)
    rh_dn[1] = y_sum(s_dn[yy, quarter_dn(xx)], rx_dn).astype(BF16)
    h_out.append(send(rh_dn.at[1], rh_dn.at[0], h_peer))
    arrived(x_up)
    rh_up[1] = y_sum(s_up[yy, :, quarter_up(xx)], rx_up).astype(BF16)
    h_out.append(send(rh_up.at[1], rh_up.at[0], h_peer))

    arrived(t_copies)
    total = g_t[yy, zl, co].astype(F32)
    for k in range(1, 16):
        total = total + r_t[k].astype(F32)
    c_t[0] = total.astype(BF16)
    ctx_t = ctx_sends(c_t.at[0], c_t)

    arrived(y_q)
    g_q[yy, zl, co] = y_sum(g_q[yy, zl, co], ry_q).astype(BF16)
    ctx_q = ctx_sends(g_q.at[yy, zl, co], c_q)

    arrived([h_out[0]])
    f2_dn[xx] = (rh_dn[0].astype(F32) + rh_dn[1].astype(F32)).astype(BF16)
    a_dn = [send(f2_dn.at[xx], f2_dn.at[xx], x_peer(k)) for k in (1, 2, 3)]
    arrived([h_out[1]])
    f2_up[xx] = (rh_up[0].astype(F32) + rh_up[1].astype(F32)).astype(BF16)
    a_up = [send(f2_up.at[xx], f2_up.at[xx], x_peer(k)) for k in (1, 2, 3)]

    def ctx_sum(copies, own, got):
        arrived(copies)
        total = own.astype(F32)
        for j in range(1, PEERS):
            total = total + got[j].astype(F32)
        return total

    go_ref[...] = ctx_sum(ctx_o, g_o[yy, zl, co], c_o)
    gt_ref[...] = ctx_sum(ctx_t, c_t[0], c_t)
    gq_ref[...] = ctx_sum(ctx_q, g_q[yy, zl, co], c_q)
    arrived(a_dn)
    gdn_ref[...] = f2_dn[...].astype(F32).reshape(192, WIDTH)
    arrived(a_up)
    for k in range(4):
        gup_ref[:, k * WIDTH : (k + 1) * WIDTH] = f2_up[k].astype(F32)

    for copy in started:
        copy.wait_send()


def expand(values, at, fs):
    first = jnp.zeros((16, WIDTH), BF16)
    for row, value in enumerate(values):
        first = lax.dynamic_update_slice(first, value[None], (row, fs * 48))
    value_bias, up_bias = at
    first = lax.dynamic_update_slice(first, value_bias[None], (7, HD + fs * 4))
    return lax.dynamic_update_slice(first, up_bias[None], (8 + fs // 4, (fs % 4) * 192))


def shards(
    tokens,
    lengths,
    block_map,
    first_gain,
    first_shift,
    query_weight,
    query_bias,
    keyval_weight,
    value_bias,
    output_weight,
    output_bias,
    second_gain,
    second_shift,
    up_weight,
    up_bias,
    down_weight,
    down_bias,
    cotangent,
):
    fs = lax.axis_index("fsdp")
    vecs = expand(
        (first_gain, first_shift, query_bias, output_bias, second_gain, second_shift, down_bias),
        (value_bias, up_bias),
        fs,
    )
    vmem = pl.BlockSpec(memory_space=pltpu.VMEM)
    smem = pl.BlockSpec(memory_space=pltpu.SMEM)
    hbm = pl.BlockSpec(memory_space=pl.ANY)

    def v(*shape, dtype=BF16):
        return pltpu.VMEM(shape, dtype)

    scratch = [
        v(4, 2, 2, 16, WIDTH),
        v(4, 2, 2, 48, WIDTH),
        v(4, 2, 2, 48, 2 * HD),
        v(4, 2, 2, 48, WIDTH),
        v(4, 2, 2, 48, HALF),
        v(4, 2, 48, HALF),
        v(12, 192, WIDTH),
        v(4, 2, 2, 48, WIDTH),
        v(4, 2, 2, 48, WIDTH),
        v(4, 2, 2, 48, 2 * BLK),
        v(4, 2, 2, 48, HALF),
        v(2, 2, 2, 192, WIDTH),
        v(4, 2, 48, WIDTH),
        v(4, 2, 48, WIDTH),
        v(4, 48, WIDTH),
        v(4, 48, WIDTH),
        v(4, 2, 48, HALF),
        v(2, 2, 192, WIDTH),
        v(4, 48, FF),
        v(4, 192, WIDTH),
        v(3, 48, WIDTH),
        v(3, 48, WIDTH),
        v(3, 48, FF),
        v(3, 192, WIDTH),
        v(3, 48, WIDTH),
        v(3, 48, WIDTH),
        v(2, 48, WIDTH),
        v(2, 48, WIDTH),
        v(4, 48, WIDTH),
        v(4, 48, WIDTH),
        v(16, 48, 2 * BLK),
        v(PEERS, 48, WIDTH),
        v(PEERS, 48, WIDTH),
        v(PEERS, 48, 2 * BLK),
        v(PEERS, ROWS, 2 * HD),
        v(PEERS, ROWS, 2 * HD),
        v(PEERS, ROWS, 2 * HD),
        v(KEYS, BLK),
        v(KEYS, BLK),
        v(BLK, KEYS),
        v(BLK + 16, KEYS),
        v(GROUPS, BLK, ROWS),
        v(GROUPS, ROWS, BLK),
        v(GROUPS, KEYS, ROWS),
        v(KEYS, ROWS, dtype=F32),
        v(KEYS, ROWS, dtype=F32),
        v(GROUPS, BLK, ROWS, dtype=F32),
        v(GROUPS, 16, ROWS, dtype=F32),
        v(GROUPS, BLK, ROWS),
        v(GROUPS, BLK, ROWS),
        v(GROUPS, ROWS, BLK),
        v(ROWS, WIDTH),
        v(ROWS, WIDTH),
        v(WIDTH, ROWS),
        v(ROWS, WIDTH, dtype=F32),
        v(2, ROWS, WIDTH),
        v(2, ROWS, WIDTH),
        v(2 * ROWS, HALF),
        v(2 * ROWS, HALF),
        v(ROWS, WIDTH),
        v(ROWS, WIDTH),
        v(ROWS, WIDTH, dtype=F32),
        v(ROWS, WIDTH),
        v(ROWS, WIDTH),
        pltpu.SemaphoreType.DMA((SEMS,)),
        pltpu.SemaphoreType.DMA((SEMS,)),
        pltpu.SemaphoreType.DMA((16,)),
    ]
    outs = pl.pallas_call(
        layer_kernel,
        out_shape=(
            jax.ShapeDtypeStruct((2, BLK, WIDTH), BF16),
            jax.ShapeDtypeStruct((2, BLK, WIDTH), F32),
            jax.ShapeDtypeStruct((48, WIDTH), F32),
            jax.ShapeDtypeStruct((48, WIDTH), F32),
            jax.ShapeDtypeStruct((48, 2 * BLK), F32),
            jax.ShapeDtypeStruct((48, FF), F32),
            jax.ShapeDtypeStruct((192, WIDTH), F32),
        ),
        in_specs=[smem, smem, vmem, vmem] + [hbm] * 6,
        out_specs=(vmem,) * 7,
        scratch_shapes=scratch,
        compiler_params=pltpu.CompilerParams(
            collective_id=0, has_side_effects=True, vmem_limit_bytes=62 * 2**20
        ),
    )(
        lengths,
        block_map,
        tokens[0],
        cotangent[0],
        vecs,
        query_weight,
        keyval_weight,
        output_weight,
        up_weight,
        down_weight,
    )
    layer_out, input_grad, g_query, g_output, g_tail, g_up, g_down = outs
    g_keyval = g_tail[:, : 2 * HD]

    def column(k):
        return g_tail[:, BLK + k]

    g_value_bias = lax.dynamic_slice(g_tail[0], (BLK + HD + fs * 4,), (4,))
    g_up_bias = g_tail[:, BLK : BLK + 4].T.reshape(192)
    return (
        layer_out[None],
        input_grad[None],
        column(8),
        column(9),
        g_query,
        column(10),
        g_keyval,
        g_value_bias,
        g_output,
        column(7),
        column(5),
        column(6),
        g_up,
        g_up_bias,
        g_down,
        column(4),
    )


def solution(mesh):
    rows, matrix, batch = P("fsdp"), P("fsdp", None), P("fsdp", "ctx", None, None)
    return jax.shard_map(
        shards,
        mesh=mesh,
        in_specs=(
            batch,
            rows,
            P(),
            rows,
            rows,
            matrix,
            rows,
            matrix,
            rows,
            matrix,
            rows,
            rows,
            rows,
            matrix,
            rows,
            matrix,
            rows,
            batch,
        ),
        out_specs=(
            batch,
            batch,
            rows,
            rows,
            matrix,
            rows,
            matrix,
            rows,
            matrix,
            rows,
            rows,
            rows,
            matrix,
            rows,
            matrix,
            rows,
        ),
        check_vma=False,
    )
```

```python
import functools

import jax
import jax.numpy as jnp
from jax import lax
from jax.experimental import pallas as pl
from jax.experimental.pallas import tpu as pltpu
from jax.sharding import PartitionSpec as P

EPS = 1e-05
NEG = -1e30
MESH = pl.DeviceIdType.MESH
F32 = jnp.float32
BF16 = jnp.bfloat16

WIDTH = 768
HEADS = 12
HD = 64
FF = 3072
HALF = FF // 2
BLK = 128
ROWS = 2 * BLK
GROUPS = HEADS // 2
PEERS = 8
N_A, N_B = 8, 7
ITEMS = N_A + N_B + 2
KEYS = ITEMS * BLK
SEMS = 300


class Chain:
    def __init__(self, *steps):
        self.steps = list(steps)
        self.flying = []

    def go(self, arrived):
        arrived(self.flying)
        self.flying = self.steps.pop(0)() if self.steps else []


def dot(left, right):
    return jnp.dot(left, right, preferred_element_type=F32)


def dot_nt(left, right):
    return lax.dot_general(left, right, (((1,), (1,)), ((), ())), preferred_element_type=F32)


def normalize(values):
    centre = values - jnp.mean(values, -1, keepdims=True)
    spread = jnp.mean(centre * centre, -1, keepdims=True)
    rate = lax.rsqrt(spread + EPS)
    return centre * rate, rate


def norm_back(normed, rate, grad, gain):
    scaled = grad * gain
    first = jnp.mean(scaled, -1, keepdims=True)
    second = jnp.mean(scaled * normed, -1, keepdims=True)
    return rate * (scaled - first - normed * second)


def layer_kernel(
    lengths,
    block_map,
    tokens_in,
    cotangent_in,
    own_gain1,
    own_shift1,
    own_qbias,
    own_vbias,
    own_obias,
    own_gain2,
    own_shift2,
    own_ubias,
    own_dbias,
    wq,
    wkv,
    wo,
    wup,
    wdn,
    out_hbm,
    ing_hbm,
    gq_hbm,
    go_hbm,
    gt_hbm,
    gup_hbm,
    gdn_hbm,
    tokens,
    cotangent,
    vecs,
    gq_ref,
    go_ref,
    gt_ref,
    gup_ref,
    gdn_ref,
    f_vec,
    f_q,
    f_kv,
    f_o,
    f_up,
    r_up,
    f_dn,
    g_q,
    g_o,
    g_t,
    g_up,
    g_dn,
    rc_q,
    rc_o,
    rz_q,
    rz_o,
    rz_up,
    rz_dn,
    s_up,
    s_dn,
    ry_q,
    ry_o,
    ry_up,
    ry_dn,
    rx_up,
    rx_dn,
    rh_up,
    rh_dn,
    f2_up,
    f2_dn,
    r_t,
    cx_q,
    cx_o,
    ch_q,
    ch_o,
    c_t,
    kv_all,
    dkv_out,
    dkv_in,
    k_both,
    v_both,
    kt_both,
    vt_both,
    q_both,
    q_rows,
    probs,
    score,
    acc,
    o_norm,
    l_inv,
    att_t,
    do_both,
    do_rows,
    x_low,
    xn,
    xn_t,
    mixed_s,
    n2s,
    gos,
    mid,
    dup,
    part_out,
    part_in,
    dsec_own,
    dsec_out,
    dsec_in,
    send_sem,
    recv_sem,
    local_sem,
):
    ctx = lax.axis_index("ctx")
    fs = lax.axis_index("fsdp")
    zh, xx = ctx // 4, ctx % 4
    yy, zl, co = fs // 4, (fs // 2) % 2, fs % 2
    oz, oc = 1 - zl, 1 - co

    def peer(j):
        return ((zh + j // 4) % 2) * 4 + (xx + j % 4) % 4

    def from_peer(j):
        return ((zh + j // 4) % 2) * 4 + (xx + 4 - j % 4) % 4

    def shard_peer(k):
        return ((yy + k // 4) % 4) * 4 + ((zl + (k // 2) % 2) % 2) * 2 + (co + k % 2) % 2

    sib = (ctx, fs + 1 - 2 * co)
    z_near = (ctx, fs + 2 - 4 * zl)
    z_far = (ctx + 4 - 8 * zh, fs + 2 - 4 * zl)
    z_of = (z_near, z_far)

    def y_peer(k):
        return (ctx, ((yy + k) % 4) * 4 + zl * 2 + co)

    def x_peer(k):
        return (zh * 4 + (xx + k) % 4, fs)

    h_peer = (ctx + 4 - 8 * zh, fs)
    odd = xx % 2
    x_of = ((ctx + 1 - 2 * odd, fs), (zh * 4 + 3 - xx, fs))

    count = [0]
    started = []

    def send(src, dst, to):
        i = count[0]
        count[0] += 1
        copy = pltpu.make_async_remote_copy(
            src_ref=src,
            dst_ref=dst,
            send_sem=send_sem.at[i],
            recv_sem=recv_sem.at[i],
            device_id=to,
            device_id_type=MESH,
        )
        copy.start()
        started.append(copy)
        return copy

    def arrived(copies):
        for copy in copies:
            copy.wait_recv()

    locals_ = []

    def keep(src, dst):
        i = len(locals_)
        copy = pltpu.make_async_copy(src, dst, local_sem.at[i])
        copy.start()
        locals_.append(copy)
        return copy

    got_tokens = keep(tokens_in, tokens)
    got_cotangent = keep(cotangent_in, cotangent)
    barrier = pltpu.get_barrier_semaphore()
    greeted = [(peer(j), fs) for j in range(1, PEERS)]
    greeted += [(ctx, shard_peer(k)) for k in range(1, 16)]
    greeted += [z_far]
    for device in greeted:
        pl.semaphore_signal(barrier, inc=1, device_id=device, device_id_type=MESH)

    def spread(values, at):
        size = values.shape[1]
        i = lax.broadcasted_iota(jnp.int32, (size, WIDTH), 0)
        lane = lax.broadcasted_iota(jnp.int32, (size, WIDTH), 1)
        return dot(values, jnp.where(lane == at + i, 1.0, 0.0).astype(BF16))

    plain = (own_gain1, own_shift1, own_qbias, own_obias, own_gain2, own_shift2, own_dbias)
    plain = [ref[...].reshape(1, 48) for ref in plain]
    up_row = spread(own_ubias[...].reshape(1, 192), (fs % 4) * 192)
    vecs[...] = jnp.concatenate(
        [spread(value, fs * 48) for value in plain]
        + [spread(own_vbias[...].reshape(1, 4), HD + fs * 4)]
        + [jnp.where(fs // 4 == r, up_row, 0.0) for r in range(4)]
        + [jnp.zeros((4, WIDTH), F32)],
        0,
    ).astype(BF16)

    slot0, slot1 = block_map[2 * ctx], block_map[2 * ctx + 1]
    low = jnp.minimum(slot0, slot1)
    swap = slot0 > slot1
    length = lengths[0]

    got_tokens.wait()
    t0, t1 = tokens[0], tokens[1]
    x_low[0:BLK] = jnp.where(swap, t1, t0)
    x_low[BLK:ROWS] = jnp.where(swap, t0, t1)

    row = lax.broadcasted_iota(jnp.int32, (ROWS, 1), 0)
    pos = jnp.where(row < BLK, low * BLK, (14 - low) * BLK) + row
    valid = (pos < length).astype(F32)

    def grad_out():
        c0, c1 = cotangent[0], cotangent[1]
        both = jnp.concatenate([jnp.where(swap, c1, c0), jnp.where(swap, c0, c1)], 0)
        return valid * both

    got_cotangent.wait()
    gos[0] = grad_out().astype(BF16)

    pl.semaphore_wait(barrier, len(greeted))

    def thirds_of(start, width):
        return (
            pl.ds(pl.multiple_of(start + odd * width, BLK), 2 * width),
            pl.ds(pl.multiple_of(start + odd * 2 * width, BLK), width),
            pl.ds(pl.multiple_of(start + (1 - odd) * 2 * width, BLK), width),
        )

    every = slice(None)

    class Whole:
        def __init__(self, src, full, cols=None, rows=every, dst=None, src_at=0):
            self.src, self.full, self.rows = src, full, rows
            self.dst = full if dst is None else dst
            self.fetch, self.own, self.other = (every,) * 3 if cols is None else thirds_of(*cols)
            self.src_cols = self.fetch
            if cols is not None:
                self.src_cols = pl.ds(
                    pl.multiple_of(src_at + cols[0] + odd * cols[1], BLK), 2 * cols[1]
                )

        def at(self, y, z, cols):
            return self.full.at[y, z, co, self.rows, cols]

        def y(self):
            src, dst = self.src.at[self.rows, self.src_cols], self.at(yy, zl, self.fetch)
            self.kept = keep(src, dst)
            return [send(src, dst, y_peer(k)) for k in (1, 2, 3)]

        def z(self):
            self.kept.wait()
            refs = [self.at(pl.ds(2 * e, 2), zl, self.fetch) for e in (0, 1)]
            return [send(ref, ref, z_of[e]) for e, ref in enumerate(refs)]

        def x(self):
            refs = [self.at(pl.ds(2 * e, 2), every, self.own) for e in (0, 1)]
            return [send(ref, ref, x_of[e]) for e, ref in enumerate(refs)]

        def c(self, cols, z=every):
            ref = self.at(every, z, cols)
            return [send(ref, self.dst.at[every, z, co, self.rows, cols], sib)]

    class Part(Whole):
        def at(self, y, z, cols):
            return self.full.at[y, z, self.rows, cols]

    class Mine(Whole):
        def c(self, cols, z=every):
            return []

    class Units(Whole):
        def at(self, y, z, cols):
            e = yy // 2 if y is yy else y
            other = e + co - 2 * e * co
            lead = (1 - other) * co + 2 * other
            return self.full.at[lead, yy % 2 if y is yy else every, z, self.rows, cols]

        def z(self):
            self.kept.wait()
            refs = [self.at(e, zl, self.fetch) for e in (0, 1)]
            return [send(ref, ref, z_of[e]) for e, ref in enumerate(refs)]

        def x(self):
            refs = [self.at(e, every, self.own) for e in (0, 1)]
            return [send(ref, ref, x_of[e]) for e, ref in enumerate(refs)]

        def c(self, cols, z=every):
            ref = self.full.at[2, every, z, self.rows, cols]
            return [send(ref, self.full.at[co, every, z, self.rows, cols], sib)]

    def each(arrays, action):
        return [copy for array in arrays for copy in action(array)]

    def narrow(*arrays):
        first = []

        def after_y():
            out = each(arrays, lambda a: a.z())
            first.extend(each(arrays, lambda a: a.c(every, zl)))
            return out

        return Chain(
            lambda: each(arrays, lambda a: a.y()),
            after_y,
            lambda: each(arrays, lambda a: a.c(every, oz)) + first,
        )

    def wide(*arrays):
        first = []

        def after_z():
            out = each(arrays, lambda a: a.x())
            first.extend(each(arrays, lambda a: a.c(a.fetch)))
            return out

        return Chain(
            lambda: each(arrays, lambda a: a.y()),
            lambda: each(arrays, lambda a: a.z()),
            after_z,
            lambda: each(arrays, lambda a: a.c(a.other)) + first,
        )

    def step(*chains):
        for chain in chains:
            chain.go(arrived)

    def up_chunk(j):
        cols = (j * WIDTH, WIDTH // 3)
        return wide(
            Mine(wup, f_up, cols, src_at=co * HALF),
            Part(wup, r_up, cols, dst=f_up, src_at=oc * HALF),
        )

    kvv = narrow(Whole(vecs, f_vec), Whole(wkv, f_kv))
    wq_in, wo_in = wide(Whole(wq, f_q, (0, 256))), wide(Whole(wo, f_o, (0, 256)))
    dn_a, dn_b = (wide(Units(wdn, f_dn, (0, 256), pl.ds(96 * i, 96))) for i in (0, 1))
    up_a, up_b = up_chunk(0), up_chunk(1)

    step(kvv, wq_in, wo_in)
    step(kvv, dn_a)
    step(wq_in, kvv, dn_b)
    step(wo_in, kvv)
    vec = f_vec[...].astype(F32).reshape(16, 16, WIDTH)
    vec = jnp.sum(vec, 0)
    gain1, shift1, qbias, obias = vec[0:1], vec[1:2], vec[2:3], vec[3:4]
    gain2, shift2, dbias, kvbias = vec[4:5], vec[5:6], vec[6:7], vec[7:8, 0 : 2 * HD]

    n1, _ = normalize(x_low[...].astype(F32))
    xn_v = n1 * gain1 + shift1
    xn[...] = xn_v.astype(BF16)
    xn_t[...] = xn_v.T.astype(BF16)

    kv = dot(xn[...], f_kv[...].reshape(WIDTH, 2 * HD)) + kvbias
    kv_all[0] = kv.astype(BF16)
    kv_copies = [send(kv_all.at[0], kv_all.at[j], (peer(j), fs)) for j in (1, 2, 3)]
    kv_far = send(kv_all.at[0], kv_all.at[4], h_peer)
    step(wq_in, dn_a, up_a, wo_in)
    arrived([kv_far])
    kv_copies += [send(kv_all.at[4], kv_all.at[4 + j], (peer(j), fs)) for j in (1, 2, 3)]
    step(wq_in, dn_b, up_b, wq_in)
    go_copy = send(gos.at[0], gos.at[1], sib)
    step(dn_a, wo_in)

    q = dot(xn[...], f_q[...].reshape(WIDTH, WIDTH)) + qbias
    q = (q.astype(BF16).astype(F32) * (HD**-0.5)).T
    for g in range(GROUPS):
        h0, h1 = q[g * BLK : g * BLK + HD], q[g * BLK + HD : (g + 1) * BLK]
        both = jnp.concatenate(
            [
                jnp.concatenate([h0[:, BLK:], h1[:, BLK:]], 1),
                jnp.concatenate([h0[:, :BLK], h1[:, :BLK]], 1),
            ],
            0,
        )
        q_both[g] = both.astype(BF16)
        q_rows[g] = both.T.astype(BF16)

    arrived(kv_copies)
    step(up_a)
    lane = lax.broadcasted_iota(jnp.int32, (BLK, BLK), 1)
    sub = lax.broadcasted_iota(jnp.int32, (BLK, BLK), 0)
    extra = lax.broadcasted_iota(jnp.int32, (16, BLK), 0)

    picks, limits = [], []
    for j in range(1, PEERS):
        c = from_peer(j)
        other = jnp.minimum(block_map[2 * c], block_map[2 * c + 1])
        high = other > low
        picks.append(jnp.where(high, 1.0, 0.0).astype(F32))
        limits.append(length - jnp.where(high, 15 - other, other) * BLK)

    def place(item, block, to_high):
        rows = pl.ds(item * BLK, BLK)
        left = jnp.where(lane < HD, to_high, 1.0 - to_high)
        kk = jnp.concatenate([block[:, :HD], block[:, :HD]], 1) * left
        vv = jnp.concatenate([block[:, HD:], block[:, HD:]], 1) * left
        k_both[rows] = kk.astype(BF16)
        v_both[rows] = vv.astype(BF16)
        kt_both[:, rows] = kk.T.astype(BF16)
        vt_both[0:BLK, rows] = vv.T.astype(BF16)
        vt_both[BLK : BLK + 16, rows] = jnp.where(extra < 8, to_high, 1.0 - to_high).astype(BF16)

    one, zero = jnp.float32(1.0), jnp.float32(0.0)
    for j in range(PEERS):
        block = kv_all[j].astype(F32)
        place(j, block[:BLK], one)
        if j:
            pick = picks[j - 1]
            place(N_A + j - 1, jnp.where(pick > 0.5, block[BLK:], block[:BLK]), pick)
        else:
            place(N_A + N_B, block[BLK:], one)
            place(N_A + N_B + 1, block[:BLK], zero)

    sub2 = lax.broadcasted_iota(jnp.int32, (BLK, ROWS), 0)
    lane2 = lax.broadcasted_iota(jnp.int32, (BLK, ROWS), 1) % BLK

    def fold(values, op):
        return op(values.reshape(BLK // 8, 8, ROWS), 0)

    def forward_group(g, carry):
        score[...] = dot(k_both[...], q_both[g])
        top_h = jnp.full((8, ROWS), NEG, F32)
        top_l = jnp.full((8, ROWS), NEG, F32)
        for item in range(ITEMS):
            rows = slice(item * BLK, (item + 1) * BLK)
            s = score[rows]
            if item < N_A:
                top_h = jnp.maximum(top_h, fold(s, jnp.max))
            elif item < N_A + N_B:
                j = item - N_A
                s = jnp.where(sub2 < limits[j], s, NEG)
                score[rows] = s
                best = fold(s, jnp.max)
                top_h = jnp.maximum(top_h, jnp.where(picks[j] > 0.5, best, NEG))
                top_l = jnp.maximum(top_l, jnp.where(picks[j] > 0.5, NEG, best))
            elif item == N_A + N_B:
                limit = length - (15 - low) * BLK
                s = jnp.where((sub2 <= lane2) & (sub2 < limit), s, NEG)
                score[rows] = s
                top_h = jnp.maximum(top_h, fold(s, jnp.max))
            else:
                s = jnp.where(sub2 <= lane2, s, NEG)
                score[rows] = s
                top_l = jnp.maximum(top_l, fold(s, jnp.max))
        top_h = jnp.max(top_h, 0, keepdims=True)
        top_l = jnp.max(top_l, 0, keepdims=True)
        for item in range(ITEMS):
            rows = slice(item * BLK, (item + 1) * BLK)
            if item < N_A or item == N_A + N_B:
                top = top_h
            elif item < N_A + N_B:
                top = jnp.where(picks[item - N_A] > 0.5, top_h, top_l)
            else:
                top = top_l
            probs[g, rows] = jnp.exp(score[rows] - top).astype(BF16)
        o = dot(vt_both[...], probs[g])
        inv_h = 1.0 / o[BLK : BLK + 1]
        inv_l = 1.0 / o[BLK + 8 : BLK + 9]
        high, lower = o[0:HD] * inv_h, o[HD:BLK] * inv_l
        o_norm[g, 0:HD] = high
        o_norm[g, HD:BLK] = lower
        l_inv[g, 0:8] = jnp.broadcast_to(inv_h, (8, ROWS))
        l_inv[g, 8:16] = jnp.broadcast_to(inv_l, (8, ROWS))
        att_t[g, 0:HD, 0:BLK] = lower[:, :BLK].astype(BF16)
        att_t[g, 0:HD, BLK:ROWS] = high[:, :BLK].astype(BF16)
        att_t[g, HD:BLK, 0:BLK] = lower[:, BLK:].astype(BF16)
        att_t[g, HD:BLK, BLK:ROWS] = high[:, BLK:].astype(BF16)
        return carry

    lax.fori_loop(0, 2, forward_group, 0)
    step(dn_a, dn_b)
    lax.fori_loop(2, 4, forward_group, 0)
    step(up_b, up_a)
    lax.fori_loop(4, 6, forward_group, 0)
    step(dn_b, up_a, up_b)

    step(wo_in)
    attended = att_t[...].reshape(WIDTH, ROWS).astype(F32).T.astype(BF16)
    mixed = x_low[...].astype(F32) + dot(attended, f_o[...].reshape(WIDTH, WIDTH)) + obias
    mixed_s[...] = mixed
    n2, _ = normalize(mixed)
    n2s[0] = (n2 * gain2 + shift2).astype(BF16)
    n2_copy = send(n2s.at[0], n2s.at[1], sib)

    step(up_b)
    arrived([go_copy])
    step(dn_a, dn_b, up_a)
    arrived([n2_copy])

    def unit_rows(j, start, size):
        blocks = []
        while size:
            k, r = start // 192, start % 192
            n = min(size, 192 - r)
            blocks.append(f_dn[k % 2, j, k // 2, r : r + n])
            start, size = start + n, size - n
        return jnp.concatenate(blocks, 0)

    sub_cols = 256
    n_sub = HALF // sub_cols
    coef = 0.7978845608028654

    up_sums = []
    for s in range(n_sub):
        cols = slice(s * sub_cols, (s + 1) * sub_cols)
        per = WIDTH // sub_cols
        if s == per:
            step(up_b)
        bias_row = jnp.where(co == 0, vec[8 + s // per : 9 + s // per], vec[10 + s // per : 11 + s // per])
        bias = bias_row[:, (s % per) * sub_cols : (s % per + 1) * sub_cols]
        n2b = n2s[...].reshape(2 * ROWS, WIDTH)
        gob = gos[...].reshape(2 * ROWS, WIDTH)
        up = dot(n2b, f_up[:, :, :, :, cols].reshape(WIDTH, sub_cols)) + bias
        w_rows = unit_rows(s // per, (s % per) * sub_cols, sub_cols)
        dmid = dot_nt(gob, w_rows)
        square = up * up
        th = jnp.tanh(coef * up * (1.0 + 0.044715 * square))
        half_sum = 0.5 + 0.5 * th
        mid[:, cols] = (up * half_sum).astype(BF16)
        slope = half_sum + 0.5 * up * (1.0 - th * th) * coef * (1.0 + 3 * 0.044715 * square)
        du = (dmid * slope).astype(BF16)
        dup[:, cols] = du
        up_sums.append(jnp.sum(du.astype(F32), 0, keepdims=True))

    thirds = [slice(256 * n, 256 * (n + 1)) for n in range(3)]
    for j in (0, 1):
        m_t = mid[:, j * WIDTH : (j + 1) * WIDTH].astype(F32).T.astype(BF16)
        for n in thirds:
            piece = dot(m_t, gos[:, :, n].reshape(2 * ROWS, 256))
            g_dn[j, :, :, :, n] = piece.astype(BF16).reshape(2, 2, 192, 256)

    def low_sum(own, *others):
        total = own.astype(F32)
        for other in others:
            total = total + other.astype(F32)
        return total.astype(BF16)

    class Down:
        def __init__(self, rows):
            self.rows = rows

        def z(self):
            rows = self.rows
            return [send(g_dn.at[j, oz, :, rows], rz_dn.at[j, :, rows], z_of[j]) for j in (0, 1)]

        def c(self):
            rows = self.rows
            for j in (0, 1):
                g_dn[j, zl, :, rows] = low_sum(g_dn[j, zl, :, rows], rz_dn[j, :, rows])
                s_dn[2 * co + j, rows] = g_dn[j, zl, co, rows]
            return [send(g_dn.at[:, zl, oc, rows], s_dn.at[pl.ds(2 * co, 2), rows], sib)]

        def y(self):
            rows = self.rows
            return [
                send(s_dn.at[(yy + k) % 4, rows], ry_dn.at[k - 1, rows], y_peer(k)) for k in (1, 2, 3)
            ]

        def y_sum(self):
            rows = self.rows
            s_dn[yy, rows] = low_sum(s_dn[yy, rows], *[ry_dn[k, rows] for k in range(3)])
            return []

        def x(self):
            self.y_sum()
            return [
                send(s_dn.at[yy, quarter_dn((xx + k) % 4)], rx_dn.at[k - 1], x_peer(k))
                for k in (1, 2, 3)
            ]

        def h(self):
            rh_dn[1] = low_sum(s_dn[yy, quarter_dn(xx)], *[rx_dn[k] for k in range(3)])
            return [send(rh_dn.at[1], rh_dn.at[0], h_peer)]

        def a(self):
            f2_dn[xx] = low_sum(rh_dn[0], rh_dn[1])
            return [send(f2_dn.at[xx], f2_dn.at[xx], x_peer(k)) for k in (1, 2, 3)]

    def quarter_dn(k):
        return pl.ds(pl.multiple_of(k * 48, 16), 48)

    class Up:
        def __init__(self, i):
            self.i, self.cols = i, slice(512 * i, 512 * (i + 1))

        def quarter(self, k):
            return pl.ds(pl.multiple_of(512 * self.i + k * BLK, BLK), BLK)

        def z(self):
            return [
                send(
                    g_up.at[pl.ds(2 * e, 2), oz, :, :, self.cols],
                    rz_up.at[pl.ds(2 * e, 2), :, :, self.cols],
                    z_of[e],
                )
                for e in (0, 1)
            ]

        def c(self):
            cols = self.cols
            g_up[:, zl, :, :, cols] = low_sum(g_up[:, zl, :, :, cols], rz_up[:, :, :, cols])
            s_up[:, co, :, cols] = g_up[:, zl, co, :, cols]
            return [send(g_up.at[:, zl, oc, :, cols], s_up.at[:, co, :, cols], sib)]

        def y(self):
            cols = self.cols
            return [
                send(s_up.at[(yy + k) % 4, :, :, cols], ry_up.at[k - 1, :, :, cols], y_peer(k))
                for k in (1, 2, 3)
            ]

        def x(self):
            cols = self.cols
            s_up[yy, :, :, cols] = low_sum(
                s_up[yy, :, :, cols], *[ry_up[k, :, :, cols] for k in range(3)]
            )
            return [
                send(s_up.at[yy, :, :, self.quarter((xx + k) % 4)], rx_up.at[self.i, k - 1], x_peer(k))
                for k in (1, 2, 3)
            ]

        def h(self):
            got = [rx_up[self.i, k] for k in range(3)]
            rh_up[self.i, 1] = low_sum(s_up[yy, :, :, self.quarter(xx)], *got)
            return [send(rh_up.at[self.i, 1], rh_up.at[self.i, 0], h_peer)]

        def a(self):
            f2_up[self.i, xx] = low_sum(rh_up[self.i, 0], rh_up[self.i, 1])
            ref = f2_up.at[self.i, xx]
            return [send(ref, ref, x_peer(k)) for k in (1, 2, 3)]

    down = [Down(slice(96 * i, 96 * (i + 1))) for i in (0, 1)]
    down_a = Chain(down[0].z, down[0].c, down[0].y, down[0].y_sum)
    down_b = Chain(down[1].z, down[1].c, down[1].y, down[1].x, down[1].h, down[1].a)
    ups = [Chain(u.z, u.c, u.y, u.x, u.h, u.a) for u in map(Up, range(3))]

    def square(grad, rc, rz, ry, cx, ch):
        def c():
            return [send(grad.at[:, :, oc], rc, sib)]

        def z():
            grad[:, :, co] = low_sum(grad[:, :, co], rc[...])
            return [
                send(grad.at[pl.ds(2 * e, 2), oz, co], rz.at[pl.ds(2 * e, 2)], z_of[e])
                for e in (0, 1)
            ]

        def y():
            grad[:, zl, co] = low_sum(grad[:, zl, co], rz[...])
            return [
                send(grad.at[(yy + k) % 4, zl, co], ry.at[k - 1], y_peer(k)) for k in (1, 2, 3)
            ]

        def x():
            cx[0] = low_sum(grad[yy, zl, co], *[ry[k] for k in range(3)])
            return [send(cx.at[0], cx.at[k], x_peer(k)) for k in (1, 2, 3)]

        def h():
            ch[0] = low_sum(cx[0], *[cx[k] for k in (1, 2, 3)])
            return [send(ch.at[0], ch.at[1], h_peer)]

        return Chain(c, z, y, x, h)

    out_w = square(g_o, rc_o, rz_o, ry_o, cx_o, ch_o)
    query_w = square(g_q, rc_q, rz_q, ry_q, cx_q, ch_q)

    step(down_a)
    for n in thirds:
        w = f_up[...].reshape(WIDTH, HALF)[n]
        piece = dot_nt(dup[...], w)
        dsec_own[:, n] = piece[:ROWS]
        dsec_out[:, n] = piece[ROWS:].astype(BF16)
    dsec_copy = send(dsec_out, dsec_in, sib)

    n2_t = n2s[...].reshape(2 * ROWS, WIDTH).astype(F32).T.astype(BF16)
    for s in range(n_sub):
        cols = slice(s * sub_cols, (s + 1) * sub_cols)
        piece = dot(n2_t, dup[:, cols])
        g_up[:, :, :, :, cols] = piece.astype(BF16).reshape(4, 2, 2, 48, sub_cols)
    step(down_b)

    arrived([dsec_copy])
    dsec = dsec_own[...] + dsec_in[...].astype(F32)
    n2, rate2 = normalize(mixed_s[...])
    sum_gain2 = jnp.sum(dsec * n2, 0, keepdims=True)
    sum_shift2 = jnp.sum(dsec, 0, keepdims=True)
    dmix = grad_out() + norm_back(n2, rate2, dsec, gain2)
    cotangent[0] = dmix[:BLK]
    cotangent[1] = dmix[BLK:]
    dmix_low = dmix.astype(BF16)
    dmix_r = dmix_low.astype(F32)
    sum_obias = jnp.sum(dmix_r, 0, keepdims=True)
    sum_dbias = jnp.sum(gos[0].astype(F32), 0, keepdims=True)

    g_o[...] = (
        dot(att_t[...].reshape(WIDTH, ROWS), dmix_low).astype(BF16).reshape(4, 2, 2, 48, WIDTH)
    )
    step(out_w)

    for n in thirds:
        blocks = [f_dn[c, j, z, :, n] for j in (0, 1) for z in (0, 1) for c in (0, 1)]
        piece = dot(mid[...], jnp.concatenate(blocks, 0))
        dsec_own[:, n] = piece[:ROWS]
        part_out[:, n] = piece[ROWS:].astype(BF16)
    part_copy = send(part_out, part_in, sib)

    datt = dot(f_o[...].reshape(WIDTH, WIDTH), dmix_r.T.astype(BF16)).astype(BF16).astype(F32)
    deltas = []
    for g in range(GROUPS):
        h0, h1 = datt[g * BLK : g * BLK + HD], datt[g * BLK + HD : (g + 1) * BLK]
        high = jnp.concatenate([h0[:, BLK:], h1[:, BLK:]], 1) * l_inv[g, 0:1]
        lower = jnp.concatenate([h0[:, :BLK], h1[:, :BLK]], 1) * l_inv[g, 8:9]
        both = jnp.concatenate([high, lower], 0)
        do_both[g] = both.astype(BF16)
        do_rows[g] = both.T.astype(BF16)
        both = both.astype(BF16).astype(F32) * o_norm[g]
        l_inv[g, 0:8] = jnp.broadcast_to(jnp.sum(both[:HD], 0, keepdims=True), (8, ROWS))
        l_inv[g, 8:16] = jnp.broadcast_to(jnp.sum(both[HD:], 0, keepdims=True), (8, ROWS))

    acc[...] = jnp.zeros_like(acc)

    def backward_group(g, carry):
        acc[:, BLK:ROWS] += dot(probs[g], do_rows[g])
        delta_h, delta_l = l_inv[g, 0:1], l_inv[g, 8:9]
        score[...] = dot(v_both[...], do_both[g])
        for item in range(ITEMS):
            rows = slice(item * BLK, (item + 1) * BLK)
            if item < N_A or item == N_A + N_B:
                delta = delta_h
            elif item < N_A + N_B:
                delta = jnp.where(picks[item - N_A] > 0.5, delta_h, delta_l)
            else:
                delta = delta_l
            probs[g, rows] = (probs[g, rows].astype(F32) * (score[rows] - delta)).astype(BF16)
        dq = dot(kt_both[...], probs[g]) * (HD**-0.5)
        do_both[g, 0:HD, 0:BLK] = dq[HD:, :BLK].astype(BF16)
        do_both[g, 0:HD, BLK:ROWS] = dq[:HD, :BLK].astype(BF16)
        do_both[g, HD:BLK, 0:BLK] = dq[HD:, BLK:].astype(BF16)
        do_both[g, HD:BLK, BLK:ROWS] = dq[:HD, BLK:].astype(BF16)
        acc[:, 0:BLK] += dot(probs[g], q_rows[g])
        return carry

    lax.fori_loop(0, 2, backward_group, 0)
    step(out_w)
    lax.fori_loop(2, 4, backward_group, 0)
    step(down_a, ups[0])
    lax.fori_loop(4, 6, backward_group, 0)
    step(down_a)

    def halves(item, second):
        rows = slice(item * BLK, (item + 1) * BLK)
        at = HD if second else 0
        return jnp.concatenate(
            [acc[rows, at : at + HD], acc[rows, BLK + at : BLK + at + HD]], 1
        )

    dkv_copies = []
    for j in range(1, PEERS):
        item = N_A + j - 1
        pick = picks[j - 1]
        other = jnp.where(pick > 0.5, halves(item, False), halves(item, True))
        dkv_out[j, 0:BLK] = (halves(j, False) + (1.0 - pick) * other).astype(BF16)
        dkv_out[j, BLK:ROWS] = (pick * other).astype(BF16)
        dkv_copies.append(send(dkv_out.at[j], dkv_in.at[j], (from_peer(j), fs)))

    dq = do_both[...].reshape(WIDTH, ROWS).astype(F32).T
    sum_qbias = jnp.sum(dq, 0, keepdims=True)
    dq = dq.astype(BF16)
    g_q[...] = dot(xn_t[...], dq).astype(BF16).reshape(4, 2, 2, 48, WIDTH)
    step(query_w, down_b, ups[1])
    dfirst = dot_nt(dq, f_q[...].reshape(WIDTH, WIDTH))

    step(query_w, down_b, out_w, down_a, ups[0], ups[2])

    top = halves(0, False) + halves(N_A + N_B + 1, True)
    dkv = jnp.concatenate([top, halves(N_A + N_B, False)], 0)
    arrived(dkv_copies)
    for j in range(1, PEERS):
        dkv = dkv + dkv_in[j].astype(F32)
    dkv = dkv.astype(BF16)
    sum_kv = jnp.sum(dkv.astype(F32), 0, keepdims=True)
    g_kv = dot(xn_t[...], dkv)
    dfirst = dfirst + dot_nt(dkv, f_kv[...].reshape(WIDTH, 2 * HD))

    n1, rate1 = normalize(x_low[...].astype(F32))
    sum_gain1 = jnp.sum(dfirst * n1, 0, keepdims=True)
    sum_shift1 = jnp.sum(dfirst, 0, keepdims=True)

    zeros = jnp.zeros((1, WIDTH), F32)
    columns = jnp.concatenate(
        [zeros] * 4
        + [sum_dbias, sum_gain2, sum_shift2, sum_obias, sum_gain1, sum_shift1, sum_qbias]
        + [jnp.zeros((BLK - 11, WIDTH), F32)],
        0,
    ).T
    lanes = lax.broadcasted_iota(jnp.int32, (WIDTH, BLK), 1)
    columns = jnp.where(lanes < HD, columns, sum_kv)
    g_t[:, :, :, :, 0:BLK] = g_kv.astype(BF16).reshape(4, 2, 2, 48, BLK)
    g_t[:, :, :, :, BLK:ROWS] = columns.astype(BF16).reshape(4, 2, 2, 48, BLK)
    lanes = lax.broadcasted_iota(jnp.int32, (48, BLK), 1)
    for j in (0, 1):
        sums = jnp.concatenate(up_sums[3 * j : 3 * j + 3], 1)
        sums = jnp.broadcast_to(sums, (BLK, WIDTH)).T
        for k in range(4):
            block = g_t[2 * co + j, k // 2, k % 2, :, BLK:ROWS].astype(F32)
            for r in range(4):
                at = k * 192 + r * 48
                block = jnp.where(lanes == r, sums[at : at + 48], block)
            g_t[2 * co + j, k // 2, k % 2, :, BLK:ROWS] = block.astype(BF16)

    t_copies = []
    for k in range(1, 16):
        dst = shard_peer(k)
        t_copies.append(
            send(g_t.at[dst // 4, (dst // 2) % 2, dst % 2], r_t.at[k], (ctx, dst))
        )

    step(ups[0], down_b, query_w, out_w)

    ing = cotangent[...].reshape(ROWS, WIDTH) + norm_back(n1, rate1, dfirst, gain1)
    cotangent[0] = jnp.where(swap, ing[BLK:], ing[:BLK])
    cotangent[1] = jnp.where(swap, ing[:BLK], ing[BLK:])
    done = [keep(cotangent, ing_hbm)]
    arrived([part_copy])
    res = valid * (mixed_s[...] + dsec_own[...] + part_in[...].astype(F32) + dbias)
    tokens[0] = jnp.where(swap, res[BLK:], res[:BLK]).astype(BF16)
    tokens[1] = jnp.where(swap, res[:BLK], res[BLK:]).astype(BF16)
    done.append(keep(tokens, out_hbm))

    step(ups[1], ups[0], ups[1], down_b, out_w)

    arrived(t_copies)
    total = g_t[yy, zl, co].astype(F32)
    for k in range(1, 16):
        total = total + r_t[k].astype(F32)
    c_t[0] = total.astype(BF16)
    ctx_t = [send(c_t.at[0], c_t.at[j], (peer(j), fs)) for j in range(1, PEERS)]

    step(ups[2], ups[2], query_w, ups[0], ups[1], down_b, query_w, ups[0], ups[2])
    step(out_w, ups[1], ups[2], query_w, ups[1], ups[2], ups[2])

    go_ref[...] = ch_o[0].astype(F32) + ch_o[1].astype(F32)
    done.append(keep(go_ref, go_hbm))
    step(down_b)
    gdn_ref[...] = f2_dn[...].astype(F32).reshape(192, WIDTH)
    done.append(keep(gdn_ref, gdn_hbm))
    step(*ups)
    for i in range(3):
        for k in range(4):
            for half in (0, 1):
                at = half * HALF + 512 * i + k * BLK
                gup_ref[:, at : at + BLK] = f2_up[i, k, half].astype(F32)
    done.append(keep(gup_ref, gup_hbm))
    arrived(ctx_t)
    total = c_t[0].astype(F32)
    for j in range(1, PEERS):
        total = total + c_t[j].astype(F32)
    gt_ref[...] = total
    done.append(keep(gt_ref, gt_hbm))
    step(query_w)
    gq_ref[...] = ch_q[0].astype(F32) + ch_q[1].astype(F32)
    done.append(keep(gq_ref, gq_hbm))
    for chain in (kvv, wq_in, wo_in, dn_a, dn_b, up_a, up_b, down_a, down_b, out_w, query_w, *ups):
        assert not chain.steps and not chain.flying
    for copy in done:
        copy.wait()

    for copy in started:
        copy.wait_send()


def finish_kernel(
    out_in,
    ing_in,
    gq_in,
    go_in,
    gt_in,
    gup_in,
    gdn_in,
    out,
    ing,
    gain1,
    shift1,
    gq,
    qbias,
    gkv,
    vbias,
    go,
    obias,
    gain2,
    shift2,
    gup,
    ubias,
    gdn,
    dbias,
    stage0,
    stage1,
    stage2,
    stage3,
    stage4,
    stage5,
    sems,
):
    stages = (stage0, stage1, stage2, stage3, stage4, stage5)
    pairs = ((ing_in, ing), (gup_in, gup), (gdn_in, gdn), (out_in, out), (gq_in, gq), (go_in, go))
    loads, stores = [], []
    for i, ((src, dst), stage) in enumerate(zip(pairs, stages)):
        loads.append(pltpu.make_async_copy(src, stage, sems.at[i]))
        stores.append(pltpu.make_async_copy(stage, dst, sems.at[6 + i]))
        loads[i].start()
    fs = lax.axis_index("fsdp")
    gkv[...] = gt_in[:, 0:BLK]
    columns = gt_in[:, BLK : 2 * BLK]
    rows = jnp.concatenate([columns, jnp.zeros((BLK - 48, BLK), F32)], 0).T
    for k, ref in ((4, dbias), (5, gain2), (6, shift2), (7, obias), (8, gain1), (9, shift1), (10, qbias)):
        ref[...] = rows[k, 0:48]
    ubias[...] = jnp.concatenate([rows[r : r + 1, 0:48] for r in range(4)], 1)[0]
    lane = lax.broadcasted_iota(jnp.int32, (8, BLK), 1)
    pick = jnp.zeros((8, BLK), F32)
    for i in range(4):
        value = jnp.sum(jnp.where(lane == HD + fs * 4 + i, columns[0:8], 0.0), 1, keepdims=True)
        pick = jnp.where(lane == i, value, pick)
    vbias[...] = pick[0, 0:4]
    for load, store in zip(loads, stores):
        load.wait()
        store.start()
    for store in stores:
        store.wait()


def shards(
    tokens,
    lengths,
    block_map,
    first_gain,
    first_shift,
    query_weight,
    query_bias,
    keyval_weight,
    value_bias,
    output_weight,
    output_bias,
    second_gain,
    second_shift,
    up_weight,
    up_bias,
    down_weight,
    down_bias,
    cotangent,
):
    vmem = pl.BlockSpec(memory_space=pltpu.VMEM)
    smem = pl.BlockSpec(memory_space=pltpu.SMEM)
    hbm = pl.BlockSpec(memory_space=pl.ANY)

    def v(*shape, dtype=BF16):
        return pltpu.VMEM(shape, dtype)

    shapes = (
        jax.ShapeDtypeStruct((2, BLK, WIDTH), BF16),
        jax.ShapeDtypeStruct((2, BLK, WIDTH), F32),
        jax.ShapeDtypeStruct((48, WIDTH), F32),
        jax.ShapeDtypeStruct((48, WIDTH), F32),
        jax.ShapeDtypeStruct((48, 2 * BLK), F32),
        jax.ShapeDtypeStruct((48, FF), F32),
        jax.ShapeDtypeStruct((192, WIDTH), F32),
    )
    scratch = [
        v(2, BLK, WIDTH),
        v(2, BLK, WIDTH, dtype=F32),
        v(16, WIDTH),
    ]
    scratch += [v(*shape.shape, dtype=shape.dtype) for shape in shapes[2:]]
    scratch += [
        v(4, 2, 2, 16, WIDTH),
        v(4, 2, 2, 48, WIDTH),
        v(4, 2, 2, 48, 2 * HD),
        v(4, 2, 2, 48, WIDTH),
        v(4, 2, 2, 48, HALF),
        v(4, 2, 48, HALF),
        v(3, 2, 2, 192, WIDTH),
        v(4, 2, 2, 48, WIDTH),
        v(4, 2, 2, 48, WIDTH),
        v(4, 2, 2, 48, 2 * BLK),
        v(4, 2, 2, 48, HALF),
        v(2, 2, 2, 192, WIDTH),
        v(4, 2, 48, WIDTH),
        v(4, 2, 48, WIDTH),
        v(4, 48, WIDTH),
        v(4, 48, WIDTH),
        v(4, 2, 48, HALF),
        v(2, 2, 192, WIDTH),
        v(4, 2, 48, HALF),
        v(4, 192, WIDTH),
        v(3, 48, WIDTH),
        v(3, 48, WIDTH),
        v(3, 2, 48, HALF),
        v(3, 192, WIDTH),
        v(3, 3, 2, 48, BLK),
        v(3, 48, WIDTH),
        v(3, 2, 2, 48, BLK),
        v(2, 48, WIDTH),
        v(3, 4, 2, 48, BLK),
        v(4, 48, WIDTH),
        v(16, 48, 2 * BLK),
        v(4, 48, WIDTH),
        v(4, 48, WIDTH),
        v(2, 48, WIDTH),
        v(2, 48, WIDTH),
        v(PEERS, 48, 2 * BLK),
        v(PEERS, ROWS, 2 * HD),
        v(PEERS, ROWS, 2 * HD),
        v(PEERS, ROWS, 2 * HD),
        v(KEYS, BLK),
        v(KEYS, BLK),
        v(BLK, KEYS),
        v(BLK + 16, KEYS),
        v(GROUPS, BLK, ROWS),
        v(GROUPS, ROWS, BLK),
        v(GROUPS, KEYS, ROWS),
        v(KEYS, ROWS, dtype=F32),
        v(KEYS, ROWS, dtype=F32),
        v(GROUPS, BLK, ROWS, dtype=F32),
        v(GROUPS, 16, ROWS, dtype=F32),
        v(GROUPS, BLK, ROWS),
        v(GROUPS, BLK, ROWS),
        v(GROUPS, ROWS, BLK),
        v(ROWS, WIDTH),
        v(ROWS, WIDTH),
        v(WIDTH, ROWS),
        v(ROWS, WIDTH, dtype=F32),
        v(2, ROWS, WIDTH),
        v(2, ROWS, WIDTH),
        v(2 * ROWS, HALF),
        v(2 * ROWS, HALF),
        v(ROWS, WIDTH),
        v(ROWS, WIDTH),
        v(ROWS, WIDTH, dtype=F32),
        v(ROWS, WIDTH),
        v(ROWS, WIDTH),
        pltpu.SemaphoreType.DMA((SEMS,)),
        pltpu.SemaphoreType.DMA((SEMS,)),
        pltpu.SemaphoreType.DMA((32,)),
    ]
    outs = pl.pallas_call(
        layer_kernel,
        out_shape=shapes,
        in_specs=[smem, smem, hbm, hbm] + [vmem] * 9 + [hbm] * 5,
        out_specs=(hbm,) * 7,
        scratch_shapes=scratch,
        compiler_params=pltpu.CompilerParams(
            collective_id=0, has_side_effects=True, vmem_limit_bytes=62 * 2**20
        ),
    )(
        lengths,
        block_map,
        tokens[0],
        cotangent[0],
        first_gain,
        first_shift,
        query_bias,
        value_bias,
        output_bias,
        second_gain,
        second_shift,
        up_bias,
        down_bias,
        query_weight,
        keyval_weight,
        output_weight,
        up_weight,
        down_weight,
    )

    def f(*shape):
        return jax.ShapeDtypeStruct(shape, F32)

    results = pl.pallas_call(
        finish_kernel,
        out_shape=(
            shapes[0],
            shapes[1],
            f(48),
            f(48),
            f(48, WIDTH),
            f(48),
            f(48, 2 * HD),
            f(4),
            f(48, WIDTH),
            f(48),
            f(48),
            f(48),
            f(48, FF),
            f(192),
            f(192, WIDTH),
            f(48),
        ),
        in_specs=[hbm] * 4 + [vmem] + [hbm] * 2,
        out_specs=tuple(
            hbm if i in (0, 1, 4, 8, 12, 14) else vmem for i in range(16)
        ),
        scratch_shapes=[
            pltpu.VMEM(shapes[i].shape, shapes[i].dtype) for i in (1, 5, 6, 0, 2, 3)
        ]
        + [pltpu.SemaphoreType.DMA((12,))],
    )(*outs)
    return (results[0][None], results[1][None]) + tuple(results[2:])


def solution(mesh):
    rows, matrix, batch = P("fsdp"), P("fsdp", None), P("fsdp", "ctx", None, None)
    return jax.shard_map(
        shards,
        mesh=mesh,
        in_specs=(
            batch,
            rows,
            P(),
            rows,
            rows,
            matrix,
            rows,
            matrix,
            rows,
            matrix,
            rows,
            rows,
            rows,
            matrix,
            rows,
            matrix,
            rows,
            batch,
        ),
        out_specs=(
            batch,
            batch,
            rows,
            rows,
            matrix,
            rows,
            matrix,
            rows,
            matrix,
            rows,
            rows,
            rows,
            matrix,
            rows,
            matrix,
            rows,
        ),
        check_vma=False,
    )
```

```python
import functools

import jax
import jax.numpy as jnp
from jax import lax
from jax.experimental import pallas as pl
from jax.experimental.pallas import tpu as pltpu
from jax.sharding import PartitionSpec as P

EPS = 1e-05
NEG = -1e30
MESH = pl.DeviceIdType.MESH
F32 = jnp.float32
BF16 = jnp.bfloat16

WIDTH = 768
HEADS = 12
HD = 64
FF = 3072
HALF = FF // 2
BLK = 128
ROWS = 2 * BLK
GROUPS = HEADS // 2
PEERS = 8
N_A, N_B = 8, 7
ITEMS = N_A + N_B + 2
KEYS = ITEMS * BLK
SEMS = 300


class Chain:
    def __init__(self, *steps):
        self.steps = list(steps)
        self.flying = []

    def go(self, arrived):
        arrived(self.flying)
        self.flying = self.steps.pop(0)() if self.steps else []


def dot(left, right):
    return jnp.dot(left, right, preferred_element_type=F32)


def dot_nt(left, right):
    return lax.dot_general(left, right, (((1,), (1,)), ((), ())), preferred_element_type=F32)


def normalize(values):
    centre = values - jnp.mean(values, -1, keepdims=True)
    spread = jnp.mean(centre * centre, -1, keepdims=True)
    rate = lax.rsqrt(spread + EPS)
    return centre * rate, rate


def norm_back(normed, rate, grad, gain):
    scaled = grad * gain
    first = jnp.mean(scaled, -1, keepdims=True)
    second = jnp.mean(scaled * normed, -1, keepdims=True)
    return rate * (scaled - first - normed * second)


def layer_kernel(
    lengths,
    block_map,
    tokens_in,
    cotangent_in,
    own_gain1,
    own_shift1,
    own_qbias,
    own_vbias,
    own_obias,
    own_gain2,
    own_shift2,
    own_ubias,
    own_dbias,
    wq,
    wkv,
    wo,
    wup,
    wdn,
    out_hbm,
    ing_hbm,
    gq_hbm,
    go_hbm,
    gt_hbm,
    gup_hbm,
    gdn_hbm,
    tokens,
    cotangent,
    vecs,
    gq_ref,
    go_ref,
    gt_ref,
    gup_ref,
    gdn_ref,
    f_vec,
    f_q,
    f_kv,
    f_o,
    f_up,
    r_up,
    f_dn,
    g_q,
    g_o,
    g_t,
    g_up,
    g_dn,
    rc_q,
    rc_o,
    rz_q,
    rz_o,
    rz_up,
    rz_dn,
    s_up,
    s_dn,
    ry_q,
    ry_o,
    ry_up,
    ry_dn,
    rx_up,
    rx_dn,
    rh_up,
    rh_dn,
    f2_up,
    f2_dn,
    fx,
    fg,
    fz,
    fs_up,
    fy,
    fh,
    fa,
    g_r,
    rc_r,
    rz_r,
    ry_r,
    cx_r,
    ch_r,
    rc_t,
    r_t,
    cx_q,
    cx_o,
    ch_q,
    ch_o,
    c_t,
    kv_all,
    dkv_out,
    dkv_in,
    k_both,
    v_both,
    kt_both,
    vt_both,
    q_both,
    q_rows,
    probs,
    score,
    acc,
    o_norm,
    l_inv,
    att_t,
    do_both,
    do_rows,
    x_low,
    xn,
    xn_t,
    mixed_s,
    n2s,
    n2_t,
    gos,
    mid,
    dup,
    part_out,
    part_in,
    dsec_own,
    dsec_out,
    dsec_in,
    send_sem,
    recv_sem,
    local_sem,
):
    ctx = lax.axis_index("ctx")
    fs = lax.axis_index("fsdp")
    zh, xx = ctx // 4, ctx % 4
    yy, zl, co = fs // 4, (fs // 2) % 2, fs % 2
    oz, oc = 1 - zl, 1 - co

    def peer(j):
        return ((zh + j // 4) % 2) * 4 + (xx + j % 4) % 4

    def from_peer(j):
        return ((zh + j // 4) % 2) * 4 + (xx + 4 - j % 4) % 4

    def shard_peer(k):
        return ((yy + k // 4) % 4) * 4 + ((zl + (k // 2) % 2) % 2) * 2 + (co + k % 2) % 2

    sib = (ctx, fs + 1 - 2 * co)
    z_near = (ctx, fs + 2 - 4 * zl)
    z_far = (ctx + 4 - 8 * zh, fs + 2 - 4 * zl)
    z_of = (z_near, z_far)

    def y_peer(k):
        return (ctx, ((yy + k) % 4) * 4 + zl * 2 + co)

    def x_peer(k):
        return (zh * 4 + (xx + k) % 4, fs)

    h_peer = (ctx + 4 - 8 * zh, fs)
    odd = xx % 2
    x_of = ((ctx + 1 - 2 * odd, fs), (zh * 4 + 3 - xx, fs))

    count = [0]
    started = []

    def send(src, dst, to):
        i = count[0]
        count[0] += 1
        copy = pltpu.make_async_remote_copy(
            src_ref=src,
            dst_ref=dst,
            send_sem=send_sem.at[i],
            recv_sem=recv_sem.at[i],
            device_id=to,
            device_id_type=MESH,
        )
        copy.start()
        started.append(copy)
        return copy

    def arrived(copies):
        for copy in copies:
            copy.wait_recv()

    locals_ = []

    def keep(src, dst):
        i = len(locals_)
        copy = pltpu.make_async_copy(src, dst, local_sem.at[i])
        copy.start()
        locals_.append(copy)
        return copy

    got_tokens = keep(tokens_in, tokens)
    got_cotangent = keep(cotangent_in, cotangent)
    barrier = pltpu.get_barrier_semaphore()
    greeted = [(peer(j), fs) for j in (1, 2, 3, 4)]
    greeted += [(ctx, shard_peer(k)) for k in (1, 2, 4, 8, 12)] + [z_far]
    for device in greeted:
        pl.semaphore_signal(barrier, inc=1, device_id=device, device_id_type=MESH)

    def spread(values, at):
        size = values.shape[1]
        i = lax.broadcasted_iota(jnp.int32, (size, WIDTH), 0)
        lane = lax.broadcasted_iota(jnp.int32, (size, WIDTH), 1)
        return dot(values, jnp.where(lane == at + i, 1.0, 0.0).astype(BF16))

    plain = (own_gain1, own_shift1, own_qbias, own_obias, own_gain2, own_shift2, own_dbias)
    plain = [ref[...].reshape(1, 48) for ref in plain]
    up_row = spread(own_ubias[...].reshape(1, 192), (fs % 4) * 192)
    vecs[...] = jnp.concatenate(
        [spread(value, fs * 48) for value in plain]
        + [spread(own_vbias[...].reshape(1, 4), HD + fs * 4)]
        + [jnp.where(fs // 4 == r, up_row, 0.0) for r in range(4)]
        + [jnp.zeros((4, WIDTH), F32)],
        0,
    ).astype(BF16)

    slot0, slot1 = block_map[2 * ctx], block_map[2 * ctx + 1]
    low = jnp.minimum(slot0, slot1)
    swap = slot0 > slot1
    length = lengths[0]

    got_tokens.wait()
    t0, t1 = tokens[0], tokens[1]
    x_low[0:BLK] = jnp.where(swap, t1, t0)
    x_low[BLK:ROWS] = jnp.where(swap, t0, t1)

    row = lax.broadcasted_iota(jnp.int32, (ROWS, 1), 0)
    pos = jnp.where(row < BLK, low * BLK, (14 - low) * BLK) + row
    valid = (pos < length).astype(F32)

    def grad_out():
        c0, c1 = cotangent[0], cotangent[1]
        both = jnp.concatenate([jnp.where(swap, c1, c0), jnp.where(swap, c0, c1)], 0)
        return valid * both

    got_cotangent.wait()
    gos[0] = grad_out().astype(BF16)

    pl.semaphore_wait(barrier, len(greeted))

    def thirds_of(start, width):
        return (
            pl.ds(pl.multiple_of(start + odd * width, BLK), 2 * width),
            pl.ds(pl.multiple_of(start + odd * 2 * width, BLK), width),
            pl.ds(pl.multiple_of(start + (1 - odd) * 2 * width, BLK), width),
        )

    every = slice(None)

    class Whole:
        def __init__(self, src, full, cols=None, rows=every, dst=None, src_at=0):
            self.src, self.full, self.rows = src, full, rows
            self.dst = full if dst is None else dst
            self.fetch, self.own, self.other = (every,) * 3 if cols is None else thirds_of(*cols)
            self.src_cols = self.fetch
            if cols is not None:
                self.src_cols = pl.ds(
                    pl.multiple_of(src_at + cols[0] + odd * cols[1], BLK), 2 * cols[1]
                )

        def at(self, y, z, cols):
            return self.full.at[y, z, co, self.rows, cols]

        def y(self):
            src, dst = self.src.at[self.rows, self.src_cols], self.at(yy, zl, self.fetch)
            self.kept = keep(src, dst)
            return [send(src, dst, y_peer(k)) for k in (1, 2, 3)]

        def z(self):
            self.kept.wait()
            refs = [self.at(pl.ds(2 * e, 2), zl, self.fetch) for e in (0, 1)]
            return [send(ref, ref, z_of[e]) for e, ref in enumerate(refs)]

        def x(self):
            refs = [self.at(pl.ds(2 * e, 2), every, self.own) for e in (0, 1)]
            return [send(ref, ref, x_of[e]) for e, ref in enumerate(refs)]

        def c(self, cols, z=every):
            ref = self.at(every, z, cols)
            return [send(ref, self.dst.at[every, z, co, self.rows, cols], sib)]

    class Part(Whole):
        def at(self, y, z, cols):
            return self.full.at[y, z, self.rows, cols]

    class Mine(Whole):
        def c(self, cols, z=every):
            return []

    class Units(Whole):
        def at(self, e, z, cols, y=every):
            other = e + co - 2 * e * co
            lead = (1 - other) * co + 2 * other
            return self.full.at[lead, y, z, self.rows, cols]

        def y(self):
            src, dst = self.src.at[self.rows, self.src_cols], self.at(yy // 2, zl, self.fetch, yy % 2)
            self.kept = keep(src, dst)
            return [send(src, dst, y_peer(k)) for k in (1, 2, 3)]

        def z(self):
            self.kept.wait()
            refs = [self.at(e, zl, self.fetch) for e in (0, 1)]
            return [send(ref, ref, z_of[e]) for e, ref in enumerate(refs)]

        def x(self):
            refs = [self.at(e, every, self.own) for e in (0, 1)]
            return [send(ref, ref, x_of[e]) for e, ref in enumerate(refs)]

        def c(self, cols, z=every):
            ref = self.full.at[2, every, z, self.rows, cols]
            return [send(ref, self.full.at[co, every, z, self.rows, cols], sib)]

    def each(arrays, action):
        return [copy for array in arrays for copy in action(array)]

    def narrow(*arrays):
        first = []

        def after_y():
            out = each(arrays, lambda a: a.z())
            first.extend(each(arrays, lambda a: a.c(every, zl)))
            return out

        return Chain(
            lambda: each(arrays, lambda a: a.y()),
            after_y,
            lambda: each(arrays, lambda a: a.c(every, oz)) + first,
        )

    def wide(*arrays):
        first = []

        def after_z():
            out = each(arrays, lambda a: a.x())
            first.extend(each(arrays, lambda a: a.c(a.fetch)))
            return out

        return Chain(
            lambda: each(arrays, lambda a: a.y()),
            lambda: each(arrays, lambda a: a.z()),
            after_z,
            lambda: each(arrays, lambda a: a.c(a.other)) + first,
        )

    def step(*chains):
        for chain in chains:
            chain.go(arrived)

    def up_chunk(j):
        cols = (j * WIDTH, WIDTH // 3)
        return wide(
            Mine(wup, f_up, cols, src_at=co * HALF),
            Part(wup, r_up, cols, dst=f_up, src_at=oc * HALF),
        )

    kvv = narrow(Whole(vecs, f_vec), Whole(wkv, f_kv))
    wq_in, wo_in = narrow(Whole(wq, f_q)), wide(Whole(wo, f_o, (0, 256)))
    dn_a, dn_b = (wide(Units(wdn, f_dn, (0, 256), pl.ds(96 * i, 96))) for i in (0, 1))
    up_a, up_b = up_chunk(0), up_chunk(1)

    step(kvv, wq_in, wo_in, dn_a, dn_b, up_a, up_b)
    step(kvv)
    step(wq_in, kvv)
    step(kvv)
    vec = f_vec[...].astype(F32).reshape(16, 16, WIDTH)
    vec = jnp.sum(vec, 0)
    gain1, shift1, qbias, obias = vec[0:1], vec[1:2], vec[2:3], vec[3:4]
    gain2, shift2, dbias, kvbias = vec[4:5], vec[5:6], vec[6:7], vec[7:8, 0 : 2 * HD]

    n1, _ = normalize(x_low[...].astype(F32))
    xn_v = n1 * gain1 + shift1
    xn[...] = xn_v.astype(BF16)
    xn_t[...] = xn_v.T.astype(BF16)

    kv = dot(xn[...], f_kv[...].reshape(WIDTH, 2 * HD)) + kvbias
    kv_all[0] = kv.astype(BF16)
    kv_copies = [send(kv_all.at[0], kv_all.at[j], (peer(j), fs)) for j in (1, 2, 3)]
    kv_far = send(kv_all.at[0], kv_all.at[4], h_peer)
    step(wo_in, wq_in)
    arrived([kv_far])
    kv_copies += [send(kv_all.at[4], kv_all.at[4 + j], (peer(j), fs)) for j in (1, 2, 3)]
    step(dn_a, wo_in, wq_in)
    go_copy = send(gos.at[0], gos.at[1], sib)

    q = dot(xn[...], f_q[...].reshape(WIDTH, WIDTH)) + qbias
    q = (q.astype(BF16).astype(F32) * (HD**-0.5)).T
    for g in range(GROUPS):
        h0, h1 = q[g * BLK : g * BLK + HD], q[g * BLK + HD : (g + 1) * BLK]
        both = jnp.concatenate(
            [
                jnp.concatenate([h0[:, BLK:], h1[:, BLK:]], 1),
                jnp.concatenate([h0[:, :BLK], h1[:, :BLK]], 1),
            ],
            0,
        )
        q_both[g] = both.astype(BF16)
        q_rows[g] = both.T.astype(BF16)

    arrived(kv_copies)
    step(dn_b)
    lane = lax.broadcasted_iota(jnp.int32, (BLK, BLK), 1)
    sub = lax.broadcasted_iota(jnp.int32, (BLK, BLK), 0)
    extra = lax.broadcasted_iota(jnp.int32, (16, BLK), 0)

    picks, limits = [], []
    for j in range(1, PEERS):
        c = from_peer(j)
        other = jnp.minimum(block_map[2 * c], block_map[2 * c + 1])
        high = other > low
        picks.append(jnp.where(high, 1.0, 0.0).astype(F32))
        limits.append(length - jnp.where(high, 15 - other, other) * BLK)

    def place(item, block, to_high):
        rows = pl.ds(item * BLK, BLK)
        left = jnp.where(lane < HD, to_high, 1.0 - to_high)
        kk = jnp.concatenate([block[:, :HD], block[:, :HD]], 1) * left
        vv = jnp.concatenate([block[:, HD:], block[:, HD:]], 1) * left
        k_both[rows] = kk.astype(BF16)
        v_both[rows] = vv.astype(BF16)
        kt_both[:, rows] = kk.T.astype(BF16)
        vt_both[0:BLK, rows] = vv.T.astype(BF16)
        vt_both[BLK : BLK + 16, rows] = jnp.where(extra < 8, to_high, 1.0 - to_high).astype(BF16)

    one, zero = jnp.float32(1.0), jnp.float32(0.0)
    for j in range(PEERS):
        block = kv_all[j].astype(F32)
        place(j, block[:BLK], one)
        if j:
            pick = picks[j - 1]
            place(N_A + j - 1, jnp.where(pick > 0.5, block[BLK:], block[:BLK]), pick)
        else:
            place(N_A + N_B, block[BLK:], one)
            place(N_A + N_B + 1, block[:BLK], zero)

    sub2 = lax.broadcasted_iota(jnp.int32, (BLK, ROWS), 0)
    lane2 = lax.broadcasted_iota(jnp.int32, (BLK, ROWS), 1) % BLK

    def fold(values, op):
        return op(values.reshape(BLK // 8, 8, ROWS), 0)

    def forward_group(g, carry):
        score[...] = dot(k_both[...], q_both[g])
        top_h = jnp.full((8, ROWS), NEG, F32)
        top_l = jnp.full((8, ROWS), NEG, F32)
        for item in range(ITEMS):
            rows = slice(item * BLK, (item + 1) * BLK)
            s = score[rows]
            if item < N_A:
                top_h = jnp.maximum(top_h, fold(s, jnp.max))
            elif item < N_A + N_B:
                j = item - N_A
                s = jnp.where(sub2 < limits[j], s, NEG)
                score[rows] = s
                best = fold(s, jnp.max)
                top_h = jnp.maximum(top_h, jnp.where(picks[j] > 0.5, best, NEG))
                top_l = jnp.maximum(top_l, jnp.where(picks[j] > 0.5, NEG, best))
            elif item == N_A + N_B:
                limit = length - (15 - low) * BLK
                s = jnp.where((sub2 <= lane2) & (sub2 < limit), s, NEG)
                score[rows] = s
                top_h = jnp.maximum(top_h, fold(s, jnp.max))
            else:
                s = jnp.where(sub2 <= lane2, s, NEG)
                score[rows] = s
                top_l = jnp.maximum(top_l, fold(s, jnp.max))
        top_h = jnp.max(top_h, 0, keepdims=True)
        top_l = jnp.max(top_l, 0, keepdims=True)
        for item in range(ITEMS):
            rows = slice(item * BLK, (item + 1) * BLK)
            if item < N_A or item == N_A + N_B:
                top = top_h
            elif item < N_A + N_B:
                top = jnp.where(picks[item - N_A] > 0.5, top_h, top_l)
            else:
                top = top_l
            probs[g, rows] = jnp.exp(score[rows] - top).astype(BF16)
        o = dot(vt_both[...], probs[g])
        inv_h = 1.0 / o[BLK : BLK + 1]
        inv_l = 1.0 / o[BLK + 8 : BLK + 9]
        high, lower = o[0:HD] * inv_h, o[HD:BLK] * inv_l
        o_norm[g, 0:HD] = high
        o_norm[g, HD:BLK] = lower
        l_inv[g, 0:8] = jnp.broadcast_to(inv_h, (8, ROWS))
        l_inv[g, 8:16] = jnp.broadcast_to(inv_l, (8, ROWS))
        att_t[g, 0:HD, 0:BLK] = lower[:, :BLK].astype(BF16)
        att_t[g, 0:HD, BLK:ROWS] = high[:, :BLK].astype(BF16)
        att_t[g, HD:BLK, 0:BLK] = lower[:, BLK:].astype(BF16)
        att_t[g, HD:BLK, BLK:ROWS] = high[:, BLK:].astype(BF16)
        return carry

    lax.fori_loop(0, 2, forward_group, 0)
    step(up_a, dn_a)
    lax.fori_loop(2, 4, forward_group, 0)
    step(dn_b, wo_in)
    lax.fori_loop(4, 6, forward_group, 0)
    step(up_b, up_a, dn_a, wo_in)
    attended = att_t[...].reshape(WIDTH, ROWS).astype(F32).T.astype(BF16)
    mixed = x_low[...].astype(F32) + dot(attended, f_o[...].reshape(WIDTH, WIDTH)) + obias
    mixed_s[...] = mixed
    n2, _ = normalize(mixed)
    n2s[0] = (n2 * gain2 + shift2).astype(BF16)
    n2_copy = send(n2s.at[0], n2s.at[1], sib)

    step(dn_b, up_a, up_b)
    arrived([go_copy, n2_copy])

    def unit_rows(j, start, size):
        blocks = []
        while size:
            k, r = start // 192, start % 192
            n = min(size, 192 - r)
            blocks.append(f_dn[k % 2, j, k // 2, r : r + n])
            start, size = start + n, size - n
        return jnp.concatenate(blocks, 0)

    coef = 0.7978845608028654

    def low_sum(own, *others):
        total = own.astype(F32)
        for other in others:
            total = total + other.astype(F32)
        return total.astype(BF16)

    class Down:
        def __init__(self, j):
            self.j = j

        def z(self):
            halves_ = [(j, slice(96 * j, 96 * (j + 1))) for j in (0, 1)]
            return [
                send(g_dn.at[self.j, oz, :, rows], rz_dn.at[self.j, :, rows], z_of[e])
                for e, rows in halves_
            ]

        def c(self):
            j = self.j
            g_dn[j, zl] = low_sum(g_dn[j, zl], rz_dn[j])
            s_dn[2 * co + j] = g_dn[j, zl, co]
            return [send(g_dn.at[j, zl, oc], s_dn.at[2 * co + j], sib)]

        def y(self):
            return [send(s_dn.at[(yy + k) % 4], ry_dn.at[k - 1], y_peer(k)) for k in (1, 2, 3)]

        def x(self):
            s_dn[yy] = low_sum(s_dn[yy], *[ry_dn[k] for k in range(3)])
            return [
                send(s_dn.at[yy, quarter_dn((xx + k) % 4)], rx_dn.at[k - 1], x_peer(k))
                for k in (1, 2, 3)
            ]

        def h(self):
            rh_dn[1] = low_sum(s_dn[yy, quarter_dn(xx)], *[rx_dn[k] for k in range(3)])
            return [send(rh_dn.at[1], rh_dn.at[0], h_peer)]

        def a(self):
            f2_dn[xx] = low_sum(rh_dn[0], rh_dn[1])
            return [send(f2_dn.at[xx], f2_dn.at[xx], x_peer(k)) for k in (1, 2, 3)]

    def quarter_dn(k):
        return pl.ds(pl.multiple_of(k * 48, 16), 48)

    class Near:
        def __init__(self, j):
            self.j, self.cols = j, slice(j * WIDTH + 512, (j + 1) * WIDTH)

        def quarter(self, k):
            return k // 2, slice(None), pl.ds(pl.multiple_of((k % 2) * BLK, BLK), BLK)

        def z(self):
            return [
                send(
                    g_up.at[pl.ds(2 * e, 2), oz, :, :, self.cols],
                    rz_up.at[self.j, pl.ds(2 * e, 2)],
                    z_of[e],
                )
                for e in (0, 1)
            ]

        def c(self):
            cols, j = self.cols, self.j
            g_up[:, zl, :, :, cols] = low_sum(g_up[:, zl, :, :, cols], rz_up[j])
            s_up[j, :, co] = g_up[:, zl, co, :, cols]
            return [send(g_up.at[:, zl, oc, :, cols], s_up.at[j, :, co], sib)]

        def y(self):
            j = self.j
            return [
                send(s_up.at[j, (yy + k) % 4], ry_up.at[j, k - 1], y_peer(k)) for k in (1, 2, 3)
            ]

        def x(self):
            j = self.j
            s_up[j, yy] = low_sum(s_up[j, yy], *[ry_up[j, k] for k in range(3)])
            return [
                send(s_up.at[(j, yy) + self.quarter((xx + k) % 4)], rx_up.at[j, k - 1], x_peer(k))
                for k in (1, 2, 3)
            ]

        def h(self):
            j = self.j
            rh_up[j, 1] = low_sum(s_up[(j, yy) + self.quarter(xx)], *[rx_up[j, k] for k in range(3)])
            return [send(rh_up.at[j, 1], rh_up.at[j, 0], h_peer)]

        def a(self):
            ref = f2_up.at[self.j, xx]
            f2_up[self.j, xx] = low_sum(rh_up[self.j, 0], rh_up[self.j, 1])
            return [send(ref, ref, x_peer(k)) for k in (1, 2, 3)]

    class Far:
        def __init__(self, j):
            self.j = j

        def quarter(self, k):
            return pl.ds(pl.multiple_of(self.j * WIDTH + k * BLK, BLK), BLK)

        def x(self):
            return [
                send(g_up.at[:, :, :, :, self.quarter((xx + k) % 4)], fx.at[self.j, k - 1], x_peer(k))
                for k in (1, 2, 3)
            ]

        def z(self):
            j = self.j
            fg[j] = low_sum(g_up[:, :, :, :, self.quarter(xx)], *[fx[j, k] for k in range(3)])
            return [
                send(fg.at[j, pl.ds(2 * e, 2), oz], fz.at[j, pl.ds(2 * e, 2)], z_of[e])
                for e in (0, 1)
            ]

        def c(self):
            j = self.j
            fg[j, :, zl] = low_sum(fg[j, :, zl], fz[j])
            fs_up[j, :, co] = fg[j, :, zl, co]
            return [send(fg.at[j, :, zl, oc], fs_up.at[j, :, co], sib)]

        def y(self):
            j = self.j
            return [
                send(fs_up.at[j, (yy + k) % 4], fy.at[j, k - 1], y_peer(k)) for k in (1, 2, 3)
            ]

        def h(self):
            j = self.j
            fh[j, 1] = low_sum(fs_up[j, yy], *[fy[j, k] for k in range(3)])
            return [send(fh.at[j, 1], fh.at[j, 0], h_peer)]

        def a(self):
            ref = fa.at[self.j, xx]
            fa[self.j, xx] = low_sum(fh[self.j, 0], fh[self.j, 1])
            return [send(ref, ref, x_peer(k)) for k in (1, 2, 3)]

    down = [Down(j) for j in (0, 1)]
    downs = [
        Chain(down[0].z, down[0].c),
        Chain(down[1].z, down[1].c, down[1].y, down[1].x, down[1].h, down[1].a),
    ]
    nears = [Chain(u.z, u.c, u.y, u.x, u.h, u.a) for u in map(Near, (0, 1))]
    fars = [Chain(u.x, u.z, u.c, u.y, u.h, u.a) for u in map(Far, (0, 1))]

    def square(grad, rc, rz, ry, cx, ch):
        def c():
            return [send(grad.at[:, :, oc], rc, sib)]

        def z():
            grad[:, :, co] = low_sum(grad[:, :, co], rc[...])
            return [
                send(grad.at[pl.ds(2 * e, 2), oz, co], rz.at[pl.ds(2 * e, 2)], z_of[e])
                for e in (0, 1)
            ]

        def y():
            grad[:, zl, co] = low_sum(grad[:, zl, co], rz[...])
            return [
                send(grad.at[(yy + k) % 4, zl, co], ry.at[k - 1], y_peer(k)) for k in (1, 2, 3)
            ]

        def x():
            cx[0] = low_sum(grad[yy, zl, co], *[ry[k] for k in range(3)])
            return [send(cx.at[0], cx.at[k], x_peer(k)) for k in (1, 2, 3)]

        def h():
            ch[0] = low_sum(cx[0], *[cx[k] for k in (1, 2, 3)])
            return [send(ch.at[0], ch.at[1], h_peer)]

        return Chain(c, z, y, x, h)

    def direct(grad, rc, got, shares):
        def c():
            return [send(grad.at[:, :, oc], rc, sib)]

        def group():
            grad[:, :, co] = low_sum(grad[:, :, co], rc[...])
            out = []
            for k in range(1, 8):
                dst = shard_peer(2 * k)
                out.append(send(grad.at[dst // 4, (dst // 2) % 2, co], got.at[k], (ctx, dst)))
            return out

        def peers():
            shares[0] = low_sum(grad[yy, zl, co], *[got[k] for k in range(1, 8)])
            return [send(shares.at[0], shares.at[j], (peer(j), fs)) for j in range(1, PEERS)]

        return Chain(c, group, peers)

    def total_of(shares, n):
        total = shares[0].astype(F32)
        for j in range(1, n):
            total = total + shares[j].astype(F32)
        return total

    out_w = square(g_o, rc_o, rz_o, ry_o, cx_o, ch_o)
    query_a = square(g_q, rc_q, rz_q, ry_q, cx_q, ch_q)
    query_b = square(g_r, rc_r, rz_r, ry_r, cx_r, ch_r)
    tail = direct(g_t, rc_t, r_t, c_t)

    thirds = [slice(256 * n, 256 * (n + 1)) for n in range(3)]
    n2_t[...] = n2s[...].reshape(2 * ROWS, WIDTH).astype(F32).T.astype(BF16)
    up_sums = []

    def middle(j):
        for n in thirds:
            cols = slice(j * WIDTH + n.start, j * WIDTH + n.stop)
            bias = jnp.where(co == 0, vec[8 + j : 9 + j, n], vec[10 + j : 11 + j, n])
            n2b = n2s[...].reshape(2 * ROWS, WIDTH)
            gob = gos[...].reshape(2 * ROWS, WIDTH)
            up = dot(n2b, f_up[:, :, :, :, cols].reshape(WIDTH, 256)) + bias
            dmid = dot_nt(gob, unit_rows(j, n.start, 256))
            square = up * up
            th = jnp.tanh(coef * up * (1.0 + 0.044715 * square))
            half_sum = 0.5 + 0.5 * th
            mid[:, cols] = (up * half_sum).astype(BF16)
            slope = half_sum + 0.5 * up * (1.0 - th * th) * coef * (1.0 + 3 * 0.044715 * square)
            du = (dmid * slope).astype(BF16)
            dup[:, cols] = du
            up_sums.append(jnp.sum(du.astype(F32), 0, keepdims=True))

    def weight_grads(j):
        m_t = mid[:, j * WIDTH : (j + 1) * WIDTH].astype(F32).T.astype(BF16)
        for n in thirds:
            piece = dot(m_t, gos[:, :, n].reshape(2 * ROWS, 256))
            g_dn[j, :, :, :, n] = piece.astype(BF16).reshape(2, 2, 192, 256)
        step(downs[j])
        for n in thirds:
            cols = slice(j * WIDTH + n.start, j * WIDTH + n.stop)
            piece = dot(n2_t[...], dup[:, cols])
            g_up[:, :, :, :, cols] = piece.astype(BF16).reshape(4, 2, 2, 48, 256)
            if n.stop == 512:
                step(fars[j])
        step(nears[j])

    step(dn_a, dn_b, up_a)
    middle(0)
    step(up_b)
    weight_grads(0)
    step(up_b)
    middle(1)
    for n in thirds:
        w = f_up[...].reshape(WIDTH, HALF)[n]
        piece = dot_nt(dup[...], w)
        dsec_own[:, n] = piece[:ROWS]
        dsec_out[:, n] = piece[ROWS:].astype(BF16)
    dsec_copy = send(dsec_out, dsec_in, sib)
    weight_grads(1)

    arrived([dsec_copy])
    dsec = dsec_own[...] + dsec_in[...].astype(F32)
    n2, rate2 = normalize(mixed_s[...])
    sum_gain2 = jnp.sum(dsec * n2, 0, keepdims=True)
    sum_shift2 = jnp.sum(dsec, 0, keepdims=True)
    dmix = grad_out() + norm_back(n2, rate2, dsec, gain2)
    cotangent[0] = dmix[:BLK]
    cotangent[1] = dmix[BLK:]
    dmix_low = dmix.astype(BF16)
    dmix_r = dmix_low.astype(F32)
    sum_obias = jnp.sum(dmix_r, 0, keepdims=True)
    sum_dbias = jnp.sum(gos[0].astype(F32), 0, keepdims=True)

    g_o[...] = (
        dot(att_t[...].reshape(WIDTH, ROWS), dmix_low).astype(BF16).reshape(4, 2, 2, 48, WIDTH)
    )
    step(out_w)

    for n in thirds:
        blocks = [f_dn[c, j, z, :, n] for j in (0, 1) for z in (0, 1) for c in (0, 1)]
        piece = dot(mid[...], jnp.concatenate(blocks, 0))
        dsec_own[:, n] = piece[:ROWS]
        part_out[:, n] = piece[ROWS:].astype(BF16)
    part_copy = send(part_out, part_in, sib)

    datt = dot(f_o[...].reshape(WIDTH, WIDTH), dmix_r.T.astype(BF16)).astype(BF16).astype(F32)
    deltas = []
    for g in range(GROUPS):
        h0, h1 = datt[g * BLK : g * BLK + HD], datt[g * BLK + HD : (g + 1) * BLK]
        high = jnp.concatenate([h0[:, BLK:], h1[:, BLK:]], 1) * l_inv[g, 0:1]
        lower = jnp.concatenate([h0[:, :BLK], h1[:, :BLK]], 1) * l_inv[g, 8:9]
        both = jnp.concatenate([high, lower], 0)
        do_both[g] = both.astype(BF16)
        do_rows[g] = both.T.astype(BF16)
        both = both.astype(BF16).astype(F32) * o_norm[g]
        l_inv[g, 0:8] = jnp.broadcast_to(jnp.sum(both[:HD], 0, keepdims=True), (8, ROWS))
        l_inv[g, 8:16] = jnp.broadcast_to(jnp.sum(both[HD:], 0, keepdims=True), (8, ROWS))

    acc[...] = jnp.zeros_like(acc)

    def backward_group(g, carry, query=True):
        acc[:, BLK:ROWS] += dot(probs[g], do_rows[g])
        delta_h, delta_l = l_inv[g, 0:1], l_inv[g, 8:9]
        score[...] = dot(v_both[...], do_both[g])
        for item in range(ITEMS):
            rows = slice(item * BLK, (item + 1) * BLK)
            if item < N_A or item == N_A + N_B:
                delta = delta_h
            elif item < N_A + N_B:
                delta = jnp.where(picks[item - N_A] > 0.5, delta_h, delta_l)
            else:
                delta = delta_l
            probs[g, rows] = (probs[g, rows].astype(F32) * (score[rows] - delta)).astype(BF16)
        acc[:, 0:BLK] += dot(probs[g], q_rows[g])
        if query:
            query_grad(g)
        return carry

    def query_grad(g):
        dq = dot(kt_both[...], probs[g]) * (HD**-0.5)
        do_both[g, 0:HD, 0:BLK] = dq[HD:, :BLK].astype(BF16)
        do_both[g, 0:HD, BLK:ROWS] = dq[:HD, :BLK].astype(BF16)
        do_both[g, HD:BLK, 0:BLK] = dq[HD:, BLK:].astype(BF16)
        do_both[g, HD:BLK, BLK:ROWS] = dq[:HD, BLK:].astype(BF16)

    step(downs[0])
    lax.fori_loop(0, 2, backward_group, 0)
    step(nears[0], fars[0], out_w)
    lax.fori_loop(2, 4, backward_group, 0)
    dq_a = do_both[0:4].reshape(512, ROWS).astype(F32).T
    sum_qa = jnp.sum(dq_a, 0, keepdims=True)
    dq_a = dq_a.astype(BF16)
    g_q[...] = dot(xn_t[...], dq_a).astype(BF16).reshape(4, 2, 2, 48, 512)
    step(query_a, nears[0])
    lax.fori_loop(4, 6, functools.partial(backward_group, query=False), 0)

    def halves(item, second):
        rows = slice(item * BLK, (item + 1) * BLK)
        at = HD if second else 0
        return jnp.concatenate(
            [acc[rows, at : at + HD], acc[rows, BLK + at : BLK + at + HD]], 1
        )

    dkv_copies = []
    for j in range(1, PEERS):
        item = N_A + j - 1
        pick = picks[j - 1]
        other = jnp.where(pick > 0.5, halves(item, False), halves(item, True))
        dkv_out[j, 0:BLK] = (halves(j, False) + (1.0 - pick) * other).astype(BF16)
        dkv_out[j, BLK:ROWS] = (pick * other).astype(BF16)
        dkv_copies.append(send(dkv_out.at[j], dkv_in.at[j], (from_peer(j), fs)))

    query_grad(4)
    query_grad(5)
    dq_b = do_both[4:6].reshape(256, ROWS).astype(F32).T
    sum_qbias = jnp.concatenate([sum_qa, jnp.sum(dq_b, 0, keepdims=True)], 1)
    dq_b = dq_b.astype(BF16)
    g_r[...] = dot(xn_t[...], dq_b).astype(BF16).reshape(4, 2, 2, 48, 256)
    step(query_b)
    step(downs[1], downs[0], fars[1], query_a)
    dfirst = dot_nt(dq_a, f_q[:, :, :, :, 0:512].reshape(WIDTH, 512))
    dfirst = dfirst + dot_nt(dq_b, f_q[:, :, :, :, 512:WIDTH].reshape(WIDTH, 256))

    zeros = jnp.zeros((1, WIDTH), F32)
    g_t[:, :, :, :, BLK:ROWS] = (
        jnp.concatenate(
            [zeros] * 4
            + [sum_dbias, sum_gain2, sum_shift2, sum_obias, zeros, zeros, sum_qbias]
            + [jnp.zeros((BLK - 11, WIDTH), F32)],
            0,
        )
        .T.astype(BF16)
        .reshape(4, 2, 2, 48, BLK)
    )
    lanes = lax.broadcasted_iota(jnp.int32, (48, BLK), 1)
    for j in (0, 1):
        sums = jnp.concatenate(up_sums[3 * j : 3 * j + 3], 1)
        sums = jnp.broadcast_to(sums, (BLK, WIDTH)).T
        for k in range(4):
            block = g_t[2 * co + j, k // 2, k % 2, :, BLK:ROWS].astype(F32)
            for r in range(4):
                at = k * 192 + r * 48
                block = jnp.where(lanes == r, sums[at : at + 48], block)
            g_t[2 * co + j, k // 2, k % 2, :, BLK:ROWS] = block.astype(BF16)

    step(fars[0], nears[1], query_b, downs[1], nears[0], fars[0], nears[1], out_w, fars[1], query_a)

    top = halves(0, False) + halves(N_A + N_B + 1, True)
    dkv = jnp.concatenate([top, halves(N_A + N_B, False)], 0)
    arrived(dkv_copies)
    for j in range(1, PEERS):
        dkv = dkv + dkv_in[j].astype(F32)
    dkv = dkv.astype(BF16)
    sum_kv = jnp.sum(dkv.astype(F32), 0, keepdims=True)
    g_kv = dot(xn_t[...], dkv)
    dfirst = dfirst + dot_nt(dkv, f_kv[...].reshape(WIDTH, 2 * HD))

    n1, rate1 = normalize(x_low[...].astype(F32))
    sum_gain1 = jnp.sum(dfirst * n1, 0, keepdims=True)
    sum_shift1 = jnp.sum(dfirst, 0, keepdims=True)

    columns = jnp.concatenate(
        [zeros] * 8 + [sum_gain1, sum_shift1] + [jnp.zeros((BLK - 10, WIDTH), F32)], 0
    ).T
    lanes = lax.broadcasted_iota(jnp.int32, (WIDTH, BLK), 1)
    known = g_t[:, :, :, :, BLK:ROWS].reshape(WIDTH, BLK).astype(F32)
    columns = jnp.where((lanes == 8) | (lanes == 9), columns, known)
    columns = jnp.where(lanes < HD, columns, sum_kv)
    g_t[:, :, :, :, 0:BLK] = g_kv.astype(BF16).reshape(4, 2, 2, 48, BLK)
    g_t[:, :, :, :, BLK:ROWS] = columns.astype(BF16).reshape(4, 2, 2, 48, BLK)
    step(tail)

    ing = cotangent[...].reshape(ROWS, WIDTH) + norm_back(n1, rate1, dfirst, gain1)
    cotangent[0] = jnp.where(swap, ing[BLK:], ing[:BLK])
    cotangent[1] = jnp.where(swap, ing[:BLK], ing[BLK:])
    done = [keep(cotangent, ing_hbm)]
    arrived([part_copy])
    res = valid * (mixed_s[...] + dsec_own[...] + part_in[...].astype(F32) + dbias)
    tokens[0] = jnp.where(swap, res[BLK:], res[:BLK]).astype(BF16)
    tokens[1] = jnp.where(swap, res[:BLK], res[BLK:]).astype(BF16)
    done.append(keep(tokens, out_hbm))

    step(tail, query_b, fars[1], out_w, downs[1], nears[0], fars[0], nears[1], query_a, query_b, out_w)
    step(tail)
    step(fars[1], downs[1], nears[0], nears[1], fars[0], query_a, query_b)
    step(downs[1], nears[1], fars[1], query_b)
    step(out_w)
    go_ref[...] = total_of(ch_o, 2)
    done.append(keep(go_ref, go_hbm))
    step(downs[1], nears[1], fars[1], query_a)
    step(query_b)
    gq_ref[:, 0:512] = total_of(ch_q, 2)
    gq_ref[:, 512:WIDTH] = total_of(ch_r, 2)
    done.append(keep(gq_ref, gq_hbm))
    step(fars[0], nears[0], downs[1])
    gdn_ref[...] = f2_dn[...].astype(F32).reshape(192, WIDTH)
    done.append(keep(gdn_ref, gdn_hbm))
    step(nears[1], fars[1])
    for j in (0, 1):
        for k in range(4):
            at = (k // 2) * HALF + j * WIDTH + 512 + (k % 2) * BLK
            gup_ref[:, at : at + BLK] = f2_up[j, k].astype(F32)
            for half in (0, 1):
                at = half * HALF + j * WIDTH + k * BLK
                gup_ref[:, at : at + BLK] = fa[j, k, half].astype(F32)
    done.append(keep(gup_ref, gup_hbm))
    step(tail)
    gt_ref[...] = total_of(c_t, PEERS)
    done.append(keep(gt_ref, gt_hbm))
    gathers = (kvv, wq_in, wo_in, dn_a, dn_b, up_a, up_b)
    for chain in gathers + (out_w, query_a, query_b, tail, *downs, *nears, *fars):
        assert not chain.steps and not chain.flying
    for copy in done:
        copy.wait()

    for copy in started:
        copy.wait_send()


def finish_kernel(
    out_in,
    ing_in,
    gq_in,
    go_in,
    gt_in,
    gup_in,
    gdn_in,
    out,
    ing,
    gain1,
    shift1,
    gq,
    qbias,
    gkv,
    vbias,
    go,
    obias,
    gain2,
    shift2,
    gup,
    ubias,
    gdn,
    dbias,
    stage0,
    stage1,
    stage2,
    stage3,
    stage4,
    stage5,
    sems,
):
    stages = (stage0, stage1, stage2, stage3, stage4, stage5)
    pairs = ((ing_in, ing), (gup_in, gup), (gdn_in, gdn), (out_in, out), (gq_in, gq), (go_in, go))
    loads, stores = [], []
    for i, ((src, dst), stage) in enumerate(zip(pairs, stages)):
        loads.append(pltpu.make_async_copy(src, stage, sems.at[i]))
        stores.append(pltpu.make_async_copy(stage, dst, sems.at[6 + i]))
        loads[i].start()
    fs = lax.axis_index("fsdp")
    gkv[...] = gt_in[:, 0:BLK]
    columns = gt_in[:, BLK : 2 * BLK]
    rows = jnp.concatenate([columns, jnp.zeros((BLK - 48, BLK), F32)], 0).T
    for k, ref in ((4, dbias), (5, gain2), (6, shift2), (7, obias), (8, gain1), (9, shift1), (10, qbias)):
        ref[...] = rows[k, 0:48]
    ubias[...] = jnp.concatenate([rows[r : r + 1, 0:48] for r in range(4)], 1)[0]
    lane = lax.broadcasted_iota(jnp.int32, (8, BLK), 1)
    pick = jnp.zeros((8, BLK), F32)
    for i in range(4):
        value = jnp.sum(jnp.where(lane == HD + fs * 4 + i, columns[0:8], 0.0), 1, keepdims=True)
        pick = jnp.where(lane == i, value, pick)
    vbias[...] = pick[0, 0:4]
    for load, store in zip(loads, stores):
        load.wait()
        store.start()
    for store in stores:
        store.wait()


def shards(
    tokens,
    lengths,
    block_map,
    first_gain,
    first_shift,
    query_weight,
    query_bias,
    keyval_weight,
    value_bias,
    output_weight,
    output_bias,
    second_gain,
    second_shift,
    up_weight,
    up_bias,
    down_weight,
    down_bias,
    cotangent,
):
    vmem = pl.BlockSpec(memory_space=pltpu.VMEM)
    smem = pl.BlockSpec(memory_space=pltpu.SMEM)
    hbm = pl.BlockSpec(memory_space=pl.ANY)

    def v(*shape, dtype=BF16):
        return pltpu.VMEM(shape, dtype)

    shapes = (
        jax.ShapeDtypeStruct((2, BLK, WIDTH), BF16),
        jax.ShapeDtypeStruct((2, BLK, WIDTH), F32),
        jax.ShapeDtypeStruct((48, WIDTH), F32),
        jax.ShapeDtypeStruct((48, WIDTH), F32),
        jax.ShapeDtypeStruct((48, 2 * BLK), F32),
        jax.ShapeDtypeStruct((48, FF), F32),
        jax.ShapeDtypeStruct((192, WIDTH), F32),
    )
    scratch = [
        v(2, BLK, WIDTH),
        v(2, BLK, WIDTH, dtype=F32),
        v(16, WIDTH),
    ]
    scratch += [v(*shape.shape, dtype=shape.dtype) for shape in shapes[2:]]
    scratch += [
        v(4, 2, 2, 16, WIDTH),
        v(4, 2, 2, 48, WIDTH),
        v(4, 2, 2, 48, 2 * HD),
        v(4, 2, 2, 48, WIDTH),
        v(4, 2, 2, 48, HALF),
        v(4, 2, 48, HALF),
        v(3, 2, 2, 192, WIDTH),
        v(4, 2, 2, 48, 512),
        v(4, 2, 2, 48, WIDTH),
        v(4, 2, 2, 48, 2 * BLK),
        v(4, 2, 2, 48, HALF),
        v(2, 2, 2, 192, WIDTH),
        v(4, 2, 48, 512),
        v(4, 2, 48, WIDTH),
        v(4, 48, 512),
        v(4, 48, WIDTH),
        v(2, 4, 2, 48, 256),
        v(2, 2, 192, WIDTH),
        v(2, 4, 2, 48, 256),
        v(4, 192, WIDTH),
        v(3, 48, 512),
        v(3, 48, WIDTH),
        v(2, 3, 2, 48, 256),
        v(3, 192, WIDTH),
        v(2, 3, 48, BLK),
        v(3, 48, WIDTH),
        v(2, 2, 48, BLK),
        v(2, 48, WIDTH),
        v(2, 4, 48, BLK),
        v(4, 48, WIDTH),
        v(2, 3, 4, 2, 2, 48, BLK),
        v(2, 4, 2, 2, 48, BLK),
        v(2, 4, 2, 48, BLK),
        v(2, 4, 2, 48, BLK),
        v(2, 3, 2, 48, BLK),
        v(2, 2, 2, 48, BLK),
        v(2, 4, 2, 48, BLK),
        v(4, 2, 2, 48, 256),
        v(4, 2, 48, 256),
        v(4, 48, 256),
        v(3, 48, 256),
        v(4, 48, 256),
        v(2, 48, 256),
        v(4, 2, 48, 256),
        v(8, 48, 2 * BLK),
        v(4, 48, 512),
        v(4, 48, WIDTH),
        v(2, 48, 512),
        v(2, 48, WIDTH),
        v(PEERS, 48, 2 * BLK),
        v(PEERS, ROWS, 2 * HD),
        v(PEERS, ROWS, 2 * HD),
        v(PEERS, ROWS, 2 * HD),
        v(KEYS, BLK),
        v(KEYS, BLK),
        v(BLK, KEYS),
        v(BLK + 16, KEYS),
        v(GROUPS, BLK, ROWS),
        v(GROUPS, ROWS, BLK),
        v(GROUPS, KEYS, ROWS),
        v(KEYS, ROWS, dtype=F32),
        v(KEYS, ROWS, dtype=F32),
        v(GROUPS, BLK, ROWS, dtype=F32),
        v(GROUPS, 16, ROWS, dtype=F32),
        v(GROUPS, BLK, ROWS),
        v(GROUPS, BLK, ROWS),
        v(GROUPS, ROWS, BLK),
        v(ROWS, WIDTH),
        v(ROWS, WIDTH),
        v(WIDTH, ROWS),
        v(ROWS, WIDTH, dtype=F32),
        v(2, ROWS, WIDTH),
        v(WIDTH, 2 * ROWS),
        v(2, ROWS, WIDTH),
        v(2 * ROWS, HALF),
        v(2 * ROWS, HALF),
        v(ROWS, WIDTH),
        v(ROWS, WIDTH),
        v(ROWS, WIDTH, dtype=F32),
        v(ROWS, WIDTH),
        v(ROWS, WIDTH),
        pltpu.SemaphoreType.DMA((SEMS,)),
        pltpu.SemaphoreType.DMA((SEMS,)),
        pltpu.SemaphoreType.DMA((32,)),
    ]
    outs = pl.pallas_call(
        layer_kernel,
        out_shape=shapes,
        in_specs=[smem, smem, hbm, hbm] + [vmem] * 9 + [hbm] * 5,
        out_specs=(hbm,) * 7,
        scratch_shapes=scratch,
        compiler_params=pltpu.CompilerParams(
            collective_id=0, has_side_effects=True, vmem_limit_bytes=62 * 2**20
        ),
    )(
        lengths,
        block_map,
        tokens[0],
        cotangent[0],
        first_gain,
        first_shift,
        query_bias,
        value_bias,
        output_bias,
        second_gain,
        second_shift,
        up_bias,
        down_bias,
        query_weight,
        keyval_weight,
        output_weight,
        up_weight,
        down_weight,
    )

    def f(*shape):
        return jax.ShapeDtypeStruct(shape, F32)

    results = pl.pallas_call(
        finish_kernel,
        out_shape=(
            shapes[0],
            shapes[1],
            f(48),
            f(48),
            f(48, WIDTH),
            f(48),
            f(48, 2 * HD),
            f(4),
            f(48, WIDTH),
            f(48),
            f(48),
            f(48),
            f(48, FF),
            f(192),
            f(192, WIDTH),
            f(48),
        ),
        in_specs=[hbm] * 4 + [vmem] + [hbm] * 2,
        out_specs=tuple(
            hbm if i in (0, 1, 4, 8, 12, 14) else vmem for i in range(16)
        ),
        scratch_shapes=[
            pltpu.VMEM(shapes[i].shape, shapes[i].dtype) for i in (1, 5, 6, 0, 2, 3)
        ]
        + [pltpu.SemaphoreType.DMA((12,))],
    )(*outs)
    return (results[0][None], results[1][None]) + tuple(results[2:])


def solution(mesh):
    rows, matrix, batch = P("fsdp"), P("fsdp", None), P("fsdp", "ctx", None, None)
    return jax.shard_map(
        shards,
        mesh=mesh,
        in_specs=(
            batch,
            rows,
            P(),
            rows,
            rows,
            matrix,
            rows,
            matrix,
            rows,
            matrix,
            rows,
            rows,
            rows,
            matrix,
            rows,
            matrix,
            rows,
            batch,
        ),
        out_specs=(
            batch,
            batch,
            rows,
            rows,
            matrix,
            rows,
            matrix,
            rows,
            matrix,
            rows,
            rows,
            rows,
            matrix,
            rows,
            matrix,
            rows,
        ),
        check_vma=False,
    )
```

```python
import functools

import jax
import jax.numpy as jnp
from jax import lax
from jax.experimental import pallas as pl
from jax.experimental.pallas import tpu as pltpu
from jax.sharding import PartitionSpec as P

EPS = 1e-05
NEG = -1e30
MESH = pl.DeviceIdType.MESH
F32 = jnp.float32
BF16 = jnp.bfloat16

WIDTH = 768
HEADS = 12
HD = 64
FF = 3072
HALF = FF // 2
BLK = 128
ROWS = 2 * BLK
GROUPS = HEADS // 2
PEERS = 8
N_A, N_B = 8, 7
ITEMS = N_A + N_B + 2
KEYS = ITEMS * BLK
SEMS = 300


class Chain:
    def __init__(self, *steps):
        self.steps = list(steps)
        self.flying = []

    def go(self, arrived):
        arrived(self.flying)
        self.flying = self.steps.pop(0)() if self.steps else []


def dot(left, right):
    return jnp.dot(left, right, preferred_element_type=F32)


def dot_nt(left, right):
    return lax.dot_general(left, right, (((1,), (1,)), ((), ())), preferred_element_type=F32)


def normalize(values):
    centre = values - jnp.mean(values, -1, keepdims=True)
    spread = jnp.mean(centre * centre, -1, keepdims=True)
    rate = lax.rsqrt(spread + EPS)
    return centre * rate, rate


def norm_back(normed, rate, grad, gain):
    scaled = grad * gain
    first = jnp.mean(scaled, -1, keepdims=True)
    second = jnp.mean(scaled * normed, -1, keepdims=True)
    return rate * (scaled - first - normed * second)


def layer_kernel(
    lengths,
    block_map,
    tokens_in,
    cotangent_in,
    own_gain1,
    own_shift1,
    own_qbias,
    own_vbias,
    own_obias,
    own_gain2,
    own_shift2,
    own_ubias,
    own_dbias,
    wq,
    wkv,
    wo,
    wup,
    wdn,
    out_hbm,
    ing_hbm,
    gq_hbm,
    go_hbm,
    gt_hbm,
    gup_hbm,
    gdn_hbm,
    tokens,
    cotangent,
    vecs,
    gq_ref,
    go_ref,
    gt_ref,
    gup_ref,
    gdn_ref,
    f_vec,
    f_q,
    f_kv,
    f_o,
    f_up,
    r_up,
    f_dn,
    g_q,
    g_o,
    g_t,
    g_up,
    g_dn,
    rc_q,
    rc_o,
    rz_q,
    rz_o,
    rz_up,
    rz_dn,
    s_up,
    s_dn,
    ry_q,
    ry_o,
    ry_up,
    ry_dn,
    rx_up,
    rx_dn,
    rh_up,
    rh_dn,
    f2_up,
    f2_dn,
    fx,
    fg,
    fz,
    fs_dn,
    fy,
    g_r,
    rc_r,
    rz_r,
    ry_r,
    cx_r,
    ch_r,
    rc_t,
    r_t,
    cx_q,
    cx_o,
    ch_q,
    ch_o,
    c_t,
    kv_all,
    dkv_out,
    dkv_in,
    k_both,
    v_both,
    kt_both,
    vt_both,
    q_both,
    q_rows,
    probs,
    score,
    acc,
    o_norm,
    l_inv,
    att_t,
    do_both,
    do_rows,
    x_low,
    xn,
    xn_t,
    mixed_s,
    n2s,
    n2_t,
    gos,
    mid,
    dup,
    part_out,
    part_in,
    dsec_own,
    dsec_out,
    dsec_in,
    send_sem,
    recv_sem,
    local_sem,
):
    ctx = lax.axis_index("ctx")
    fs = lax.axis_index("fsdp")
    zh, xx = ctx // 4, ctx % 4
    yy, zl, co = fs // 4, (fs // 2) % 2, fs % 2
    oz, oc = 1 - zl, 1 - co

    def peer(j):
        return ((zh + j // 4) % 2) * 4 + (xx + j % 4) % 4

    def from_peer(j):
        return ((zh + j // 4) % 2) * 4 + (xx + 4 - j % 4) % 4

    def shard_peer(k):
        return ((yy + k // 4) % 4) * 4 + ((zl + (k // 2) % 2) % 2) * 2 + (co + k % 2) % 2

    sib = (ctx, fs + 1 - 2 * co)
    z_near = (ctx, fs + 2 - 4 * zl)
    z_far = (ctx + 4 - 8 * zh, fs + 2 - 4 * zl)
    z_of = (z_near, z_far)

    def y_peer(k):
        return (ctx, ((yy + k) % 4) * 4 + zl * 2 + co)

    def x_peer(k):
        return (zh * 4 + (xx + k) % 4, fs)

    h_peer = (ctx + 4 - 8 * zh, fs)
    odd = xx % 2
    x_of = ((ctx + 1 - 2 * odd, fs), (zh * 4 + 3 - xx, fs))

    count = [0]
    started = []

    def send(src, dst, to):
        i = count[0]
        count[0] += 1
        copy = pltpu.make_async_remote_copy(
            src_ref=src,
            dst_ref=dst,
            send_sem=send_sem.at[i],
            recv_sem=recv_sem.at[i],
            device_id=to,
            device_id_type=MESH,
        )
        copy.start()
        started.append(copy)
        return copy

    def arrived(copies):
        for copy in copies:
            copy.wait_recv()

    locals_ = []

    def keep(src, dst):
        i = len(locals_)
        copy = pltpu.make_async_copy(src, dst, local_sem.at[i])
        copy.start()
        locals_.append(copy)
        return copy

    got_tokens = keep(tokens_in, tokens)
    got_cotangent = keep(cotangent_in, cotangent)
    barrier = pltpu.get_barrier_semaphore()
    greeted = [(peer(j), fs) for j in (1, 2, 3, 4)]
    greeted += [(ctx, shard_peer(k)) for k in (1, 2, 4, 8, 12)] + [z_far]
    for device in greeted:
        pl.semaphore_signal(barrier, inc=1, device_id=device, device_id_type=MESH)

    def spread(values, at):
        size = values.shape[1]
        i = lax.broadcasted_iota(jnp.int32, (size, WIDTH), 0)
        lane = lax.broadcasted_iota(jnp.int32, (size, WIDTH), 1)
        return dot(values, jnp.where(lane == at + i, 1.0, 0.0).astype(BF16))

    plain = (own_gain1, own_shift1, own_qbias, own_obias, own_gain2, own_shift2, own_dbias)
    plain = [ref[...].reshape(1, 48) for ref in plain]
    up_row = spread(own_ubias[...].reshape(1, 192), (fs % 4) * 192)
    vecs[...] = jnp.concatenate(
        [spread(value, fs * 48) for value in plain]
        + [spread(own_vbias[...].reshape(1, 4), HD + fs * 4)]
        + [jnp.where(fs // 4 == r, up_row, 0.0) for r in range(4)]
        + [jnp.zeros((4, WIDTH), F32)],
        0,
    ).astype(BF16)

    slot0, slot1 = block_map[2 * ctx], block_map[2 * ctx + 1]
    low = jnp.minimum(slot0, slot1)
    swap = slot0 > slot1
    length = lengths[0]

    got_tokens.wait()
    t0, t1 = tokens[0], tokens[1]
    x_low[0:BLK] = jnp.where(swap, t1, t0)
    x_low[BLK:ROWS] = jnp.where(swap, t0, t1)

    row = lax.broadcasted_iota(jnp.int32, (ROWS, 1), 0)
    pos = jnp.where(row < BLK, low * BLK, (14 - low) * BLK) + row
    valid = (pos < length).astype(F32)

    def grad_out():
        c0, c1 = cotangent[0], cotangent[1]
        both = jnp.concatenate([jnp.where(swap, c1, c0), jnp.where(swap, c0, c1)], 0)
        return valid * both

    got_cotangent.wait()
    gos[0] = grad_out().astype(BF16)

    n1, _ = normalize(x_low[...].astype(F32))
    pl.semaphore_wait(barrier, len(greeted))

    def thirds_of(start, width):
        return (
            pl.ds(pl.multiple_of(start + odd * width, BLK), 2 * width),
            pl.ds(pl.multiple_of(start + odd * 2 * width, BLK), width),
            pl.ds(pl.multiple_of(start + (1 - odd) * 2 * width, BLK), width),
        )

    every = slice(None)

    class Whole:
        def __init__(self, src, full, cols=None, rows=every, dst=None, src_at=0):
            self.src, self.full, self.rows = src, full, rows
            self.dst = full if dst is None else dst
            self.fetch, self.own, self.other = (every,) * 3 if cols is None else thirds_of(*cols)
            self.src_cols = self.fetch
            if cols is not None:
                self.src_cols = pl.ds(
                    pl.multiple_of(src_at + cols[0] + odd * cols[1], BLK), 2 * cols[1]
                )

        def at(self, y, z, cols):
            return self.full.at[y, z, co, self.rows, cols]

        def y(self):
            src, dst = self.src.at[self.rows, self.src_cols], self.at(yy, zl, self.fetch)
            self.kept = keep(src, dst)
            return [send(src, dst, y_peer(k)) for k in (1, 2, 3)]

        def z(self):
            self.kept.wait()
            refs = [self.at(pl.ds(2 * e, 2), zl, self.fetch) for e in (0, 1)]
            return [send(ref, ref, z_of[e]) for e, ref in enumerate(refs)]

        def x(self):
            refs = [self.at(pl.ds(2 * e, 2), every, self.own) for e in (0, 1)]
            return [send(ref, ref, x_of[e]) for e, ref in enumerate(refs)]

        def c(self, cols, z=every):
            ref = self.at(every, z, cols)
            return [send(ref, self.dst.at[every, z, co, self.rows, cols], sib)]

    class Part(Whole):
        def at(self, y, z, cols):
            return self.full.at[y, z, self.rows, cols]

    class Mine(Whole):
        def c(self, cols, z=every):
            return []

    class Units(Whole):
        def at(self, e, z, cols, y=every):
            other = e + co - 2 * e * co
            lead = (1 - other) * co + 2 * other
            return self.full.at[lead, y, z, self.rows, cols]

        def y(self):
            src, dst = self.src.at[self.rows, self.src_cols], self.at(yy // 2, zl, self.fetch, yy % 2)
            self.kept = keep(src, dst)
            return [send(src, dst, y_peer(k)) for k in (1, 2, 3)]

        def z(self):
            self.kept.wait()
            refs = [self.at(e, zl, self.fetch) for e in (0, 1)]
            return [send(ref, ref, z_of[e]) for e, ref in enumerate(refs)]

        def x(self):
            refs = [self.at(e, every, self.own) for e in (0, 1)]
            return [send(ref, ref, x_of[e]) for e, ref in enumerate(refs)]

        def c(self, cols, z=every):
            ref = self.full.at[2, every, z, self.rows, cols]
            return [send(ref, self.full.at[co, every, z, self.rows, cols], sib)]

    def each(arrays, action):
        return [copy for array in arrays for copy in action(array)]

    def narrow(*arrays):
        first = []

        def after_y():
            out = each(arrays, lambda a: a.z())
            first.extend(each(arrays, lambda a: a.c(every, zl)))
            return out

        return Chain(
            lambda: each(arrays, lambda a: a.y()),
            after_y,
            lambda: each(arrays, lambda a: a.c(every, oz)) + first,
        )

    def wide(*arrays):
        first = []

        def after_z():
            out = each(arrays, lambda a: a.x())
            first.extend(each(arrays, lambda a: a.c(a.fetch)))
            return out

        return Chain(
            lambda: each(arrays, lambda a: a.y()),
            lambda: each(arrays, lambda a: a.z()),
            after_z,
            lambda: each(arrays, lambda a: a.c(a.other)) + first,
        )

    def step(*chains):
        for chain in chains:
            chain.go(arrived)

    def up_chunk(j):
        cols = (j * WIDTH, WIDTH // 3)
        return wide(
            Mine(wup, f_up, cols, src_at=co * HALF),
            Part(wup, r_up, cols, dst=f_up, src_at=oc * HALF),
        )

    kvv = narrow(Whole(vecs, f_vec), Whole(wkv, f_kv))
    wq_in, wo_in = narrow(Whole(wq, f_q)), wide(Whole(wo, f_o, (0, 256)))
    dn_a, dn_b = (wide(Units(wdn, f_dn, (0, 256), pl.ds(96 * i, 96))) for i in (0, 1))
    up_a, up_b = up_chunk(0), up_chunk(1)

    step(kvv, wq_in, wo_in, dn_a, dn_b, up_a, up_b)
    step(kvv)
    step(wq_in, kvv)
    step(kvv)
    vec = f_vec[...].astype(F32).reshape(16, 16, WIDTH)
    vec = jnp.sum(vec, 0)
    gain1, shift1, qbias, obias = vec[0:1], vec[1:2], vec[2:3], vec[3:4]
    gain2, shift2, dbias, kvbias = vec[4:5], vec[5:6], vec[6:7], vec[7:8, 0 : 2 * HD]

    xn_v = n1 * gain1 + shift1
    xn[...] = xn_v.astype(BF16)

    kv = dot(xn[...], f_kv[...].reshape(WIDTH, 2 * HD)) + kvbias
    kv_all[0] = kv.astype(BF16)
    kv_copies = [send(kv_all.at[0], kv_all.at[j], (peer(j), fs)) for j in (1, 2, 3)]
    kv_far = send(kv_all.at[0], kv_all.at[4], h_peer)
    xn_t[...] = xn[...].astype(F32).T.astype(BF16)
    step(wo_in, wq_in)
    arrived([kv_far])
    kv_copies += [send(kv_all.at[4], kv_all.at[4 + j], (peer(j), fs)) for j in (1, 2, 3)]
    step(wq_in)

    q = dot(xn[...], f_q[...].reshape(WIDTH, WIDTH)) + qbias
    q = (q.astype(BF16).astype(F32) * (HD**-0.5)).T
    for g in range(GROUPS):
        h0, h1 = q[g * BLK : g * BLK + HD], q[g * BLK + HD : (g + 1) * BLK]
        both = jnp.concatenate(
            [
                jnp.concatenate([h0[:, BLK:], h1[:, BLK:]], 1),
                jnp.concatenate([h0[:, :BLK], h1[:, :BLK]], 1),
            ],
            0,
        )
        q_both[g] = both.astype(BF16)
        q_rows[g] = both.T.astype(BF16)

    step(dn_a, wo_in)
    go_copy = send(gos.at[0], gos.at[1], sib)

    arrived(kv_copies)
    step(dn_b)
    lane = lax.broadcasted_iota(jnp.int32, (BLK, BLK), 1)
    sub = lax.broadcasted_iota(jnp.int32, (BLK, BLK), 0)
    extra = lax.broadcasted_iota(jnp.int32, (16, BLK), 0)

    picks, limits = [], []
    for j in range(1, PEERS):
        c = from_peer(j)
        other = jnp.minimum(block_map[2 * c], block_map[2 * c + 1])
        high = other > low
        picks.append(jnp.where(high, 1.0, 0.0).astype(F32))
        limits.append(length - jnp.where(high, 15 - other, other) * BLK)

    def place(item, block, to_high):
        rows = pl.ds(item * BLK, BLK)
        left = jnp.where(lane < HD, to_high, 1.0 - to_high)
        kk = jnp.concatenate([block[:, :HD], block[:, :HD]], 1) * left
        vv = jnp.concatenate([block[:, HD:], block[:, HD:]], 1) * left
        k_both[rows] = kk.astype(BF16)
        v_both[rows] = vv.astype(BF16)
        kt_both[:, rows] = kk.T.astype(BF16)
        vt_both[0:BLK, rows] = vv.T.astype(BF16)
        vt_both[BLK : BLK + 16, rows] = jnp.where(extra < 8, to_high, 1.0 - to_high).astype(BF16)

    one, zero = jnp.float32(1.0), jnp.float32(0.0)
    for j in range(PEERS):
        block = kv_all[j].astype(F32)
        place(j, block[:BLK], one)
        if j:
            pick = picks[j - 1]
            place(N_A + j - 1, jnp.where(pick > 0.5, block[BLK:], block[:BLK]), pick)
        else:
            place(N_A + N_B, block[BLK:], one)
            place(N_A + N_B + 1, block[:BLK], zero)

    sub2 = lax.broadcasted_iota(jnp.int32, (BLK, ROWS), 0)
    lane2 = lax.broadcasted_iota(jnp.int32, (BLK, ROWS), 1) % BLK

    def fold(values, op):
        return op(values.reshape(BLK // 8, 8, ROWS), 0)

    def forward_group(g, carry):
        score[...] = dot(k_both[...], q_both[g])
        top_h = jnp.full((8, ROWS), NEG, F32)
        top_l = jnp.full((8, ROWS), NEG, F32)
        for item in range(ITEMS):
            rows = slice(item * BLK, (item + 1) * BLK)
            s = score[rows]
            if item < N_A:
                top_h = jnp.maximum(top_h, fold(s, jnp.max))
            elif item < N_A + N_B:
                j = item - N_A
                s = jnp.where(sub2 < limits[j], s, NEG)
                score[rows] = s
                best = fold(s, jnp.max)
                top_h = jnp.maximum(top_h, jnp.where(picks[j] > 0.5, best, NEG))
                top_l = jnp.maximum(top_l, jnp.where(picks[j] > 0.5, NEG, best))
            elif item == N_A + N_B:
                limit = length - (15 - low) * BLK
                s = jnp.where((sub2 <= lane2) & (sub2 < limit), s, NEG)
                score[rows] = s
                top_h = jnp.maximum(top_h, fold(s, jnp.max))
            else:
                s = jnp.where(sub2 <= lane2, s, NEG)
                score[rows] = s
                top_l = jnp.maximum(top_l, fold(s, jnp.max))
        top_h = jnp.max(top_h, 0, keepdims=True)
        top_l = jnp.max(top_l, 0, keepdims=True)
        for item in range(ITEMS):
            rows = slice(item * BLK, (item + 1) * BLK)
            if item < N_A or item == N_A + N_B:
                top = top_h
            elif item < N_A + N_B:
                top = jnp.where(picks[item - N_A] > 0.5, top_h, top_l)
            else:
                top = top_l
            probs[g, rows] = jnp.exp(score[rows] - top).astype(BF16)
        o = dot(vt_both[...], probs[g])
        inv_h = 1.0 / o[BLK : BLK + 1]
        inv_l = 1.0 / o[BLK + 8 : BLK + 9]
        high, lower = o[0:HD] * inv_h, o[HD:BLK] * inv_l
        o_norm[g, 0:HD] = high
        o_norm[g, HD:BLK] = lower
        l_inv[g, 0:8] = jnp.broadcast_to(inv_h, (8, ROWS))
        l_inv[g, 8:16] = jnp.broadcast_to(inv_l, (8, ROWS))
        att_t[g, 0:HD, 0:BLK] = lower[:, :BLK].astype(BF16)
        att_t[g, 0:HD, BLK:ROWS] = high[:, :BLK].astype(BF16)
        att_t[g, HD:BLK, 0:BLK] = lower[:, BLK:].astype(BF16)
        att_t[g, HD:BLK, BLK:ROWS] = high[:, BLK:].astype(BF16)
        return carry

    step(dn_a)
    lax.fori_loop(0, 2, forward_group, 0)
    step(up_a)
    lax.fori_loop(2, 4, forward_group, 0)
    step(dn_b, wo_in)
    lax.fori_loop(4, 6, forward_group, 0)
    step(up_b, up_a, dn_a, wo_in)
    attended = att_t[...].reshape(WIDTH, ROWS).astype(F32).T.astype(BF16)
    mixed = x_low[...].astype(F32) + dot(attended, f_o[...].reshape(WIDTH, WIDTH)) + obias
    mixed_s[...] = mixed
    n2, _ = normalize(mixed)
    n2s[0] = (n2 * gain2 + shift2).astype(BF16)
    n2_copy = send(n2s.at[0], n2s.at[1], sib)

    step(dn_b, up_a, up_b)
    arrived([go_copy, n2_copy])

    def unit_rows(j, start, size):
        blocks = []
        while size:
            k, r = start // 192, start % 192
            n = min(size, 192 - r)
            blocks.append(f_dn[k % 2, j, k // 2, r : r + n])
            start, size = start + n, size - n
        return jnp.concatenate(blocks, 0)

    coef = 0.7978845608028654

    def low_sum(own, *others):
        total = own.astype(F32)
        for other in others:
            total = total + other.astype(F32)
        return total.astype(BF16)

    def corner(half, k):
        rows = pl.ds(pl.multiple_of(96 * half + (k // 2) * 48, 16), 48)
        return rows, pl.ds(pl.multiple_of((k % 2) * 384, BLK), 384)

    class DownNear:
        def z(self, j):
            rows = [slice(48 * e, 48 * (e + 1)) for e in (0, 1)]
            return [
                send(g_dn.at[j, oz, :, r], rz_dn.at[j, :, r], z_of[e]) for e, r in enumerate(rows)
            ]

        def c(self):
            for j in (0, 1):
                g_dn[j, zl, :, 0:96] = low_sum(g_dn[j, zl, :, 0:96], rz_dn[j])
                s_dn[2 * co + j] = g_dn[j, zl, co, 0:96]
            return [send(g_dn.at[:, zl, oc, 0:96], s_dn.at[pl.ds(2 * co, 2)], sib)]

        def y(self):
            return [send(s_dn.at[(yy + k) % 4], ry_dn.at[k - 1], y_peer(k)) for k in (1, 2, 3)]

        def x(self):
            s_dn[yy] = low_sum(s_dn[yy], *[ry_dn[k] for k in range(3)])
            return [
                send(s_dn.at[(yy,) + corner(0, (xx + k) % 4)], rx_dn.at[k - 1], x_peer(k))
                for k in (1, 2, 3)
            ]

        def h(self):
            rh_dn[0, 1] = low_sum(s_dn[(yy,) + corner(0, xx)], *[rx_dn[k] for k in range(3)])
            return [send(rh_dn.at[0, 1], rh_dn.at[0, 0], h_peer)]

        def a(self, i=0):
            f2_dn[i, xx] = low_sum(rh_dn[i, 0], rh_dn[i, 1])
            return [send(f2_dn.at[i, xx], f2_dn.at[i, xx], x_peer(k)) for k in (1, 2, 3)]

    class DownFar:
        def x(self, j):
            return [
                send(g_dn.at[(j, every, every) + corner(1, (xx + k) % 4)], fx.at[j, k - 1], x_peer(k))
                for k in (1, 2, 3)
            ]

        def z(self):
            for j in (0, 1):
                own = g_dn[(j, every, every) + corner(1, xx)]
                fg[j] = low_sum(own, *[fx[j, k] for k in range(3)])
            return [send(fg.at[j, oz], fz.at[j], z_of[j]) for j in (0, 1)]

        def c(self):
            for j in (0, 1):
                fg[j, zl] = low_sum(fg[j, zl], fz[j])
                fs_dn[2 * co + j] = fg[j, zl, co]
            return [send(fg.at[:, zl, oc], fs_dn.at[pl.ds(2 * co, 2)], sib)]

        def y(self):
            return [send(fs_dn.at[(yy + k) % 4], fy.at[k - 1], y_peer(k)) for k in (1, 2, 3)]

        def h(self):
            rh_dn[1, 1] = low_sum(fs_dn[yy], *[fy[k] for k in range(3)])
            return [send(rh_dn.at[1, 1], rh_dn.at[1, 0], h_peer)]

    class Up:
        def __init__(self, j, start, width):
            self.j, self.start, self.half = j, start, width // 2
            self.cols = slice(start, start + width)
            self.from_cols = slice(j * WIDTH + start, j * WIDTH + start + width)
            self.quarter_cols = slice(start // 2, start // 2 + width // 2)

        def quarter(self, k):
            start = pl.multiple_of(self.start + (k % 2) * self.half, BLK)
            return k // 2, every, pl.ds(start, self.half)

        def z(self):
            return [
                send(
                    g_up.at[pl.ds(2 * e, 2), oz, :, :, self.from_cols],
                    rz_up.at[self.j, pl.ds(2 * e, 2), :, :, self.cols],
                    z_of[e],
                )
                for e in (0, 1)
            ]

        def c(self):
            src, cols, j = self.from_cols, self.cols, self.j
            g_up[:, zl, :, :, src] = low_sum(g_up[:, zl, :, :, src], rz_up[j, :, :, :, cols])
            s_up[j, :, co, :, cols] = g_up[:, zl, co, :, src]
            return [send(g_up.at[:, zl, oc, :, src], s_up.at[j, :, co, :, cols], sib)]

        def y(self):
            j, cols = self.j, self.cols
            return [
                send(s_up.at[j, (yy + k) % 4, :, :, cols], ry_up.at[j, k - 1, :, :, cols], y_peer(k))
                for k in (1, 2, 3)
            ]

        def x(self):
            j, cols, part = self.j, self.cols, self.quarter_cols
            s_up[j, yy, :, :, cols] = low_sum(
                s_up[j, yy, :, :, cols], *[ry_up[j, k, :, :, cols] for k in range(3)]
            )
            return [
                send(
                    s_up.at[(j, yy) + self.quarter((xx + k) % 4)],
                    rx_up.at[j, k - 1, :, part],
                    x_peer(k),
                )
                for k in (1, 2, 3)
            ]

        def h(self):
            j, part = self.j, self.quarter_cols
            got = [rx_up[j, k, :, part] for k in range(3)]
            rh_up[j, 1, :, part] = low_sum(s_up[(j, yy) + self.quarter(xx)], *got)
            return [send(rh_up.at[j, 1, :, part], rh_up.at[j, 0, :, part], h_peer)]

        def a(self):
            j, part = self.j, self.quarter_cols
            f2_up[j, xx, :, part] = low_sum(rh_up[j, 0, :, part], rh_up[j, 1, :, part])
            ref = f2_up.at[j, xx, :, part]
            return [send(ref, ref, x_peer(k)) for k in (1, 2, 3)]

    near, far = DownNear(), DownFar()
    dn_near = Chain(near.c, near.y, near.x, near.h, near.a)
    dn_far = Chain(far.z, far.c, far.y, far.h, functools.partial(near.a, 1))
    ups = [
        [Chain(u.z, u.c, u.y, u.x, u.h, u.a) for u in (Up(j, 0, 512), Up(j, 512, 256))] for j in (0, 1)
    ]

    def square(grad, rc, rz, ry, cx, ch):
        def c():
            return [send(grad.at[:, :, oc], rc, sib)]

        def z():
            grad[:, :, co] = low_sum(grad[:, :, co], rc[...])
            return [
                send(grad.at[pl.ds(2 * e, 2), oz, co], rz.at[pl.ds(2 * e, 2)], z_of[e])
                for e in (0, 1)
            ]

        def y():
            grad[:, zl, co] = low_sum(grad[:, zl, co], rz[...])
            return [
                send(grad.at[(yy + k) % 4, zl, co], ry.at[k - 1], y_peer(k)) for k in (1, 2, 3)
            ]

        def x():
            cx[0] = low_sum(grad[yy, zl, co], *[ry[k] for k in range(3)])
            return [send(cx.at[0], cx.at[k], x_peer(k)) for k in (1, 2, 3)]

        def h():
            ch[0] = low_sum(cx[0], *[cx[k] for k in (1, 2, 3)])
            return [send(ch.at[0], ch.at[1], h_peer)]

        return Chain(c, z, y, x, h)

    def direct(grad, rc, got, shares):
        def c():
            return [send(grad.at[:, :, oc], rc, sib)]

        def group():
            grad[:, :, co] = low_sum(grad[:, :, co], rc[...])
            out = []
            for k in range(1, 8):
                dst = shard_peer(2 * k)
                out.append(send(grad.at[dst // 4, (dst // 2) % 2, co], got.at[k], (ctx, dst)))
            return out

        def peers():
            shares[0] = low_sum(grad[yy, zl, co], *[got[k] for k in range(1, 8)])
            return [send(shares.at[0], shares.at[j], (peer(j), fs)) for j in range(1, PEERS)]

        return Chain(c, group, peers)

    def total_of(shares, n):
        total = shares[0].astype(F32)
        for j in range(1, n):
            total = total + shares[j].astype(F32)
        return total

    out_w = square(g_o, rc_o, rz_o, ry_o, cx_o, ch_o)
    query_a = square(g_q, rc_q, rz_q, ry_q, cx_q, ch_q)
    query_b = square(g_r, rc_r, rz_r, ry_r, cx_r, ch_r)
    tail = direct(g_t, rc_t, r_t, c_t)

    thirds = [slice(256 * n, 256 * (n + 1)) for n in range(3)]
    n2_t[...] = n2s[...].reshape(2 * ROWS, WIDTH).astype(F32).T.astype(BF16)
    up_sums = []

    def middle(j):
        for n in thirds:
            cols = slice(j * WIDTH + n.start, j * WIDTH + n.stop)
            bias = jnp.where(co == 0, vec[8 + j : 9 + j, n], vec[10 + j : 11 + j, n])
            n2b = n2s[...].reshape(2 * ROWS, WIDTH)
            gob = gos[...].reshape(2 * ROWS, WIDTH)
            up = dot(n2b, f_up[:, :, :, :, cols].reshape(WIDTH, 256)) + bias
            dmid = dot_nt(gob, unit_rows(j, n.start, 256))
            square = up * up
            th = jnp.tanh(coef * up * (1.0 + 0.044715 * square))
            half_sum = 0.5 + 0.5 * th
            mid[:, cols] = (up * half_sum).astype(BF16)
            slope = half_sum + 0.5 * up * (1.0 - th * th) * coef * (1.0 + 3 * 0.044715 * square)
            du = (dmid * slope).astype(BF16)
            dup[:, cols] = du
            up_sums.append(jnp.sum(du.astype(F32), 0, keepdims=True))

    def weight_grads(j):
        m_t = mid[:, j * WIDTH : (j + 1) * WIDTH].astype(F32).T.astype(BF16)
        for n in thirds:
            piece = dot(m_t, gos[:, :, n].reshape(2 * ROWS, 256))
            g_dn[j, :, :, :, n] = piece.astype(BF16).reshape(2, 2, 192, 256)
        dn_near.flying += near.z(j)
        dn_far.flying += far.x(j)
        for n in thirds:
            cols = slice(j * WIDTH + n.start, j * WIDTH + n.stop)
            piece = dot(n2_t[...], dup[:, cols])
            g_up[:, :, :, :, cols] = piece.astype(BF16).reshape(4, 2, 2, 48, 256)
            if n.stop == 512:
                step(ups[j][0])
        step(ups[j][1])

    step(dn_a, dn_b, up_a)
    middle(0)
    step(up_b)
    weight_grads(0)
    step(up_b)
    middle(1)
    for n in thirds:
        w = f_up[...].reshape(WIDTH, HALF)[n]
        piece = dot_nt(dup[...], w)
        dsec_own[:, n] = piece[:ROWS]
        dsec_out[:, n] = piece[ROWS:].astype(BF16)
    dsec_copy = send(dsec_out, dsec_in, sib)
    weight_grads(1)

    arrived([dsec_copy])
    dsec = dsec_own[...] + dsec_in[...].astype(F32)
    n2, rate2 = normalize(mixed_s[...])
    sum_gain2 = jnp.sum(dsec * n2, 0, keepdims=True)
    sum_shift2 = jnp.sum(dsec, 0, keepdims=True)
    dmix = grad_out() + norm_back(n2, rate2, dsec, gain2)
    cotangent[0] = dmix[:BLK]
    cotangent[1] = dmix[BLK:]
    dmix_low = dmix.astype(BF16)
    dmix_r = dmix_low.astype(F32)
    sum_obias = jnp.sum(dmix_r, 0, keepdims=True)
    sum_dbias = jnp.sum(gos[0].astype(F32), 0, keepdims=True)

    g_o[...] = (
        dot(att_t[...].reshape(WIDTH, ROWS), dmix_low).astype(BF16).reshape(4, 2, 2, 48, WIDTH)
    )
    step(out_w)

    datt = dot(f_o[...].reshape(WIDTH, WIDTH), dmix_r.T.astype(BF16)).astype(BF16).astype(F32)
    deltas = []
    for g in range(GROUPS):
        h0, h1 = datt[g * BLK : g * BLK + HD], datt[g * BLK + HD : (g + 1) * BLK]
        high = jnp.concatenate([h0[:, BLK:], h1[:, BLK:]], 1) * l_inv[g, 0:1]
        lower = jnp.concatenate([h0[:, :BLK], h1[:, :BLK]], 1) * l_inv[g, 8:9]
        both = jnp.concatenate([high, lower], 0)
        do_both[g] = both.astype(BF16)
        do_rows[g] = both.T.astype(BF16)
        both = both.astype(BF16).astype(F32) * o_norm[g]
        l_inv[g, 0:8] = jnp.broadcast_to(jnp.sum(both[:HD], 0, keepdims=True), (8, ROWS))
        l_inv[g, 8:16] = jnp.broadcast_to(jnp.sum(both[HD:], 0, keepdims=True), (8, ROWS))

    acc[...] = jnp.zeros_like(acc)

    def backward_group(g, carry, query=True):
        acc[:, BLK:ROWS] += dot(probs[g], do_rows[g])
        delta_h, delta_l = l_inv[g, 0:1], l_inv[g, 8:9]
        score[...] = dot(v_both[...], do_both[g])
        for item in range(ITEMS):
            rows = slice(item * BLK, (item + 1) * BLK)
            if item < N_A or item == N_A + N_B:
                delta = delta_h
            elif item < N_A + N_B:
                delta = jnp.where(picks[item - N_A] > 0.5, delta_h, delta_l)
            else:
                delta = delta_l
            probs[g, rows] = (probs[g, rows].astype(F32) * (score[rows] - delta)).astype(BF16)
        acc[:, 0:BLK] += dot(probs[g], q_rows[g])
        if query:
            query_grad(g)
        return carry

    def query_grad(g):
        dq = dot(kt_both[...], probs[g]) * (HD**-0.5)
        do_both[g, 0:HD, 0:BLK] = dq[HD:, :BLK].astype(BF16)
        do_both[g, 0:HD, BLK:ROWS] = dq[:HD, :BLK].astype(BF16)
        do_both[g, HD:BLK, 0:BLK] = dq[HD:, BLK:].astype(BF16)
        do_both[g, HD:BLK, BLK:ROWS] = dq[:HD, BLK:].astype(BF16)

    step(ups[0][0])
    lax.fori_loop(0, 2, backward_group, 0)
    step(ups[0][1], ups[0][0], out_w)
    lax.fori_loop(2, 4, backward_group, 0)
    dq_a = do_both[0:4].reshape(512, ROWS).astype(F32).T
    sum_qa = jnp.sum(dq_a, 0, keepdims=True)
    dq_a = dq_a.astype(BF16)
    g_q[...] = dot(xn_t[...], dq_a).astype(BF16).reshape(4, 2, 2, 48, 512)
    step(query_a, dn_near, dn_far, ups[0][1])
    lax.fori_loop(4, 6, functools.partial(backward_group, query=False), 0)

    def halves(item, second):
        rows = slice(item * BLK, (item + 1) * BLK)
        at = HD if second else 0
        return jnp.concatenate(
            [acc[rows, at : at + HD], acc[rows, BLK + at : BLK + at + HD]], 1
        )

    dkv_copies = []
    for j in range(1, PEERS):
        item = N_A + j - 1
        pick = picks[j - 1]
        other = jnp.where(pick > 0.5, halves(item, False), halves(item, True))
        dkv_out[j, 0:BLK] = (halves(j, False) + (1.0 - pick) * other).astype(BF16)
        dkv_out[j, BLK:ROWS] = (pick * other).astype(BF16)
        dkv_copies.append(send(dkv_out.at[j], dkv_in.at[j], (from_peer(j), fs)))

    query_grad(4)
    query_grad(5)
    dq_b = do_both[4:6].reshape(256, ROWS).astype(F32).T
    sum_qbias = jnp.concatenate([sum_qa, jnp.sum(dq_b, 0, keepdims=True)], 1)
    dq_b = dq_b.astype(BF16)
    g_r[...] = dot(xn_t[...], dq_b).astype(BF16).reshape(4, 2, 2, 48, 256)
    step(query_b)
    step(dn_near, ups[1][0], query_a, dn_far)
    for n in thirds:
        blocks = [f_dn[c, j, z, :, n] for j in (0, 1) for z in (0, 1) for c in (0, 1)]
        piece = dot(mid[...], jnp.concatenate(blocks, 0))
        dsec_own[:, n] = piece[:ROWS]
        part_out[:, n] = piece[ROWS:].astype(BF16)
    part_copy = send(part_out, part_in, sib)

    dfirst = dot_nt(dq_a, f_q[:, :, :, :, 0:512].reshape(WIDTH, 512))
    dfirst = dfirst + dot_nt(dq_b, f_q[:, :, :, :, 512:WIDTH].reshape(WIDTH, 256))

    zeros = jnp.zeros((1, WIDTH), F32)
    g_t[:, :, :, :, BLK:ROWS] = (
        jnp.concatenate(
            [zeros] * 4
            + [sum_dbias, sum_gain2, sum_shift2, sum_obias, zeros, zeros, sum_qbias]
            + [jnp.zeros((BLK - 11, WIDTH), F32)],
            0,
        )
        .T.astype(BF16)
        .reshape(4, 2, 2, 48, BLK)
    )
    lanes = lax.broadcasted_iota(jnp.int32, (48, BLK), 1)
    for j in (0, 1):
        sums = jnp.concatenate(up_sums[3 * j : 3 * j + 3], 1)
        sums = jnp.broadcast_to(sums, (BLK, WIDTH)).T
        for k in range(4):
            block = g_t[2 * co + j, k // 2, k % 2, :, BLK:ROWS].astype(F32)
            for r in range(4):
                at = k * 192 + r * 48
                block = jnp.where(lanes == r, sums[at : at + 48], block)
            g_t[2 * co + j, k // 2, k % 2, :, BLK:ROWS] = block.astype(BF16)

    step(ups[1][1], ups[0][0], ups[1][0], dn_far, query_b, out_w)

    top = halves(0, False) + halves(N_A + N_B + 1, True)
    dkv = jnp.concatenate([top, halves(N_A + N_B, False)], 0)
    arrived(dkv_copies)
    for j in range(1, PEERS):
        dkv = dkv + dkv_in[j].astype(F32)
    dkv = dkv.astype(BF16)
    sum_kv = jnp.sum(dkv.astype(F32), 0, keepdims=True)
    g_kv = dot(xn_t[...], dkv)
    dfirst = dfirst + dot_nt(dkv, f_kv[...].reshape(WIDTH, 2 * HD))

    n1, rate1 = normalize(x_low[...].astype(F32))
    sum_gain1 = jnp.sum(dfirst * n1, 0, keepdims=True)
    sum_shift1 = jnp.sum(dfirst, 0, keepdims=True)

    columns = jnp.concatenate(
        [zeros] * 8 + [sum_gain1, sum_shift1] + [jnp.zeros((BLK - 10, WIDTH), F32)], 0
    ).T
    lanes = lax.broadcasted_iota(jnp.int32, (WIDTH, BLK), 1)
    known = g_t[:, :, :, :, BLK:ROWS].reshape(WIDTH, BLK).astype(F32)
    columns = jnp.where((lanes == 8) | (lanes == 9), columns, known)
    columns = jnp.where(lanes < HD, columns, sum_kv)
    g_t[:, :, :, :, 0:BLK] = g_kv.astype(BF16).reshape(4, 2, 2, 48, BLK)
    g_t[:, :, :, :, BLK:ROWS] = columns.astype(BF16).reshape(4, 2, 2, 48, BLK)
    step(tail)

    ing = cotangent[...].reshape(ROWS, WIDTH) + norm_back(n1, rate1, dfirst, gain1)
    cotangent[0] = jnp.where(swap, ing[BLK:], ing[:BLK])
    cotangent[1] = jnp.where(swap, ing[:BLK], ing[BLK:])
    done = [keep(cotangent, ing_hbm)]
    arrived([part_copy])
    res = valid * (mixed_s[...] + dsec_own[...] + part_in[...].astype(F32) + dbias)
    tokens[0] = jnp.where(swap, res[BLK:], res[:BLK]).astype(BF16)
    tokens[1] = jnp.where(swap, res[:BLK], res[BLK:]).astype(BF16)
    done.append(keep(tokens, out_hbm))

    step(ups[0][1], ups[1][1], dn_near, ups[0][0], query_a)
    step(tail, dn_far, ups[0][1], ups[1][0], query_b, out_w, ups[0][0], dn_near, ups[1][1], query_a)
    step(tail)
    step(dn_far, ups[0][1], ups[1][0], dn_near, query_b, out_w, ups[1][1], query_a)
    step(ups[1][0], query_b, ups[1][1])
    step(out_w)
    go_ref[...] = total_of(ch_o, 2)
    done.append(keep(go_ref, go_hbm))
    step(ups[1][0], ups[1][1], query_a)
    step(query_b)
    gq_ref[:, 0:512] = total_of(ch_q, 2)
    gq_ref[:, 512:WIDTH] = total_of(ch_r, 2)
    done.append(keep(gq_ref, gq_hbm))
    step(dn_far, dn_near)
    for half in (0, 1):
        for k in range(4):
            at, to = 96 * half + (k // 2) * 48, (k % 2) * 384
            gdn_ref[at : at + 48, to : to + 384] = f2_dn[half, k].astype(F32)
    done.append(keep(gdn_ref, gdn_hbm))
    step(ups[0][0], ups[0][1], ups[1][0], ups[1][1])
    for j in (0, 1):
        for k in range(4):
            for start, width in ((0, 256), (512, 128)):
                at = (k // 2) * HALF + j * WIDTH + start + (k % 2) * width
                got = f2_up[j, k, :, start // 2 : start // 2 + width]
                gup_ref[:, at : at + width] = got.astype(F32)
    done.append(keep(gup_ref, gup_hbm))
    step(tail)
    gt_ref[...] = total_of(c_t, PEERS)
    done.append(keep(gt_ref, gt_hbm))
    gathers = (kvv, wq_in, wo_in, dn_a, dn_b, up_a, up_b)
    for chain in gathers + (out_w, query_a, query_b, tail, dn_near, dn_far, *ups[0], *ups[1]):
        assert not chain.steps and not chain.flying
    for copy in done:
        copy.wait()

    for copy in started:
        copy.wait_send()


def finish_kernel(
    out_in,
    ing_in,
    gq_in,
    go_in,
    gt_in,
    gup_in,
    gdn_in,
    out,
    ing,
    gain1,
    shift1,
    gq,
    qbias,
    gkv,
    vbias,
    go,
    obias,
    gain2,
    shift2,
    gup,
    ubias,
    gdn,
    dbias,
    stage0,
    stage1,
    stage2,
    stage3,
    stage4,
    stage5,
    sems,
):
    stages = (stage0, stage1, stage2, stage3, stage4, stage5)
    pairs = ((ing_in, ing), (gup_in, gup), (gdn_in, gdn), (out_in, out), (gq_in, gq), (go_in, go))
    loads, stores = [], []
    for (src, dst), stage in zip(pairs, stages):
        if len(src.shape) == 3:
            parts = [(i, pl.ds(64 * k, 64)) for i in (0, 1) for k in (0, 1)]
        else:
            size = src.shape[0] // 3
            parts = [(pl.ds(size * k, size),) for k in range(3)]
        for part in parts:
            i = len(loads)
            loads.append(pltpu.make_async_copy(src.at[part], stage.at[part], sems.at[i]))
            stores.append(pltpu.make_async_copy(stage.at[part], dst.at[part], sems.at[20 + i]))
            loads[i].start()
    fs = lax.axis_index("fsdp")
    gkv[...] = gt_in[:, 0:BLK]
    columns = gt_in[:, BLK : 2 * BLK]
    rows = jnp.concatenate([columns, jnp.zeros((BLK - 48, BLK), F32)], 0).T
    for k, ref in ((4, dbias), (5, gain2), (6, shift2), (7, obias), (8, gain1), (9, shift1), (10, qbias)):
        ref[...] = rows[k, 0:48]
    ubias[...] = jnp.concatenate([rows[r : r + 1, 0:48] for r in range(4)], 1)[0]
    lane = lax.broadcasted_iota(jnp.int32, (8, BLK), 1)
    pick = jnp.zeros((8, BLK), F32)
    for i in range(4):
        value = jnp.sum(jnp.where(lane == HD + fs * 4 + i, columns[0:8], 0.0), 1, keepdims=True)
        pick = jnp.where(lane == i, value, pick)
    vbias[...] = pick[0, 0:4]
    for load, store in zip(loads, stores):
        load.wait()
        store.start()
    for store in stores:
        store.wait()


def shards(
    tokens,
    lengths,
    block_map,
    first_gain,
    first_shift,
    query_weight,
    query_bias,
    keyval_weight,
    value_bias,
    output_weight,
    output_bias,
    second_gain,
    second_shift,
    up_weight,
    up_bias,
    down_weight,
    down_bias,
    cotangent,
):
    vmem = pl.BlockSpec(memory_space=pltpu.VMEM)
    smem = pl.BlockSpec(memory_space=pltpu.SMEM)
    hbm = pl.BlockSpec(memory_space=pl.ANY)

    def v(*shape, dtype=BF16):
        return pltpu.VMEM(shape, dtype)

    shapes = (
        jax.ShapeDtypeStruct((2, BLK, WIDTH), BF16),
        jax.ShapeDtypeStruct((2, BLK, WIDTH), F32),
        jax.ShapeDtypeStruct((48, WIDTH), F32),
        jax.ShapeDtypeStruct((48, WIDTH), F32),
        jax.ShapeDtypeStruct((48, 2 * BLK), F32),
        jax.ShapeDtypeStruct((48, FF), F32),
        jax.ShapeDtypeStruct((192, WIDTH), F32),
    )
    scratch = [
        v(2, BLK, WIDTH),
        v(2, BLK, WIDTH, dtype=F32),
        v(16, WIDTH),
    ]
    scratch += [v(*shape.shape, dtype=shape.dtype) for shape in shapes[2:]]
    scratch += [
        v(4, 2, 2, 16, WIDTH),
        v(4, 2, 2, 48, WIDTH),
        v(4, 2, 2, 48, 2 * HD),
        v(4, 2, 2, 48, WIDTH),
        v(4, 2, 2, 48, HALF),
        v(4, 2, 48, HALF),
        v(3, 2, 2, 192, WIDTH),
        v(4, 2, 2, 48, 512),
        v(4, 2, 2, 48, WIDTH),
        v(4, 2, 2, 48, 2 * BLK),
        v(4, 2, 2, 48, HALF),
        v(2, 2, 2, 192, WIDTH),
        v(4, 2, 48, 512),
        v(4, 2, 48, WIDTH),
        v(4, 48, 512),
        v(4, 48, WIDTH),
        v(2, 4, 2, 48, WIDTH),
        v(2, 2, 96, WIDTH),
        v(2, 4, 2, 48, WIDTH),
        v(4, 96, WIDTH),
        v(3, 48, 512),
        v(3, 48, WIDTH),
        v(2, 3, 2, 48, WIDTH),
        v(3, 96, WIDTH),
        v(2, 3, 48, 384),
        v(3, 48, 384),
        v(2, 2, 48, 384),
        v(2, 2, 48, 384),
        v(2, 4, 48, 384),
        v(2, 4, 48, 384),
        v(2, 3, 2, 2, 48, 384),
        v(2, 2, 2, 48, 384),
        v(2, 2, 48, 384),
        v(4, 48, 384),
        v(3, 48, 384),
        v(4, 2, 2, 48, 256),
        v(4, 2, 48, 256),
        v(4, 48, 256),
        v(3, 48, 256),
        v(4, 48, 256),
        v(2, 48, 256),
        v(4, 2, 48, 256),
        v(8, 48, 2 * BLK),
        v(4, 48, 512),
        v(4, 48, WIDTH),
        v(2, 48, 512),
        v(2, 48, WIDTH),
        v(PEERS, 48, 2 * BLK),
        v(PEERS, ROWS, 2 * HD),
        v(PEERS, ROWS, 2 * HD),
        v(PEERS, ROWS, 2 * HD),
        v(KEYS, BLK),
        v(KEYS, BLK),
        v(BLK, KEYS),
        v(BLK + 16, KEYS),
        v(GROUPS, BLK, ROWS),
        v(GROUPS, ROWS, BLK),
        v(GROUPS, KEYS, ROWS),
        v(KEYS, ROWS, dtype=F32),
        v(KEYS, ROWS, dtype=F32),
        v(GROUPS, BLK, ROWS, dtype=F32),
        v(GROUPS, 16, ROWS, dtype=F32),
        v(GROUPS, BLK, ROWS),
        v(GROUPS, BLK, ROWS),
        v(GROUPS, ROWS, BLK),
        v(ROWS, WIDTH),
        v(ROWS, WIDTH),
        v(WIDTH, ROWS),
        v(ROWS, WIDTH, dtype=F32),
        v(2, ROWS, WIDTH),
        v(WIDTH, 2 * ROWS),
        v(2, ROWS, WIDTH),
        v(2 * ROWS, HALF),
        v(2 * ROWS, HALF),
        v(ROWS, WIDTH),
        v(ROWS, WIDTH),
        v(ROWS, WIDTH, dtype=F32),
        v(ROWS, WIDTH),
        v(ROWS, WIDTH),
        pltpu.SemaphoreType.DMA((SEMS,)),
        pltpu.SemaphoreType.DMA((SEMS,)),
        pltpu.SemaphoreType.DMA((32,)),
    ]
    outs = pl.pallas_call(
        layer_kernel,
        out_shape=shapes,
        in_specs=[smem, smem, hbm, hbm] + [vmem] * 9 + [hbm] * 5,
        out_specs=(hbm,) * 7,
        scratch_shapes=scratch,
        compiler_params=pltpu.CompilerParams(
            collective_id=0, has_side_effects=True, vmem_limit_bytes=62 * 2**20
        ),
    )(
        lengths,
        block_map,
        tokens[0],
        cotangent[0],
        first_gain,
        first_shift,
        query_bias,
        value_bias,
        output_bias,
        second_gain,
        second_shift,
        up_bias,
        down_bias,
        query_weight,
        keyval_weight,
        output_weight,
        up_weight,
        down_weight,
    )

    def f(*shape):
        return jax.ShapeDtypeStruct(shape, F32)

    results = pl.pallas_call(
        finish_kernel,
        out_shape=(
            shapes[0],
            shapes[1],
            f(48),
            f(48),
            f(48, WIDTH),
            f(48),
            f(48, 2 * HD),
            f(4),
            f(48, WIDTH),
            f(48),
            f(48),
            f(48),
            f(48, FF),
            f(192),
            f(192, WIDTH),
            f(48),
        ),
        in_specs=[hbm] * 4 + [vmem] + [hbm] * 2,
        out_specs=tuple(
            hbm if i in (0, 1, 4, 8, 12, 14) else vmem for i in range(16)
        ),
        scratch_shapes=[
            pltpu.VMEM(shapes[i].shape, shapes[i].dtype) for i in (1, 5, 6, 0, 2, 3)
        ]
        + [pltpu.SemaphoreType.DMA((40,))],
    )(*outs)
    return (results[0][None], results[1][None]) + tuple(results[2:])


def solution(mesh):
    rows, matrix, batch = P("fsdp"), P("fsdp", None), P("fsdp", "ctx", None, None)
    return jax.shard_map(
        shards,
        mesh=mesh,
        in_specs=(
            batch,
            rows,
            P(),
            rows,
            rows,
            matrix,
            rows,
            matrix,
            rows,
            matrix,
            rows,
            rows,
            rows,
            matrix,
            rows,
            matrix,
            rows,
            batch,
        ),
        out_specs=(
            batch,
            batch,
            rows,
            rows,
            matrix,
            rows,
            matrix,
            rows,
            matrix,
            rows,
            rows,
            rows,
            matrix,
            rows,
            matrix,
            rows,
        ),
        check_vma=False,
    )
```

```python
import functools

import jax
import jax.numpy as jnp
from jax import lax
from jax.experimental import pallas as pl
from jax.experimental.pallas import tpu as pltpu
from jax.sharding import PartitionSpec as P

EPS = 1e-05
NEG = -1e30
MESH = pl.DeviceIdType.MESH
F32 = jnp.float32
BF16 = jnp.bfloat16

WIDTH = 768
HEADS = 12
HD = 64
FF = 3072
HALF = FF // 2
BLK = 128
ROWS = 2 * BLK
GROUPS = HEADS // 2
PEERS = 8
N_A, N_B = 8, 7
ITEMS = N_A + N_B + 2
KEYS = ITEMS * BLK
SEMS = 300


class Chain:
    def __init__(self, *steps):
        self.steps = list(steps)
        self.flying = []

    def go(self, arrived):
        arrived(self.flying)
        self.flying = self.steps.pop(0)() if self.steps else []


def dot(left, right):
    return jnp.dot(left, right, preferred_element_type=F32)


def dot_nt(left, right):
    return lax.dot_general(left, right, (((1,), (1,)), ((), ())), preferred_element_type=F32)


def normalize(values):
    centre = values - jnp.mean(values, -1, keepdims=True)
    spread = jnp.mean(centre * centre, -1, keepdims=True)
    rate = lax.rsqrt(spread + EPS)
    return centre * rate, rate


def norm_back(normed, rate, grad, gain):
    scaled = grad * gain
    first = jnp.mean(scaled, -1, keepdims=True)
    second = jnp.mean(scaled * normed, -1, keepdims=True)
    return rate * (scaled - first - normed * second)


def layer_kernel(
    lengths,
    block_map,
    tokens_in,
    cotangent_in,
    own_gain1,
    own_shift1,
    own_qbias,
    own_vbias,
    own_obias,
    own_gain2,
    own_shift2,
    own_ubias,
    own_dbias,
    wq,
    wkv,
    wo,
    wup,
    wdn,
    out_hbm,
    ing_hbm,
    gq_hbm,
    go_hbm,
    gt_hbm,
    gup_hbm,
    gdn_hbm,
    tokens,
    cotangent,
    vecs,
    gq_ref,
    go_ref,
    gt_ref,
    gup_ref,
    gdn_ref,
    f_vec,
    f_q,
    f_kv,
    f_o,
    f_up,
    r_up,
    f_dn,
    g_q,
    g_o,
    g_t,
    g_up,
    g_dn,
    rc_q,
    rc_o,
    rz_q,
    rz_o,
    rz_up,
    rz_dn,
    s_up,
    s_dn,
    ry_q,
    ry_o,
    ry_up,
    ry_dn,
    rx_up,
    rx_dn,
    rh_up,
    rh_dn,
    f2_up,
    f2_dn,
    fx,
    fg,
    fz,
    fs_dn,
    fy,
    g_r,
    rc_r,
    rz_r,
    ry_r,
    cx_r,
    ch_r,
    rc_t,
    r_t,
    cx_q,
    cx_o,
    ch_q,
    ch_o,
    c_t,
    kv_all,
    dkv_out,
    dkv_in,
    k_both,
    v_both,
    kt_both,
    vt_both,
    q_both,
    q_rows,
    probs,
    score,
    acc,
    o_norm,
    l_inv,
    att_t,
    do_both,
    do_rows,
    x_low,
    xn,
    xn_t,
    mixed_s,
    n2s,
    n2_t,
    gos,
    mid,
    dup,
    part_out,
    part_in,
    dsec_own,
    dsec_out,
    dsec_in,
    send_sem,
    recv_sem,
    local_sem,
):
    ctx = lax.axis_index("ctx")
    fs = lax.axis_index("fsdp")
    zh, xx = ctx // 4, ctx % 4
    yy, zl, co = fs // 4, (fs // 2) % 2, fs % 2
    oz, oc = 1 - zl, 1 - co

    def peer(j):
        return ((zh + j // 4) % 2) * 4 + (xx + j % 4) % 4

    def from_peer(j):
        return ((zh + j // 4) % 2) * 4 + (xx + 4 - j % 4) % 4

    def shard_peer(k):
        return ((yy + k // 4) % 4) * 4 + ((zl + (k // 2) % 2) % 2) * 2 + (co + k % 2) % 2

    sib = (ctx, fs + 1 - 2 * co)
    z_near = (ctx, fs + 2 - 4 * zl)
    z_far = (ctx + 4 - 8 * zh, fs + 2 - 4 * zl)
    z_of = (z_near, z_far)

    def y_peer(k):
        return (ctx, ((yy + k) % 4) * 4 + zl * 2 + co)

    def x_peer(k):
        return (zh * 4 + (xx + k) % 4, fs)

    h_peer = (ctx + 4 - 8 * zh, fs)
    odd = xx % 2
    x_of = ((ctx + 1 - 2 * odd, fs), (zh * 4 + 3 - xx, fs))

    count = [0]
    started = []

    def send(src, dst, to):
        i = count[0]
        count[0] += 1
        copy = pltpu.make_async_remote_copy(
            src_ref=src,
            dst_ref=dst,
            send_sem=send_sem.at[i],
            recv_sem=recv_sem.at[i],
            device_id=to,
            device_id_type=MESH,
        )
        copy.start()
        started.append(copy)
        return copy

    def arrived(copies):
        for copy in copies:
            copy.wait_recv()

    locals_ = []

    def keep(src, dst):
        i = len(locals_)
        copy = pltpu.make_async_copy(src, dst, local_sem.at[i])
        copy.start()
        locals_.append(copy)
        return copy

    got_tokens = keep(tokens_in, tokens)
    got_cotangent = keep(cotangent_in, cotangent)
    barrier = pltpu.get_barrier_semaphore()
    greeted = [(peer(j), fs) for j in (1, 2, 3, 4)]
    greeted += [(ctx, shard_peer(k)) for k in (1, 2, 4, 8, 12)] + [z_far]
    for device in greeted:
        pl.semaphore_signal(barrier, inc=1, device_id=device, device_id_type=MESH)

    def spread(values, at):
        size = values.shape[1]
        i = lax.broadcasted_iota(jnp.int32, (size, WIDTH), 0)
        lane = lax.broadcasted_iota(jnp.int32, (size, WIDTH), 1)
        return dot(values, jnp.where(lane == at + i, 1.0, 0.0).astype(BF16))

    plain = (own_gain1, own_shift1, own_qbias, own_obias, own_gain2, own_shift2, own_dbias)
    plain = [ref[...].reshape(1, 48) for ref in plain]
    up_row = spread(own_ubias[...].reshape(1, 192), (fs % 4) * 192)
    vecs[...] = jnp.concatenate(
        [spread(value, fs * 48) for value in plain]
        + [spread(own_vbias[...].reshape(1, 4), HD + fs * 4)]
        + [jnp.where(fs // 4 == r, up_row, 0.0) for r in range(4)]
        + [jnp.zeros((4, WIDTH), F32)],
        0,
    ).astype(BF16)

    slot0, slot1 = block_map[2 * ctx], block_map[2 * ctx + 1]
    low = jnp.minimum(slot0, slot1)
    swap = slot0 > slot1
    length = lengths[0]

    got_tokens.wait()
    t0, t1 = tokens[0], tokens[1]
    x_low[0:BLK] = jnp.where(swap, t1, t0)
    x_low[BLK:ROWS] = jnp.where(swap, t0, t1)

    row = lax.broadcasted_iota(jnp.int32, (ROWS, 1), 0)
    pos = jnp.where(row < BLK, low * BLK, (14 - low) * BLK) + row
    valid = (pos < length).astype(F32)

    def grad_out():
        c0, c1 = cotangent[0], cotangent[1]
        both = jnp.concatenate([jnp.where(swap, c1, c0), jnp.where(swap, c0, c1)], 0)
        return valid * both

    got_cotangent.wait()
    gos[0] = grad_out().astype(BF16)

    n1, _ = normalize(x_low[...].astype(F32))
    pl.semaphore_wait(barrier, len(greeted))

    def thirds_of(start, width):
        return (
            pl.ds(pl.multiple_of(start + odd * width, BLK), 2 * width),
            pl.ds(pl.multiple_of(start + odd * 2 * width, BLK), width),
            pl.ds(pl.multiple_of(start + (1 - odd) * 2 * width, BLK), width),
        )

    every = slice(None)

    class Whole:
        def __init__(self, src, full, cols=None, rows=every, dst=None, src_at=0):
            self.src, self.full, self.rows = src, full, rows
            self.dst = full if dst is None else dst
            self.fetch, self.own, self.other = (every,) * 3 if cols is None else thirds_of(*cols)
            self.src_cols = self.fetch
            if cols is not None:
                self.src_cols = pl.ds(
                    pl.multiple_of(src_at + cols[0] + odd * cols[1], BLK), 2 * cols[1]
                )

        def at(self, y, z, cols):
            return self.full.at[y, z, co, self.rows, cols]

        def y(self):
            src, dst = self.src.at[self.rows, self.src_cols], self.at(yy, zl, self.fetch)
            self.kept = keep(src, dst)
            return [send(src, dst, y_peer(k)) for k in (1, 2, 3)]

        def z(self):
            self.kept.wait()
            refs = [self.at(pl.ds(2 * e, 2), zl, self.fetch) for e in (0, 1)]
            return [send(ref, ref, z_of[e]) for e, ref in enumerate(refs)]

        def x(self):
            refs = [self.at(pl.ds(2 * e, 2), every, self.own) for e in (0, 1)]
            return [send(ref, ref, x_of[e]) for e, ref in enumerate(refs)]

        def c(self, cols, z=every):
            ref = self.at(every, z, cols)
            return [send(ref, self.dst.at[every, z, co, self.rows, cols], sib)]

    class Part(Whole):
        def at(self, y, z, cols):
            return self.full.at[y, z, self.rows, cols]

    class Mine(Whole):
        def c(self, cols, z=every):
            return []

    class Units(Whole):
        def at(self, e, z, cols, y=every):
            other = e + co - 2 * e * co
            lead = (1 - other) * co + 2 * other
            return self.full.at[lead, y, z, self.rows, cols]

        def y(self):
            src, dst = self.src.at[self.rows, self.src_cols], self.at(yy // 2, zl, self.fetch, yy % 2)
            self.kept = keep(src, dst)
            return [send(src, dst, y_peer(k)) for k in (1, 2, 3)]

        def z(self):
            self.kept.wait()
            refs = [self.at(e, zl, self.fetch) for e in (0, 1)]
            return [send(ref, ref, z_of[e]) for e, ref in enumerate(refs)]

        def x(self):
            refs = [self.at(e, every, self.own) for e in (0, 1)]
            return [send(ref, ref, x_of[e]) for e, ref in enumerate(refs)]

        def c(self, cols, z=every):
            ref = self.full.at[2, every, z, self.rows, cols]
            return [send(ref, self.full.at[co, every, z, self.rows, cols], sib)]

    def each(arrays, action):
        return [copy for array in arrays for copy in action(array)]

    def narrow(*arrays):
        first = []

        def after_y():
            out = each(arrays, lambda a: a.z())
            first.extend(each(arrays, lambda a: a.c(every, zl)))
            return out

        return Chain(
            lambda: each(arrays, lambda a: a.y()),
            after_y,
            lambda: each(arrays, lambda a: a.c(every, oz)) + first,
        )

    def wide(*arrays):
        first = []

        def after_z():
            out = each(arrays, lambda a: a.x())
            first.extend(each(arrays, lambda a: a.c(a.fetch)))
            return out

        return Chain(
            lambda: each(arrays, lambda a: a.y()),
            lambda: each(arrays, lambda a: a.z()),
            after_z,
            lambda: each(arrays, lambda a: a.c(a.other)) + first,
        )

    def step(*chains):
        for chain in chains:
            chain.go(arrived)

    def up_chunk(j):
        cols = (j * WIDTH, WIDTH // 3)
        return wide(
            Mine(wup, f_up, cols, src_at=co * HALF),
            Part(wup, r_up, cols, dst=f_up, src_at=oc * HALF),
        )

    kvv = narrow(Whole(vecs, f_vec), Whole(wkv, f_kv))
    wq_in, wo_in = narrow(Whole(wq, f_q)), wide(Whole(wo, f_o, (0, 256)))
    dn_a, dn_b = (wide(Units(wdn, f_dn, (0, 256), pl.ds(96 * i, 96))) for i in (0, 1))
    up_a, up_b = up_chunk(0), up_chunk(1)

    step(kvv, wq_in, wo_in, dn_a, dn_b, up_a, up_b)
    step(kvv)
    step(wq_in, kvv)
    step(kvv)
    vec = f_vec[...].astype(F32).reshape(16, 16, WIDTH)
    vec = jnp.sum(vec, 0)
    gain1, shift1, qbias, obias = vec[0:1], vec[1:2], vec[2:3], vec[3:4]
    gain2, shift2, dbias, kvbias = vec[4:5], vec[5:6], vec[6:7], vec[7:8, 0 : 2 * HD]

    xn_v = n1 * gain1 + shift1
    xn[...] = xn_v.astype(BF16)

    kv = dot(xn[...], f_kv[...].reshape(WIDTH, 2 * HD)) + kvbias
    kv_all[0] = kv.astype(BF16)
    kv_copies = [send(kv_all.at[0], kv_all.at[j], (peer(j), fs)) for j in (1, 2, 3)]
    kv_far = send(kv_all.at[0], kv_all.at[4], h_peer)
    xn_t[...] = xn[...].astype(F32).T.astype(BF16)
    step(wo_in, wq_in)
    arrived([kv_far])
    kv_copies += [send(kv_all.at[4], kv_all.at[4 + j], (peer(j), fs)) for j in (1, 2, 3)]
    step(wq_in)

    q = dot(xn[...], f_q[...].reshape(WIDTH, WIDTH)) + qbias
    q = (q.astype(BF16).astype(F32) * (HD**-0.5)).T
    for g in range(GROUPS):
        h0, h1 = q[g * BLK : g * BLK + HD], q[g * BLK + HD : (g + 1) * BLK]
        both = jnp.concatenate(
            [
                jnp.concatenate([h0[:, BLK:], h1[:, BLK:]], 1),
                jnp.concatenate([h0[:, :BLK], h1[:, :BLK]], 1),
            ],
            0,
        )
        q_both[g] = both.astype(BF16)
        q_rows[g] = both.T.astype(BF16)

    step(dn_a, wo_in)
    go_copy = send(gos.at[0], gos.at[1], sib)

    arrived(kv_copies)
    step(dn_b)
    lane = lax.broadcasted_iota(jnp.int32, (BLK, BLK), 1)
    sub = lax.broadcasted_iota(jnp.int32, (BLK, BLK), 0)
    extra = lax.broadcasted_iota(jnp.int32, (16, BLK), 0)

    picks, limits = [], []
    for j in range(1, PEERS):
        c = from_peer(j)
        other = jnp.minimum(block_map[2 * c], block_map[2 * c + 1])
        high = other > low
        picks.append(jnp.where(high, 1.0, 0.0).astype(F32))
        limits.append(length - jnp.where(high, 15 - other, other) * BLK)

    def place(item, block, to_high):
        rows = pl.ds(item * BLK, BLK)
        left = jnp.where(lane < HD, to_high, 1.0 - to_high)
        kk = jnp.concatenate([block[:, :HD], block[:, :HD]], 1) * left
        vv = jnp.concatenate([block[:, HD:], block[:, HD:]], 1) * left
        k_both[rows] = kk.astype(BF16)
        v_both[rows] = vv.astype(BF16)
        kt_both[:, rows] = kk.T.astype(BF16)
        vt_both[0:BLK, rows] = vv.T.astype(BF16)
        vt_both[BLK : BLK + 16, rows] = jnp.where(extra < 8, to_high, 1.0 - to_high).astype(BF16)

    one, zero = jnp.float32(1.0), jnp.float32(0.0)
    for j in range(PEERS):
        block = kv_all[j].astype(F32)
        place(j, block[:BLK], one)
        if j:
            pick = picks[j - 1]
            place(N_A + j - 1, jnp.where(pick > 0.5, block[BLK:], block[:BLK]), pick)
        else:
            place(N_A + N_B, block[BLK:], one)
            place(N_A + N_B + 1, block[:BLK], zero)

    sub2 = lax.broadcasted_iota(jnp.int32, (BLK, ROWS), 0)
    lane2 = lax.broadcasted_iota(jnp.int32, (BLK, ROWS), 1) % BLK

    def fold(values, op):
        return op(values.reshape(BLK // 8, 8, ROWS), 0)

    def forward_group(g, carry):
        score[...] = dot(k_both[...], q_both[g])
        top_h = jnp.full((8, ROWS), NEG, F32)
        top_l = jnp.full((8, ROWS), NEG, F32)
        for item in range(ITEMS):
            rows = slice(item * BLK, (item + 1) * BLK)
            s = score[rows]
            if item < N_A:
                top_h = jnp.maximum(top_h, fold(s, jnp.max))
            elif item < N_A + N_B:
                j = item - N_A
                s = jnp.where(sub2 < limits[j], s, NEG)
                score[rows] = s
                best = fold(s, jnp.max)
                top_h = jnp.maximum(top_h, jnp.where(picks[j] > 0.5, best, NEG))
                top_l = jnp.maximum(top_l, jnp.where(picks[j] > 0.5, NEG, best))
            elif item == N_A + N_B:
                limit = length - (15 - low) * BLK
                s = jnp.where((sub2 <= lane2) & (sub2 < limit), s, NEG)
                score[rows] = s
                top_h = jnp.maximum(top_h, fold(s, jnp.max))
            else:
                s = jnp.where(sub2 <= lane2, s, NEG)
                score[rows] = s
                top_l = jnp.maximum(top_l, fold(s, jnp.max))
        top_h = jnp.max(top_h, 0, keepdims=True)
        top_l = jnp.max(top_l, 0, keepdims=True)
        for item in range(ITEMS):
            rows = slice(item * BLK, (item + 1) * BLK)
            if item < N_A or item == N_A + N_B:
                top = top_h
            elif item < N_A + N_B:
                top = jnp.where(picks[item - N_A] > 0.5, top_h, top_l)
            else:
                top = top_l
            probs[g, rows] = jnp.exp(score[rows] - top).astype(BF16)
        o = dot(vt_both[...], probs[g])
        inv_h = 1.0 / o[BLK : BLK + 1]
        inv_l = 1.0 / o[BLK + 8 : BLK + 9]
        high, lower = o[0:HD] * inv_h, o[HD:BLK] * inv_l
        o_norm[g, 0:HD] = high
        o_norm[g, HD:BLK] = lower
        l_inv[g, 0:8] = jnp.broadcast_to(inv_h, (8, ROWS))
        l_inv[g, 8:16] = jnp.broadcast_to(inv_l, (8, ROWS))
        att_t[g, 0:HD, 0:BLK] = lower[:, :BLK].astype(BF16)
        att_t[g, 0:HD, BLK:ROWS] = high[:, :BLK].astype(BF16)
        att_t[g, HD:BLK, 0:BLK] = lower[:, BLK:].astype(BF16)
        att_t[g, HD:BLK, BLK:ROWS] = high[:, BLK:].astype(BF16)
        return carry

    step(dn_a)
    lax.fori_loop(0, 2, forward_group, 0)
    step(up_a)
    lax.fori_loop(2, 4, forward_group, 0)
    step(dn_b, wo_in)
    lax.fori_loop(4, 6, forward_group, 0)
    step(up_b, wo_in)
    attended = att_t[...].reshape(WIDTH, ROWS).astype(F32).T.astype(BF16)
    mixed = x_low[...].astype(F32) + dot(attended, f_o[...].reshape(WIDTH, WIDTH)) + obias
    mixed_s[...] = mixed
    n2, _ = normalize(mixed)
    n2s[0] = (n2 * gain2 + shift2).astype(BF16)
    n2_copy = send(n2s.at[0], n2s.at[1], sib)

    step(up_a, dn_a, dn_b, up_a, up_b)
    arrived([go_copy, n2_copy])

    def unit_rows(j, start, size):
        blocks = []
        while size:
            k, r = start // 192, start % 192
            n = min(size, 192 - r)
            blocks.append(f_dn[k % 2, j, k // 2, r : r + n])
            start, size = start + n, size - n
        return jnp.concatenate(blocks, 0)

    coef = 0.7978845608028654

    def low_sum(own, *others):
        total = own.astype(F32)
        for other in others:
            total = total + other.astype(F32)
        return total.astype(BF16)

    def corner(half, k):
        rows = pl.ds(pl.multiple_of(96 * half + (k // 2) * 48, 16), 48)
        return rows, pl.ds(pl.multiple_of((k % 2) * 384, BLK), 384)

    class DownNear:
        def z(self, j):
            rows = [slice(48 * e, 48 * (e + 1)) for e in (0, 1)]
            return [
                send(g_dn.at[j, oz, :, r], rz_dn.at[j, :, r], z_of[e]) for e, r in enumerate(rows)
            ]

        def c(self):
            for j in (0, 1):
                g_dn[j, zl, :, 0:96] = low_sum(g_dn[j, zl, :, 0:96], rz_dn[j])
                s_dn[2 * co + j] = g_dn[j, zl, co, 0:96]
            return [send(g_dn.at[:, zl, oc, 0:96], s_dn.at[pl.ds(2 * co, 2)], sib)]

        def y(self):
            return [send(s_dn.at[(yy + k) % 4], ry_dn.at[k - 1], y_peer(k)) for k in (1, 2, 3)]

        def x(self):
            s_dn[yy] = low_sum(s_dn[yy], *[ry_dn[k] for k in range(3)])
            return [
                send(s_dn.at[(yy,) + corner(0, (xx + k) % 4)], rx_dn.at[k - 1], x_peer(k))
                for k in (1, 2, 3)
            ]

        def h(self):
            rh_dn[0, 1] = low_sum(s_dn[(yy,) + corner(0, xx)], *[rx_dn[k] for k in range(3)])
            return [send(rh_dn.at[0, 1], rh_dn.at[0, 0], h_peer)]

        def a(self, i=0):
            f2_dn[i, xx] = low_sum(rh_dn[i, 0], rh_dn[i, 1])
            return [send(f2_dn.at[i, xx], f2_dn.at[i, xx], x_peer(k)) for k in (1, 2, 3)]

    class DownFar:
        def x(self, j):
            return [
                send(g_dn.at[(j, every, every) + corner(1, (xx + k) % 4)], fx.at[j, k - 1], x_peer(k))
                for k in (1, 2, 3)
            ]

        def z(self):
            for j in (0, 1):
                own = g_dn[(j, every, every) + corner(1, xx)]
                fg[j] = low_sum(own, *[fx[j, k] for k in range(3)])
            return [send(fg.at[j, oz], fz.at[j], z_of[j]) for j in (0, 1)]

        def c(self):
            for j in (0, 1):
                fg[j, zl] = low_sum(fg[j, zl], fz[j])
                fs_dn[2 * co + j] = fg[j, zl, co]
            return [send(fg.at[:, zl, oc], fs_dn.at[pl.ds(2 * co, 2)], sib)]

        def y(self):
            return [send(fs_dn.at[(yy + k) % 4], fy.at[k - 1], y_peer(k)) for k in (1, 2, 3)]

        def h(self):
            rh_dn[1, 1] = low_sum(fs_dn[yy], *[fy[k] for k in range(3)])
            return [send(rh_dn.at[1, 1], rh_dn.at[1, 0], h_peer)]

    class Up:
        def __init__(self, j, start, width):
            self.j, self.start, self.half = j, start, width // 2
            self.cols = slice(start, start + width)
            self.from_cols = slice(j * WIDTH + start, j * WIDTH + start + width)
            self.quarter_cols = slice(start // 2, start // 2 + width // 2)

        def quarter(self, k):
            start = pl.multiple_of(self.start + (k % 2) * self.half, BLK)
            return k // 2, every, pl.ds(start, self.half)

        def z(self):
            return [
                send(
                    g_up.at[pl.ds(2 * e, 2), oz, :, :, self.from_cols],
                    rz_up.at[self.j, pl.ds(2 * e, 2), :, :, self.cols],
                    z_of[e],
                )
                for e in (0, 1)
            ]

        def c(self):
            src, cols, j = self.from_cols, self.cols, self.j
            g_up[:, zl, :, :, src] = low_sum(g_up[:, zl, :, :, src], rz_up[j, :, :, :, cols])
            s_up[j, :, co, :, cols] = g_up[:, zl, co, :, src]
            return [send(g_up.at[:, zl, oc, :, src], s_up.at[j, :, co, :, cols], sib)]

        def y(self):
            j, cols = self.j, self.cols
            return [
                send(s_up.at[j, (yy + k) % 4, :, :, cols], ry_up.at[j, k - 1, :, :, cols], y_peer(k))
                for k in (1, 2, 3)
            ]

        def x(self):
            j, cols, part = self.j, self.cols, self.quarter_cols
            s_up[j, yy, :, :, cols] = low_sum(
                s_up[j, yy, :, :, cols], *[ry_up[j, k, :, :, cols] for k in range(3)]
            )
            return [
                send(
                    s_up.at[(j, yy) + self.quarter((xx + k) % 4)],
                    rx_up.at[j, k - 1, :, part],
                    x_peer(k),
                )
                for k in (1, 2, 3)
            ]

        def h(self):
            j, part = self.j, self.quarter_cols
            got = [rx_up[j, k, :, part] for k in range(3)]
            rh_up[j, 1, :, part] = low_sum(s_up[(j, yy) + self.quarter(xx)], *got)
            return [send(rh_up.at[j, 1, :, part], rh_up.at[j, 0, :, part], h_peer)]

        def a(self):
            j, part = self.j, self.quarter_cols
            f2_up[j, xx, :, part] = low_sum(rh_up[j, 0, :, part], rh_up[j, 1, :, part])
            ref = f2_up.at[j, xx, :, part]
            return [send(ref, ref, x_peer(k)) for k in (1, 2, 3)]

    near, far = DownNear(), DownFar()
    dn_near = Chain(near.c, near.y, near.x, near.h, near.a)
    dn_far = Chain(far.z, far.c, far.y, far.h, functools.partial(near.a, 1))
    ups = [
        [Chain(u.z, u.c, u.y, u.x, u.h, u.a) for u in (Up(j, 0, 512), Up(j, 512, 256))] for j in (0, 1)
    ]

    def square(grad, rc, rz, ry, cx, ch):
        def c():
            return [send(grad.at[:, :, oc], rc, sib)]

        def z():
            grad[:, :, co] = low_sum(grad[:, :, co], rc[...])
            return [
                send(grad.at[pl.ds(2 * e, 2), oz, co], rz.at[pl.ds(2 * e, 2)], z_of[e])
                for e in (0, 1)
            ]

        def y():
            grad[:, zl, co] = low_sum(grad[:, zl, co], rz[...])
            return [
                send(grad.at[(yy + k) % 4, zl, co], ry.at[k - 1], y_peer(k)) for k in (1, 2, 3)
            ]

        def x():
            cx[0] = low_sum(grad[yy, zl, co], *[ry[k] for k in range(3)])
            return [send(cx.at[0], cx.at[k], x_peer(k)) for k in (1, 2, 3)]

        def h():
            ch[0] = low_sum(cx[0], *[cx[k] for k in (1, 2, 3)])
            return [send(ch.at[0], ch.at[1], h_peer)]

        return Chain(c, z, y, x, h)

    def direct(grad, rc, got, shares):
        def c():
            return [send(grad.at[:, :, oc], rc, sib)]

        def group():
            grad[:, :, co] = low_sum(grad[:, :, co], rc[...])
            out = []
            for k in range(1, 8):
                dst = shard_peer(2 * k)
                out.append(send(grad.at[dst // 4, (dst // 2) % 2, co], got.at[k], (ctx, dst)))
            return out

        def peers():
            shares[0] = low_sum(grad[yy, zl, co], *[got[k] for k in range(1, 8)])
            return [send(shares.at[0], shares.at[j], (peer(j), fs)) for j in range(1, PEERS)]

        return Chain(c, group, peers)

    def total_of(shares, n):
        total = shares[0].astype(F32)
        for j in range(1, n):
            total = total + shares[j].astype(F32)
        return total

    out_w = square(g_o, rc_o, rz_o, ry_o, cx_o, ch_o)
    query_a = square(g_q, rc_q, rz_q, ry_q, cx_q, ch_q)
    query_b = square(g_r, rc_r, rz_r, ry_r, cx_r, ch_r)
    tail = direct(g_t, rc_t, r_t, c_t)

    thirds = [slice(256 * n, 256 * (n + 1)) for n in range(3)]
    n2_t[...] = n2s[...].reshape(2 * ROWS, WIDTH).astype(F32).T.astype(BF16)
    up_sums = []

    def middle(j):
        for n in thirds:
            cols = slice(j * WIDTH + n.start, j * WIDTH + n.stop)
            bias = jnp.where(co == 0, vec[8 + j : 9 + j, n], vec[10 + j : 11 + j, n])
            n2b = n2s[...].reshape(2 * ROWS, WIDTH)
            gob = gos[...].reshape(2 * ROWS, WIDTH)
            up = dot(n2b, f_up[:, :, :, :, cols].reshape(WIDTH, 256)) + bias
            dmid = dot_nt(gob, unit_rows(j, n.start, 256))
            square = up * up
            th = jnp.tanh(coef * up * (1.0 + 0.044715 * square))
            half_sum = 0.5 + 0.5 * th
            mid[:, cols] = (up * half_sum).astype(BF16)
            slope = half_sum + 0.5 * up * (1.0 - th * th) * coef * (1.0 + 3 * 0.044715 * square)
            du = (dmid * slope).astype(BF16)
            dup[:, cols] = du
            up_sums.append(jnp.sum(du.astype(F32), 0, keepdims=True))

    def weight_grads(j):
        m_t = mid[:, j * WIDTH : (j + 1) * WIDTH].astype(F32).T.astype(BF16)
        for n in thirds:
            piece = dot(m_t, gos[:, :, n].reshape(2 * ROWS, 256))
            g_dn[j, :, :, :, n] = piece.astype(BF16).reshape(2, 2, 192, 256)
        dn_near.flying += near.z(j)
        dn_far.flying += far.x(j)
        for n in thirds:
            cols = slice(j * WIDTH + n.start, j * WIDTH + n.stop)
            piece = dot(n2_t[...], dup[:, cols])
            g_up[:, :, :, :, cols] = piece.astype(BF16).reshape(4, 2, 2, 48, 256)
            if n.stop == 512:
                step(ups[j][0])
        step(ups[j][1])

    step(dn_a, dn_b, up_a)
    middle(0)
    step(up_b)
    weight_grads(0)
    step(up_b)
    middle(1)
    for n in thirds:
        w = f_up[...].reshape(WIDTH, HALF)[n]
        piece = dot_nt(dup[...], w)
        dsec_own[:, n] = piece[:ROWS]
        dsec_out[:, n] = piece[ROWS:].astype(BF16)
    dsec_copy = send(dsec_out, dsec_in, sib)
    weight_grads(1)

    arrived([dsec_copy])
    dsec = dsec_own[...] + dsec_in[...].astype(F32)
    n2, rate2 = normalize(mixed_s[...])
    sum_gain2 = jnp.sum(dsec * n2, 0, keepdims=True)
    sum_shift2 = jnp.sum(dsec, 0, keepdims=True)
    dmix = grad_out() + norm_back(n2, rate2, dsec, gain2)
    cotangent[0] = dmix[:BLK]
    cotangent[1] = dmix[BLK:]
    dmix_low = dmix.astype(BF16)
    dmix_r = dmix_low.astype(F32)
    sum_obias = jnp.sum(dmix_r, 0, keepdims=True)
    sum_dbias = jnp.sum(gos[0].astype(F32), 0, keepdims=True)

    g_o[...] = (
        dot(att_t[...].reshape(WIDTH, ROWS), dmix_low).astype(BF16).reshape(4, 2, 2, 48, WIDTH)
    )
    step(out_w)

    datt = dot(f_o[...].reshape(WIDTH, WIDTH), dmix_r.T.astype(BF16)).astype(BF16).astype(F32)
    deltas = []
    for g in range(GROUPS):
        h0, h1 = datt[g * BLK : g * BLK + HD], datt[g * BLK + HD : (g + 1) * BLK]
        high = jnp.concatenate([h0[:, BLK:], h1[:, BLK:]], 1) * l_inv[g, 0:1]
        lower = jnp.concatenate([h0[:, :BLK], h1[:, :BLK]], 1) * l_inv[g, 8:9]
        both = jnp.concatenate([high, lower], 0)
        do_both[g] = both.astype(BF16)
        do_rows[g] = both.T.astype(BF16)
        both = both.astype(BF16).astype(F32) * o_norm[g]
        l_inv[g, 0:8] = jnp.broadcast_to(jnp.sum(both[:HD], 0, keepdims=True), (8, ROWS))
        l_inv[g, 8:16] = jnp.broadcast_to(jnp.sum(both[HD:], 0, keepdims=True), (8, ROWS))

    acc[...] = jnp.zeros_like(acc)

    def backward_group(g, carry, query=True):
        acc[:, BLK:ROWS] += dot(probs[g], do_rows[g])
        delta_h, delta_l = l_inv[g, 0:1], l_inv[g, 8:9]
        score[...] = dot(v_both[...], do_both[g])
        for item in range(ITEMS):
            rows = slice(item * BLK, (item + 1) * BLK)
            if item < N_A or item == N_A + N_B:
                delta = delta_h
            elif item < N_A + N_B:
                delta = jnp.where(picks[item - N_A] > 0.5, delta_h, delta_l)
            else:
                delta = delta_l
            probs[g, rows] = (probs[g, rows].astype(F32) * (score[rows] - delta)).astype(BF16)
        acc[:, 0:BLK] += dot(probs[g], q_rows[g])
        if query:
            query_grad(g)
        return carry

    def query_grad(g):
        dq = dot(kt_both[...], probs[g]) * (HD**-0.5)
        do_both[g, 0:HD, 0:BLK] = dq[HD:, :BLK].astype(BF16)
        do_both[g, 0:HD, BLK:ROWS] = dq[:HD, :BLK].astype(BF16)
        do_both[g, HD:BLK, 0:BLK] = dq[HD:, BLK:].astype(BF16)
        do_both[g, HD:BLK, BLK:ROWS] = dq[:HD, BLK:].astype(BF16)

    lax.fori_loop(0, 2, backward_group, 0)
    step(ups[0][0], ups[0][1], ups[0][0], out_w)
    lax.fori_loop(2, 4, backward_group, 0)
    dq_a = do_both[0:4].reshape(512, ROWS).astype(F32).T
    sum_qa = jnp.sum(dq_a, 0, keepdims=True)
    dq_a = dq_a.astype(BF16)
    g_q[...] = dot(xn_t[...], dq_a).astype(BF16).reshape(4, 2, 2, 48, 512)
    step(dn_far, dn_near, ups[0][1], query_a)
    lax.fori_loop(4, 6, functools.partial(backward_group, query=False), 0)

    def halves(item, second):
        rows = slice(item * BLK, (item + 1) * BLK)
        at = HD if second else 0
        return jnp.concatenate(
            [acc[rows, at : at + HD], acc[rows, BLK + at : BLK + at + HD]], 1
        )

    dkv_copies = []
    for j in range(1, PEERS):
        item = N_A + j - 1
        pick = picks[j - 1]
        other = jnp.where(pick > 0.5, halves(item, False), halves(item, True))
        dkv_out[j, 0:BLK] = (halves(j, False) + (1.0 - pick) * other).astype(BF16)
        dkv_out[j, BLK:ROWS] = (pick * other).astype(BF16)
        dkv_copies.append(send(dkv_out.at[j], dkv_in.at[j], (from_peer(j), fs)))

    query_grad(4)
    query_grad(5)
    dq_b = do_both[4:6].reshape(256, ROWS).astype(F32).T
    sum_qbias = jnp.concatenate([sum_qa, jnp.sum(dq_b, 0, keepdims=True)], 1)
    dq_b = dq_b.astype(BF16)
    g_r[...] = dot(xn_t[...], dq_b).astype(BF16).reshape(4, 2, 2, 48, 256)
    step(query_b)
    step(dn_near, ups[1][0], query_a, dn_far)
    for n in thirds:
        blocks = [f_dn[c, j, z, :, n] for j in (0, 1) for z in (0, 1) for c in (0, 1)]
        piece = dot(mid[...], jnp.concatenate(blocks, 0))
        dsec_own[:, n] = piece[:ROWS]
        part_out[:, n] = piece[ROWS:].astype(BF16)
    part_copy = send(part_out, part_in, sib)

    dfirst = dot_nt(dq_a, f_q[:, :, :, :, 0:512].reshape(WIDTH, 512))
    dfirst = dfirst + dot_nt(dq_b, f_q[:, :, :, :, 512:WIDTH].reshape(WIDTH, 256))

    zeros = jnp.zeros((1, WIDTH), F32)
    g_t[:, :, :, :, BLK:ROWS] = (
        jnp.concatenate(
            [zeros] * 4
            + [sum_dbias, sum_gain2, sum_shift2, sum_obias, zeros, zeros, sum_qbias]
            + [jnp.zeros((BLK - 11, WIDTH), F32)],
            0,
        )
        .T.astype(BF16)
        .reshape(4, 2, 2, 48, BLK)
    )
    lanes = lax.broadcasted_iota(jnp.int32, (48, BLK), 1)
    for j in (0, 1):
        sums = jnp.concatenate(up_sums[3 * j : 3 * j + 3], 1)
        sums = jnp.broadcast_to(sums, (BLK, WIDTH)).T
        for k in range(4):
            block = g_t[2 * co + j, k // 2, k % 2, :, BLK:ROWS].astype(F32)
            for r in range(4):
                at = k * 192 + r * 48
                block = jnp.where(lanes == r, sums[at : at + 48], block)
            g_t[2 * co + j, k // 2, k % 2, :, BLK:ROWS] = block.astype(BF16)

    step(ups[1][1], ups[0][0], ups[1][0], dn_far, query_b, out_w)

    top = halves(0, False) + halves(N_A + N_B + 1, True)
    dkv = jnp.concatenate([top, halves(N_A + N_B, False)], 0)
    arrived(dkv_copies)
    for j in range(1, PEERS):
        dkv = dkv + dkv_in[j].astype(F32)
    dkv = dkv.astype(BF16)
    sum_kv = jnp.sum(dkv.astype(F32), 0, keepdims=True)
    g_kv = dot(xn_t[...], dkv)
    dfirst = dfirst + dot_nt(dkv, f_kv[...].reshape(WIDTH, 2 * HD))

    n1, rate1 = normalize(x_low[...].astype(F32))
    sum_gain1 = jnp.sum(dfirst * n1, 0, keepdims=True)
    sum_shift1 = jnp.sum(dfirst, 0, keepdims=True)

    columns = jnp.concatenate(
        [zeros] * 8 + [sum_gain1, sum_shift1] + [jnp.zeros((BLK - 10, WIDTH), F32)], 0
    ).T
    lanes = lax.broadcasted_iota(jnp.int32, (WIDTH, BLK), 1)
    known = g_t[:, :, :, :, BLK:ROWS].reshape(WIDTH, BLK).astype(F32)
    columns = jnp.where((lanes == 8) | (lanes == 9), columns, known)
    columns = jnp.where(lanes < HD, columns, sum_kv)
    g_t[:, :, :, :, 0:BLK] = g_kv.astype(BF16).reshape(4, 2, 2, 48, BLK)
    g_t[:, :, :, :, BLK:ROWS] = columns.astype(BF16).reshape(4, 2, 2, 48, BLK)
    step(tail)

    ing = cotangent[...].reshape(ROWS, WIDTH) + norm_back(n1, rate1, dfirst, gain1)
    cotangent[0] = jnp.where(swap, ing[BLK:], ing[:BLK])
    cotangent[1] = jnp.where(swap, ing[:BLK], ing[BLK:])
    done = [keep(cotangent, ing_hbm)]
    arrived([part_copy])
    res = valid * (mixed_s[...] + dsec_own[...] + part_in[...].astype(F32) + dbias)
    tokens[0] = jnp.where(swap, res[BLK:], res[:BLK]).astype(BF16)
    tokens[1] = jnp.where(swap, res[:BLK], res[BLK:]).astype(BF16)
    done.append(keep(tokens, out_hbm))

    step(ups[0][1], ups[1][1], dn_near, ups[0][0], query_a)
    step(tail, dn_far, ups[0][1], ups[1][0], query_b, out_w, ups[0][0], dn_near, ups[1][1], query_a)
    step(tail)
    step(dn_far, ups[0][1], ups[1][0], dn_near, query_b, out_w, ups[1][1], query_a)
    step(ups[1][0], query_b, ups[1][1])
    step(out_w)
    go_ref[...] = total_of(ch_o, 2)
    done.append(keep(go_ref, go_hbm))
    step(ups[1][0], ups[1][1], query_a)
    step(query_b)
    gq_ref[:, 0:512] = total_of(ch_q, 2)
    gq_ref[:, 512:WIDTH] = total_of(ch_r, 2)
    done.append(keep(gq_ref, gq_hbm))
    step(dn_far, dn_near)
    for half in (0, 1):
        for k in range(4):
            at, to = 96 * half + (k // 2) * 48, (k % 2) * 384
            gdn_ref[at : at + 48, to : to + 384] = f2_dn[half, k].astype(F32)
    done.append(keep(gdn_ref, gdn_hbm))
    step(ups[0][0], ups[0][1], ups[1][0], ups[1][1])
    for j in (0, 1):
        for k in range(4):
            for start, width in ((0, 256), (512, 128)):
                at = (k // 2) * HALF + j * WIDTH + start + (k % 2) * width
                got = f2_up[j, k, :, start // 2 : start // 2 + width]
                gup_ref[:, at : at + width] = got.astype(F32)
    done.append(keep(gup_ref, gup_hbm))
    step(tail)
    gt_ref[...] = total_of(c_t, PEERS)
    done.append(keep(gt_ref, gt_hbm))
    gathers = (kvv, wq_in, wo_in, dn_a, dn_b, up_a, up_b)
    for chain in gathers + (out_w, query_a, query_b, tail, dn_near, dn_far, *ups[0], *ups[1]):
        assert not chain.steps and not chain.flying
    for copy in done:
        copy.wait()

    for copy in started:
        copy.wait_send()


def finish_kernel(
    out_in,
    ing_in,
    gq_in,
    go_in,
    gt_in,
    gup_in,
    gdn_in,
    out,
    ing,
    gain1,
    shift1,
    gq,
    qbias,
    gkv,
    vbias,
    go,
    obias,
    gain2,
    shift2,
    gup,
    ubias,
    gdn,
    dbias,
    stage0,
    stage1,
    stage2,
    stage3,
    stage4,
    stage5,
    sems,
):
    stages = (stage0, stage1, stage2, stage3, stage4, stage5)
    pairs = ((ing_in, ing), (gup_in, gup), (gdn_in, gdn), (out_in, out), (gq_in, gq), (go_in, go))
    loads, stores = [], []
    for (src, dst), stage in zip(pairs, stages):
        if len(src.shape) == 3:
            parts = [(i, pl.ds(64 * k, 64)) for i in (0, 1) for k in (0, 1)]
        else:
            size = src.shape[0] // 3
            parts = [(pl.ds(size * k, size),) for k in range(3)]
        for part in parts:
            i = len(loads)
            loads.append(pltpu.make_async_copy(src.at[part], stage.at[part], sems.at[i]))
            stores.append(pltpu.make_async_copy(stage.at[part], dst.at[part], sems.at[20 + i]))
            loads[i].start()
    fs = lax.axis_index("fsdp")
    gkv[...] = gt_in[:, 0:BLK]
    columns = gt_in[:, BLK : 2 * BLK]
    rows = jnp.concatenate([columns, jnp.zeros((BLK - 48, BLK), F32)], 0).T
    for k, ref in ((4, dbias), (5, gain2), (6, shift2), (7, obias), (8, gain1), (9, shift1), (10, qbias)):
        ref[...] = rows[k, 0:48]
    ubias[...] = jnp.concatenate([rows[r : r + 1, 0:48] for r in range(4)], 1)[0]
    lane = lax.broadcasted_iota(jnp.int32, (8, BLK), 1)
    pick = jnp.zeros((8, BLK), F32)
    for i in range(4):
        value = jnp.sum(jnp.where(lane == HD + fs * 4 + i, columns[0:8], 0.0), 1, keepdims=True)
        pick = jnp.where(lane == i, value, pick)
    vbias[...] = pick[0, 0:4]
    for load, store in zip(loads, stores):
        load.wait()
        store.start()
    for store in stores:
        store.wait()


def shards(
    tokens,
    lengths,
    block_map,
    first_gain,
    first_shift,
    query_weight,
    query_bias,
    keyval_weight,
    value_bias,
    output_weight,
    output_bias,
    second_gain,
    second_shift,
    up_weight,
    up_bias,
    down_weight,
    down_bias,
    cotangent,
):
    vmem = pl.BlockSpec(memory_space=pltpu.VMEM)
    smem = pl.BlockSpec(memory_space=pltpu.SMEM)
    hbm = pl.BlockSpec(memory_space=pl.ANY)

    def v(*shape, dtype=BF16):
        return pltpu.VMEM(shape, dtype)

    shapes = (
        jax.ShapeDtypeStruct((2, BLK, WIDTH), BF16),
        jax.ShapeDtypeStruct((2, BLK, WIDTH), F32),
        jax.ShapeDtypeStruct((48, WIDTH), F32),
        jax.ShapeDtypeStruct((48, WIDTH), F32),
        jax.ShapeDtypeStruct((48, 2 * BLK), F32),
        jax.ShapeDtypeStruct((48, FF), F32),
        jax.ShapeDtypeStruct((192, WIDTH), F32),
    )
    scratch = [
        v(2, BLK, WIDTH),
        v(2, BLK, WIDTH, dtype=F32),
        v(16, WIDTH),
    ]
    scratch += [v(*shape.shape, dtype=shape.dtype) for shape in shapes[2:]]
    scratch += [
        v(4, 2, 2, 16, WIDTH),
        v(4, 2, 2, 48, WIDTH),
        v(4, 2, 2, 48, 2 * HD),
        v(4, 2, 2, 48, WIDTH),
        v(4, 2, 2, 48, HALF),
        v(4, 2, 48, HALF),
        v(3, 2, 2, 192, WIDTH),
        v(4, 2, 2, 48, 512),
        v(4, 2, 2, 48, WIDTH),
        v(4, 2, 2, 48, 2 * BLK),
        v(4, 2, 2, 48, HALF),
        v(2, 2, 2, 192, WIDTH),
        v(4, 2, 48, 512),
        v(4, 2, 48, WIDTH),
        v(4, 48, 512),
        v(4, 48, WIDTH),
        v(2, 4, 2, 48, WIDTH),
        v(2, 2, 96, WIDTH),
        v(2, 4, 2, 48, WIDTH),
        v(4, 96, WIDTH),
        v(3, 48, 512),
        v(3, 48, WIDTH),
        v(2, 3, 2, 48, WIDTH),
        v(3, 96, WIDTH),
        v(2, 3, 48, 384),
        v(3, 48, 384),
        v(2, 2, 48, 384),
        v(2, 2, 48, 384),
        v(2, 4, 48, 384),
        v(2, 4, 48, 384),
        v(2, 3, 2, 2, 48, 384),
        v(2, 2, 2, 48, 384),
        v(2, 2, 48, 384),
        v(4, 48, 384),
        v(3, 48, 384),
        v(4, 2, 2, 48, 256),
        v(4, 2, 48, 256),
        v(4, 48, 256),
        v(3, 48, 256),
        v(4, 48, 256),
        v(2, 48, 256),
        v(4, 2, 48, 256),
        v(8, 48, 2 * BLK),
        v(4, 48, 512),
        v(4, 48, WIDTH),
        v(2, 48, 512),
        v(2, 48, WIDTH),
        v(PEERS, 48, 2 * BLK),
        v(PEERS, ROWS, 2 * HD),
        v(PEERS, ROWS, 2 * HD),
        v(PEERS, ROWS, 2 * HD),
        v(KEYS, BLK),
        v(KEYS, BLK),
        v(BLK, KEYS),
        v(BLK + 16, KEYS),
        v(GROUPS, BLK, ROWS),
        v(GROUPS, ROWS, BLK),
        v(GROUPS, KEYS, ROWS),
        v(KEYS, ROWS, dtype=F32),
        v(KEYS, ROWS, dtype=F32),
        v(GROUPS, BLK, ROWS, dtype=F32),
        v(GROUPS, 16, ROWS, dtype=F32),
        v(GROUPS, BLK, ROWS),
        v(GROUPS, BLK, ROWS),
        v(GROUPS, ROWS, BLK),
        v(ROWS, WIDTH),
        v(ROWS, WIDTH),
        v(WIDTH, ROWS),
        v(ROWS, WIDTH, dtype=F32),
        v(2, ROWS, WIDTH),
        v(WIDTH, 2 * ROWS),
        v(2, ROWS, WIDTH),
        v(2 * ROWS, HALF),
        v(2 * ROWS, HALF),
        v(ROWS, WIDTH),
        v(ROWS, WIDTH),
        v(ROWS, WIDTH, dtype=F32),
        v(ROWS, WIDTH),
        v(ROWS, WIDTH),
        pltpu.SemaphoreType.DMA((SEMS,)),
        pltpu.SemaphoreType.DMA((SEMS,)),
        pltpu.SemaphoreType.DMA((32,)),
    ]
    outs = pl.pallas_call(
        layer_kernel,
        out_shape=shapes,
        in_specs=[smem, smem, hbm, hbm] + [vmem] * 9 + [hbm] * 5,
        out_specs=(hbm,) * 7,
        scratch_shapes=scratch,
        compiler_params=pltpu.CompilerParams(
            collective_id=0, has_side_effects=True, vmem_limit_bytes=62 * 2**20
        ),
    )(
        lengths,
        block_map,
        tokens[0],
        cotangent[0],
        first_gain,
        first_shift,
        query_bias,
        value_bias,
        output_bias,
        second_gain,
        second_shift,
        up_bias,
        down_bias,
        query_weight,
        keyval_weight,
        output_weight,
        up_weight,
        down_weight,
    )

    def f(*shape):
        return jax.ShapeDtypeStruct(shape, F32)

    results = pl.pallas_call(
        finish_kernel,
        out_shape=(
            shapes[0],
            shapes[1],
            f(48),
            f(48),
            f(48, WIDTH),
            f(48),
            f(48, 2 * HD),
            f(4),
            f(48, WIDTH),
            f(48),
            f(48),
            f(48),
            f(48, FF),
            f(192),
            f(192, WIDTH),
            f(48),
        ),
        in_specs=[hbm] * 4 + [vmem] + [hbm] * 2,
        out_specs=tuple(
            hbm if i in (0, 1, 4, 8, 12, 14) else vmem for i in range(16)
        ),
        scratch_shapes=[
            pltpu.VMEM(shapes[i].shape, shapes[i].dtype) for i in (1, 5, 6, 0, 2, 3)
        ]
        + [pltpu.SemaphoreType.DMA((40,))],
    )(*outs)
    return (results[0][None], results[1][None]) + tuple(results[2:])


def solution(mesh):
    rows, matrix, batch = P("fsdp"), P("fsdp", None), P("fsdp", "ctx", None, None)
    return jax.shard_map(
        shards,
        mesh=mesh,
        in_specs=(
            batch,
            rows,
            P(),
            rows,
            rows,
            matrix,
            rows,
            matrix,
            rows,
            matrix,
            rows,
            rows,
            rows,
            matrix,
            rows,
            matrix,
            rows,
            batch,
        ),
        out_specs=(
            batch,
            batch,
            rows,
            rows,
            matrix,
            rows,
            matrix,
            rows,
            matrix,
            rows,
            rows,
            rows,
            matrix,
            rows,
            matrix,
            rows,
        ),
        check_vma=False,
    )
```
